128 devices in a mesh: gx: 8 (over x_lo, z), gy: 8 (over x_hi, y), gz: 2 (over core).
Axes of the slice: x: 4 (x_hi: 2, x_lo: 2; x = x_hi * 2 + x_lo), y: 4, z: 4, core: 2. Of those that a mesh axis runs over, the one named last changes fastest.
Arguments:
- iterate: float32 [128, 512, 256], P('gx', 'gy', 'gz'), may hold values from -8 to 8
- right_side: float32 [128, 512, 256], P('gx', 'gy', 'gz'), may hold values from -4 to 4
- diffusion: float32 [128, 512, 256], P('gx', 'gy', 'gz'), may hold values from 0.5 to 4
Outputs:
- improved: float32 [128, 512, 256], P('gx', 'gy', 'gz')
The draws below stay inside these ranges and needn't reach their ends.
All inputs are finite; a program needn't handle non-finite values.
Results may differ from the reference program's by a relative error of at most 0.00002.
Values sent between devices are 32-bit elements; how exact they have to be, the bound alone decides.
A program may use at most 128 MiB of HBM per device.

```python
import math
import jax
import jax.numpy as jnp
from jax import lax

DEGREE = 4
BOTTOM = 8
NX = 128
NY = 512
NZ = 256


def draw_right_side(key, part):
    key = jax.random.fold_in(key, 11)
    grainy = 1.6 * jax.random.normal(key, (NX, NY, NZ), jnp.float32)
    return jnp.clip(grainy, -4.0, 4.0)


def steps_of(stream_key, dims, shards, least, high):
    def one(axis_at, shards_of):
        steps = jax.random.uniform(jax.random.fold_in(jax.random.fold_in(stream_key, 6), axis_at), (shards_of,), jnp.float32, least / len(shards), high / len(shards))
        return jnp.repeat(jnp.exp(steps), dims[axis_at] // shards_of).reshape((-1,) + (1,) * (len(dims) - axis_at - 1))

    factor_of = one(*shards[0])
    for cut in shards[1:]:
        factor_of = factor_of * one(*cut)
    return factor_of


def normal_values(key, dims, scale, most, split=(), kind=jnp.bfloat16):
    level = steps_of(key, dims, split, -0.22, 0.18) if split else 1.0
    entries = jax.random.normal(key, dims, jnp.float32) * scale * level
    return jnp.minimum(jnp.maximum(entries, -most), most).astype(kind)


def setup_inputs(seed: int = 0) -> dict:
    key_list = jax.random.split(jax.random.key(seed), 4)
    iterate = normal_values(key_list[0], (NX, NY, NZ), 2.0, 8.0, ((0, 8), (1, 8), (2, 2)), jnp.float32)
    right_side = draw_right_side(jax.random.fold_in(key_list[3], 71), 0)
    diffusion = jnp.clip(jnp.exp(math.log(4.0) - 2.0794415 * jax.random.uniform(key_list[2], (NX, NY, NZ), jnp.float32) ** steps_of(key_list[2], (NX, NY, NZ), ((0, 8), (1, 8), (2, 2)), -0.2, 0.2)), 0.5, 4.0)
    return dict(iterate=iterate, right_side=right_side, diffusion=diffusion)


SMOOTH_LOW = 0.25
SMOOTH_HIGH = 2.0
BOTTOM_LOW = 0.05


def chebyshev_steps(sweeps, low_end, high_end):
    center = 0.5 * (high_end + low_end)
    radius = 0.5 * (high_end - low_end)
    sigma_ratio = center / radius
    rho_old = 1.0 / sigma_ratio
    steps_out = [(0.0, 1.0 / center)]
    for sweep_index in range(1, sweeps):
        rho_new = 1.0 / (2.0 * sigma_ratio - rho_old)
        steps_out.append((rho_new * rho_old, 2.0 * rho_new / radius))
        rho_old = rho_new
    return steps_out


def neighbour_views(padded):
    return (padded[:-2, 1:-1, 1:-1], padded[2:, 1:-1, 1:-1],
            padded[1:-1, :-2, 1:-1], padded[1:-1, 2:, 1:-1],
            padded[1:-1, 1:-1, :-2], padded[1:-1, 1:-1, 2:])


def operate(padded_values, padded_beta, level_scale):
    centre_values = padded_values[1:-1, 1:-1, 1:-1]
    centre_beta = padded_beta[1:-1, 1:-1, 1:-1]
    accumulated = jnp.zeros_like(centre_values)
    for value_side, beta_side in zip(neighbour_views(padded_values), neighbour_views(padded_beta)):
        accumulated = accumulated + 0.5 * (centre_beta + beta_side) * (centre_values - value_side)
    return level_scale * accumulated


def diagonal_inverse(padded_beta, level_scale):
    centre_beta = padded_beta[1:-1, 1:-1, 1:-1]
    accumulated = jnp.zeros_like(centre_beta)
    for beta_side in neighbour_views(padded_beta):
        accumulated = accumulated + 0.5 * (centre_beta + beta_side)
    return 1.0 / (level_scale * accumulated)


def smooth(values, source, padded_beta, inverse, level_scale, sweeps, low_end, pad_values, start_zero):
    weights = chebyshev_steps(sweeps, low_end, SMOOTH_HIGH)
    direction = jnp.zeros_like(values)
    if start_zero:
        direction = weights[0][1] * (inverse * source)
        values = values + direction
        weights = weights[1:]
    keep_weights = jnp.array([item[0] for item in weights], jnp.float32).astype(values.dtype)
    new_weights = jnp.array([item[1] for item in weights], jnp.float32).astype(values.dtype)

    def sweep_once(carry, pair):
        current, previous = carry
        residual = source - operate(pad_values(current), padded_beta, level_scale)
        update = pair[0] * previous + pair[1] * (inverse * residual)
        return (current + update, update), None

    (values, direction), unused = lax.scan(sweep_once, (values, direction), (keep_weights, new_weights))
    return values


def restrict_cells(values):
    size_x, size_y, size_z = values.shape
    blocks = values.reshape(size_x // 2, 2, size_y // 2, 2, size_z // 2, 2)
    return jnp.mean(blocks, axis=(1, 3, 5))


def prolong_cells(values):
    return jnp.repeat(jnp.repeat(jnp.repeat(values, 2, axis=0), 2, axis=1), 2, axis=2)


def pad_whole(values):
    return jnp.pad(values, 1)


def level_setup(beta_level, level_scale):
    padded = pad_whole(beta_level)
    return padded, diagonal_inverse(padded, level_scale)


def bottom_solve(source, beta_level):
    padded, inverse = level_setup(beta_level, 0.015625)
    return smooth(jnp.zeros_like(source), source, padded, inverse, 0.015625, BOTTOM, BOTTOM_LOW, pad_whole, True)


def reference(iterate, right_side, diffusion):
    beta_one = restrict_cells(diffusion)
    beta_two = restrict_cells(beta_one)
    beta_three = restrict_cells(beta_two)
    padded_zero, inverse_zero = level_setup(diffusion, 1.0)
    padded_one, inverse_one = level_setup(beta_one, 0.25)
    padded_two, inverse_two = level_setup(beta_two, 0.0625)
    presmoothed = smooth(iterate, right_side, padded_zero, inverse_zero, 1.0, DEGREE, SMOOTH_LOW, pad_whole, False)
    source_one = restrict_cells(right_side - operate(pad_whole(presmoothed), padded_zero, 1.0))
    correction_one = smooth(jnp.zeros_like(source_one), source_one, padded_one, inverse_one, 0.25, DEGREE, SMOOTH_LOW, pad_whole, True)
    source_two = restrict_cells(source_one - operate(pad_whole(correction_one), padded_one, 0.25))
    correction_two = smooth(jnp.zeros_like(source_two), source_two, padded_two, inverse_two, 0.0625, DEGREE, SMOOTH_LOW, pad_whole, True)
    source_three = restrict_cells(source_two - operate(pad_whole(correction_two), padded_two, 0.0625))
    coarsest = bottom_solve(source_three, beta_three)
    corrected_two = smooth(correction_two + prolong_cells(coarsest), source_two, padded_two, inverse_two, 0.0625, DEGREE, SMOOTH_LOW, pad_whole, False)
    corrected_one = smooth(correction_one + prolong_cells(corrected_two), source_one, padded_one, inverse_one, 0.25, DEGREE, SMOOTH_LOW, pad_whole, False)
    return smooth(presmoothed + prolong_cells(corrected_one), right_side, padded_zero, inverse_zero, 1.0, DEGREE, SMOOTH_LOW, pad_whole, False)
```

```python
import jax
import jax.numpy as jnp
from jax import lax
from jax.experimental import pallas as pl
from jax.experimental.pallas import tpu as pltpu
from jax.sharding import PartitionSpec as P

DEGREE = 4
BOTTOM = 8
SMOOTH_LOW = 0.25
SMOOTH_HIGH = 2.0
BOTTOM_LOW = 0.05

F32 = jnp.float32
MESH = pl.DeviceIdType.MESH
NP = 16
NJ = 8


def chebyshev_steps(sweeps, low_end, high_end):
    center = 0.5 * (high_end + low_end)
    radius = 0.5 * (high_end - low_end)
    sigma_ratio = center / radius
    rho_old = 1.0 / sigma_ratio
    steps_out = [(0.0, 1.0 / center)]
    for sweep_index in range(1, sweeps):
        rho_new = 1.0 / (2.0 * sigma_ratio - rho_old)
        steps_out.append((rho_new * rho_old, 2.0 * rho_new / radius))
        rho_old = rho_new
    return steps_out


FINE_STEPS = chebyshev_steps(DEGREE, SMOOTH_LOW, SMOOTH_HIGH)
BOTTOM_STEPS = chebyshev_steps(BOTTOM, BOTTOM_LOW, SMOOTH_HIGH)


def loop(low, high, body):
    def step(index, carry):
        body(index)
        return carry

    lax.fori_loop(low, high, step, 0)


def lanes(shape):
    return lax.broadcasted_iota(jnp.int32, shape, len(shape) - 1)


class Moves:
    def __init__(self, place, ref, send, recv, dirs):
        self.place, self.ref, self.send, self.recv, self.dirs = place, ref, send, recv, dirs

    def copy(self, at):
        p, j = self.place
        dp, dj, src, dst = self.dirs[at]
        to = p + dp
        return pltpu.make_async_remote_copy(
            src_ref=self.ref.at[src],
            dst_ref=self.ref.at[dst],
            send_sem=self.send.at[at],
            recv_sem=self.recv.at[at],
            device_id=(to // 2, j + dj, to % 2),
            device_id_type=MESH,
        )

    def each(self, sign, act):
        p, j = self.place
        for at, (dp, dj, src, dst) in enumerate(self.dirs):
            ok = None
            for value, count, shift in ((p, NP, sign * dp), (j, NJ, sign * dj)):
                if shift > 0:
                    good = value < count - shift
                elif shift < 0:
                    good = value >= -shift
                else:
                    continue
                ok = good if ok is None else jnp.logical_and(ok, good)

            @pl.when(ok)
            def _():
                act(self.copy(at))

    def start(self):
        self.each(1, lambda c: c.start())

    def arrive(self):
        self.each(-1, lambda c: c.wait_recv())

    def drain(self):
        self.each(1, lambda c: c.wait_send())


def block_dirs(planes, first, halo, row, rows, dps, djs, wide, mid=()):
    out = []
    for dj in djs:
        for dp in dps:
            if dp == 0 and dj == 0:
                continue
            if dp > 0:
                x0 = max(0, planes * dp - halo)
                count = planes - x0
            elif dp < 0:
                x0 = 0
                count = min(planes, planes + halo + planes * dp)
            else:
                x0, count = 0, planes
            if dj == 0:
                low, size = (row - 8, rows + 16) if wide else (row, rows)
                to = low
            elif dj > 0:
                low, size, to = row + rows - 8, 8, row - 8
            else:
                low, size, to = row, 8, row + rows
            a = first + x0
            src = (pl.ds(a, count),) + mid + (pl.ds(low, size),)
            dst = (pl.ds(a - planes * dp, count),) + mid + (pl.ds(to, size),)
            out.append((dp, dj, src, dst))
    return out


def line(ref, start):
    return ref[pl.ds(start, 8, stride=2)]


def kernel(
    iterate, right_side, diffusion, out,
    sv, sc, sg, perm, back, tmp,
    va, vb, dd, gg, jj, di, wx, wl, wr, wz, wm, cc, pre, obuf,
    s1, c1, k1, va1, vb1, d1, j1, i1, wx1, wl1, wr1, zl1, zr1,
    s2, c2, k2, va2, vb2, d2, j2, i2, wx2, wl2, wr2, zl2, zr2,
    s3, c3, va3, vb3, d3, j3, i3, wx3, wl3, wr3, zl3, zr3,
    x_send, x_recv, self_sem,
    s1_send, s1_recv, s2_send, s2_recv,
    y_send, y_recv, h_send, h_recv, g_send, g_recv, o_send, o_recv,
):
    i = lax.axis_index("gx")
    j = lax.axis_index("gy")
    k = lax.axis_index("gz")
    p = 2 * i + k
    place = (p, j)

    barrier = pltpu.get_barrier_semaphore()

    def greet(to, tj):
        pl.semaphore_signal(
            barrier, inc=1, device_id=(to // 2, tj, to % 2), device_id_type=MESH
        )

    loop(1, NP, lambda q: greet((p + q) % NP, j))
    count = NP - 1
    for dj in (-1, 1, -2, 2):
        okj = jnp.logical_and(j + dj >= 0, j + dj < NJ)
        for dp in range(-3, 4) if abs(dj) == 1 else (0,):
            ok = jnp.logical_and(okj, jnp.logical_and(p + dp >= 0, p + dp < NP))
            count = count + ok.astype(jnp.int32)

            @pl.when(ok)
            def _():
                greet(p + dp, j + dj)

    pl.semaphore_wait(barrier, count)

    def fine_moves(at, src, dst, halo):
        n = 8 + halo
        sends = []

        def copy(slot_s, slot_r, x0, nx, a0, low, size, to, zh, dev):
            return pltpu.make_async_remote_copy(
                src_ref=src.at[pl.ds(x0, nx), pl.ds(low, size)],
                dst_ref=dst.at[pl.ds(a0, nx), zh, pl.ds(to, size)],
                send_sem=x_send.at[at, slot_s],
                recv_sem=x_recv.at[at, slot_r],
                device_id=dev,
                device_id_type=MESH,
            )

        mine = pltpu.make_async_copy(
            src.at[pl.ds(k * (8 - halo), n)],
            dst.at[pl.ds(5 - halo * k, n), k, pl.ds(8, 64)],
            self_sem.at[at],
        )
        other = 1 - k
        sends.append((None, copy(0, 0, other * (8 - halo), n, 5 - halo * other, 0, 64, 8, k, (i, j, other))))
        rows = [(0, 0, 64, 8), (1, 56, 8, 0), (-1, 0, 8, 72)]
        for dj, low, size, to in rows:
            okj = jnp.logical_and(j + dj >= 0, j + dj < NJ)
            turn = {0: 0, 1: 1, -1: 2}[dj]
            up = jnp.logical_and(i < 7, okj)
            down = jnp.logical_and(i > 0, okj)
            slot = 1 + 2 * turn + k
            sends.append((up, copy(1 + 2 * turn, slot, 16 - halo, halo, 5 - halo, low, size, to, k, (i + 1, j + dj, 0))))
            sends.append((down, copy(2 + 2 * turn, slot, 0, halo, 13, low, size, to, k, (i - 1, j + dj, 1))))
            if dj != 0:
                for half in (0, 1):
                    sends.append(
                        (okj, copy(5 + 2 * turn + half, 5 + 2 * turn + k, half * (8 - halo), n, 5 - halo * half, low, size, to, k, (i, j + dj, half)))
                    )

        def start():
            mine.start()
            for ok, c in sends:
                if ok is None:
                    c.start()
                else:
                    pl.when(ok)(c.start)

        def arrive():
            mine.wait()
            copy(0, 0, 0, n, 5 - halo * k, 0, 64, 8, other, (i, j, other)).wait_recv()
            beside = jnp.logical_or(jnp.logical_and(k == 0, i > 0), jnp.logical_and(k == 1, i < 7))
            a0 = (5 - halo) * (1 - k) + 13 * k
            for dj, low, size, to in rows:
                turn = {0: 0, 1: 1, -1: 2}[dj]
                okj = jnp.logical_and(j - dj >= 0, j - dj < NJ)
                ok = jnp.logical_and(beside, okj)
                for half in (0, 1):
                    pl.when(ok)(copy(0, 1 + 2 * turn + half, 0, halo, a0, low, size, to, half, (i, j, other)).wait_recv)
                    if dj != 0:
                        pl.when(okj)(copy(0, 5 + 2 * turn + half, 0, n, 5 - halo * k, low, size, to, half, (i, j, other)).wait_recv)

        def drain():
            for ok, c in sends:
                if ok is None:
                    c.wait_send()
                else:
                    pl.when(ok)(c.wait_send)

        return start, arrive, drain

    moves_c = fine_moves(0, diffusion, sc, 5)
    moves_v = fine_moves(1, iterate, sv, 5)
    moves_g = fine_moves(2, right_side, sg, 4)
    moves_c[0]()
    moves_v[0]()
    moves_g[0]()

    def clear(ref, planes, low_planes, high_from, edges, own=None):
        def wipe(a):
            ref[a] = jnp.zeros(ref.shape[1:], F32)

        loop(0, low_planes, wipe)
        loop(high_from, planes, wipe)

        def wipe_rows(low, size):
            def one(a):
                if len(ref.shape) == 4:
                    ref[a, :, low:low + size] = jnp.zeros((2, size, 128), F32)
                else:
                    ref[a, low:low + size] = jnp.zeros((size, 128), F32)

            loop(*(own or (0, planes)), one)

        for test, low, size in edges:
            pl.when(test)(lambda low=low, size=size: wipe_rows(low, size))

    def outer(first, planes, per, total):
        low = jnp.clip(first - per * p, 0, planes)
        high = jnp.clip(total - per * p + first, 0, planes)
        return low, high

    low, high = outer(5, 18, 8, 128)
    for ref in (sv, sc, sg):
        clear(ref, 18, low, high, [(j == 0, 0, 8), (j == 7, 72, 8)])
    clear(pre, 18, low, high, [(j == 0, 8, 8), (j == 7, 80, 8)], (5, 13))
    low, high = outer(6, 16, 4, 64)
    for ref, own in ((s1, None), (c1, (6, 10)), (k1, (6, 10))):
        clear(ref, 16, low, high, [(j == 0, 8, 8), (j == 7, 48, 8)], own)
    low, high = outer(7, 16, 2, 32)
    for ref, own in ((s2, None), (c2, (7, 9)), (k2, (7, 9))):
        clear(ref, 16, low, high, [(j == 0, 8, 8), (j == 7, 32, 8)], own)
    for ref in (s3, c3):
        clear(ref, 18, 1, 17, [(j == 0, 8, 16), (j == 1, 8, 8), (j == 6, 40, 8), (j == 7, 32, 16)], (p + 1, p + 2))
    for ref in (va3, vb3):
        clear(ref, 18, 1, 17, [])

    row = lax.broadcasted_iota(jnp.int32, (256, 256), 0)
    col = lax.broadcasted_iota(jnp.int32, (256, 256), 1)

    def taken(of):
        return jnp.where(of < 128, 2 * of, 2 * of - 255)

    perm[...] = jnp.where(row == taken(col), 1.0, 0.0).astype(jnp.bfloat16)
    back[...] = jnp.where(col == taken(row), 1.0, 0.0).astype(jnp.bfloat16)

    def shuffle(left, right, matrix):
        both = jnp.concatenate([left, right], axis=1)
        high = both.astype(jnp.bfloat16)
        rest = both - high.astype(F32)
        mid = rest.astype(jnp.bfloat16)
        low = (rest - mid.astype(F32)).astype(jnp.bfloat16)
        m = matrix[...]
        res = jnp.dot(high, m, preferred_element_type=F32)
        res = res + jnp.dot(mid, m, preferred_element_type=F32)
        res = res + jnp.dot(low, m, preferred_element_type=F32)
        return res[:, :128], res[:, 128:]

    def split(src, dst, low, high):
        def one(a):
            even, odd = shuffle(src[a, 0], src[a, 1], perm)
            dst[a, 0, 4:84] = even
            dst[a, 1, 4:84] = odd

        loop(low, high, one)

    def fold_rows(at):
        return line(tmp, 16 * at) + line(tmp, 16 * at + 1)

    def fold_lanes(value, step):
        even = (lanes(value.shape) // step) % 2 == 0
        return value + jnp.where(even, pltpu.roll(value, 128 - step, 1), pltpu.roll(value, step, 1))

    moves_c[1]()
    split(sc, cc, 0, 18)

    def coarsen_c(m):
        a = 5 + 2 * m
        w = slice(12, 76)
        tmp[...] = (cc[a, 0, w] + cc[a, 1, w]) + (cc[a + 1, 0, w] + cc[a + 1, 1, w])
        for t in range(4):
            c1[6 + m, 16 + 8 * t:24 + 8 * t] = 0.125 * fold_rows(t)

    loop(0, 4, coarsen_c)
    for m in range(2):
        tmp[0:32] = c1[6 + 2 * m, 16:48] + c1[7 + 2 * m, 16:48]
        for t in range(2):
            c2[7 + m, 16 + 8 * t:24 + 8 * t] = 0.125 * fold_lanes(fold_rows(t), 1)
    tmp[0:16] = c2[7, 16:32] + c2[8, 16:32]
    c3[p + 1, 24:32] = 0.125 * fold_lanes(fold_rows(0), 2)

    def y_moves(at, ref, planes, first, row, rows, mid=()):
        dirs = block_dirs(planes, first, 0, row, rows, (0,), (-1, 1), False, mid)
        return Moves(place, ref, y_send.at[at], y_recv.at[at], dirs)

    def h_moves(at, ref, planes, first, halo, row, rows, reach, mid=()):
        dps = [d for d in range(-reach, reach + 1) if d != 0]
        dirs = block_dirs(planes, first, halo, row, rows, dps, (0,), True, mid)
        return Moves(place, ref, h_send.at[at], h_recv.at[at], dirs)

    def column_moves(at, ref):
        here = (p + 1, pl.ds(24, 8))
        dirs = [(0, dj, here, (p + 1, pl.ds(24 - 8 * dj, 8))) for dj in (-2, -1, 1, 2)]
        return Moves(place, ref, y_send.at[at], y_recv.at[at], dirs)

    class Around:
        def __init__(self, at, ref):
            self.at, self.ref = at, ref

        def copy(self, q, plane):
            to = (p + q) % NP
            return pltpu.make_async_remote_copy(
                src_ref=self.ref.at[plane, pl.ds(8, 40)],
                dst_ref=self.ref.at[plane, pl.ds(8, 40)],
                send_sem=g_send.at[self.at, q],
                recv_sem=g_recv.at[self.at, q],
                device_id=(to // 2, j, to % 2),
                device_id_type=MESH,
            )

        def start(self):
            loop(1, NP, lambda q: self.copy(q, p + 1).start())

        def arrive(self):
            loop(1, NP, lambda q: self.copy(q, (p - q + NP) % NP + 1).wait_recv())

        def drain(self):
            loop(1, NP, lambda q: self.copy(q, p + 1).wait_send())

    y_c1 = y_moves(0, c1, 4, 6, 16, 32)
    y_c2 = y_moves(1, c2, 2, 7, 16, 16)
    y_c3 = column_moves(2, c3)
    h_c1 = h_moves(0, c1, 4, 6, 6, 16, 32, 2)
    h_c2 = h_moves(1, c2, 2, 7, 7, 16, 16, 4)
    h_c3 = Around(0, c3)
    y_pre = y_moves(3, pre, 8, 5, 16, 64, (slice(None),))
    h_pre = h_moves(2, pre, 8, 5, 4, 16, 64, 1, (slice(None),))
    y_k1 = y_moves(4, k1, 4, 6, 16, 32)
    h_k1 = h_moves(3, k1, 4, 6, 6, 16, 32, 2)
    y_k2 = y_moves(5, k2, 2, 7, 16, 16)
    h_k2 = h_moves(4, k2, 2, 7, 7, 16, 16, 4)
    y_s3 = column_moves(6, s3)
    h_s3 = Around(1, s3)
    m_s1 = Moves(place, s1, s1_send, s1_recv, block_dirs(4, 6, 5, 16, 32, range(-2, 3), (0, -1, 1), False))
    m_s2 = Moves(place, s2, s2_send, s2_recv, block_dirs(2, 7, 6, 16, 16, range(-3, 4), (0, -1, 1), False))

    y_c1.start()
    y_c2.start()
    y_c3.start()

    wide = slice(8, 80)
    lane = lanes((72, 128))

    def weights(a):
        wx[a, :, wide] = 0.5 * (cc[a, :, wide] + cc[a + 1, :, wide])

    def fine_setup(a):
        weights(a)
        even = cc[a, 0, wide]
        odd = cc[a, 1, wide]
        left = jnp.where(lane == 0, 0.0, pltpu.roll(odd, 1, 1))
        right = jnp.where(lane == 127, 0.0, pltpu.roll(even, 127, 1))
        wm[a, wide] = 0.5 * (even + odd)
        wz[a, 0, wide] = jnp.where(lane == 0, 0.0, 0.5 * (even + left))
        wz[a, 1, wide] = jnp.where(lane == 127, 0.0, 0.5 * (odd + right))
        for h, mid, zs in ((0, even, left + odd), (1, odd, even + right)):
            yl = cc[a, h, 7:79]
            yr = cc[a, h, 9:81]
            wl[a, h, wide] = 0.5 * (mid + yl)
            wr[a, h, wide] = 0.5 * (mid + yr)
            diag = 0.5 * (6.0 * mid + (cc[a - 1, h, wide] + cc[a + 1, h, wide]) + (yl + yr) + zs)
            di[a, h, wide] = diag
            jj[a, h, wide] = jnp.where(mid > 0.0, 1.0 / diag, 0.0)

    weights(0)
    loop(1, 17, fine_setup)

    moves_v[1]()
    split(sv, va, 0, 18)
    moves_g[1]()
    split(sg, gg, 1, 17)

    def fine_sum(src, a, low, high):
        w = slice(low, high)
        even = src[a, 0, w]
        odd = src[a, 1, w]
        res = []
        for h, mid in ((0, even), (1, odd)):
            total = gg[a, h, w] + wx[a - 1, h, w] * src[a - 1, h, w] + wx[a, h, w] * src[a + 1, h, w]
            total = total + wl[a, h, w] * src[a, h, low - 1:high - 1] + wr[a, h, w] * src[a, h, low + 1:high + 1]
            if h == 0:
                total = total + wz[a, 0, w] * pltpu.roll(odd, 1, 1) + wm[a, w] * odd
            else:
                total = total + wm[a, w] * even + wz[a, 1, w] * pltpu.roll(even, 127, 1)
            res.append((mid, total))
        return res

    def fine_sweep(src, dst, step, halo):
        keep, new = FINE_STEPS[step]

        def one(a):
            for h, (mid, total) in enumerate(fine_sum(src, a, 8, 80)):
                move = new * (jj[a, h, wide] * total - mid)
                if step > 0:
                    move = move + keep * dd[a, h, wide]
                dd[a, h, wide] = move
                dst[a, h, wide] = mid + move

        loop(5 - halo, 13 + halo, one)

    fine_sweep(va, vb, 0, 4)
    fine_sweep(vb, va, 1, 3)
    y_c1.arrive()
    y_c2.arrive()
    y_c3.arrive()
    h_c1.start()
    h_c2.start()
    h_c3.start()
    fine_sweep(va, vb, 2, 2)
    fine_sweep(vb, va, 3, 1)

    def fine_residual(m):
        w = slice(12, 76)
        total = None
        for a in (5 + 2 * m, 6 + 2 * m):
            for h, (mid, acc) in enumerate(fine_sum(va, a, 12, 76)):
                part = acc - di[a, h, w] * mid
                total = part if total is None else total + part
        tmp[...] = total
        for t in range(4):
            s1[6 + m, 16 + 8 * t:24 + 8 * t] = 0.125 * fold_rows(t)

    loop(0, 4, fine_residual)
    m_s1.start()

    def keep_fine(a):
        pre[a, :, 16:80] = va[a, :, 12:76]

    loop(5, 13, keep_fine)
    y_pre.start()

    def setup(c, jn, dn, wxn, wln, wrn, zln, zrn, planes, rows, step, scale):
        low, high = planes
        r0, r1 = rows
        w = slice(r0, r1)
        spot = lanes((r1 - r0, 128))
        half = 0.5 * scale

        def across(a):
            wxn[a, w] = half * (c[a, w] + c[a + 1, w])

        def one(a):
            across(a)
            mid = c[a, w]
            left = jnp.where(spot < step, 0.0, pltpu.roll(mid, step, 1))
            right = jnp.where(spot >= 128 - step, 0.0, pltpu.roll(mid, 128 - step, 1))
            yl = c[a, r0 - 1:r1 - 1]
            yr = c[a, r0 + 1:r1 + 1]
            wln[a, w] = half * (mid + yl)
            wrn[a, w] = half * (mid + yr)
            zln[a, w] = jnp.where(spot < step, 0.0, half * (mid + left))
            zrn[a, w] = jnp.where(spot >= 128 - step, 0.0, half * (mid + right))
            diag = half * (6.0 * mid + (c[a - 1, w] + c[a + 1, w]) + (yl + yr) + (left + right))
            dn[a, w] = diag
            jn[a, w] = jnp.where(mid > 0.0, 1.0 / diag, 0.0)

        across(low - 1)
        loop(low, high, one)

    def gather_sum(src, a, g, wxn, wln, wrn, zln, zrn, rows, step):
        r0, r1 = rows
        w = slice(r0, r1)
        mid = src[a, w]
        total = g[a, w] + wxn[a - 1, w] * src[a - 1, w] + wxn[a, w] * src[a + 1, w]
        total = total + wln[a, w] * src[a, r0 - 1:r1 - 1] + wrn[a, w] * src[a, r0 + 1:r1 + 1]
        total = total + zln[a, w] * pltpu.roll(mid, step, 1) + zrn[a, w] * pltpu.roll(mid, 128 - step, 1)
        return mid, total

    def sweep(src, dst, d, jn, ws, planes, rows, step, pair):
        keep, new = pair
        w = slice(*rows)

        def one(a):
            mid, total = gather_sum(src, a, *ws, rows, step)
            move = new * (jn[a, w] * total - mid)
            if keep != 0.0:
                move = move + keep * d[a, w]
            d[a, w] = move
            dst[a, w] = mid + move

        loop(planes[0], planes[1], one)

    def first(dst, d, g, jn, planes, rows, new):
        w = slice(*rows)

        def one(a):
            move = new * (jn[a, w] * g[a, w])
            d[a, w] = move
            dst[a, w] = move

        loop(planes[0], planes[1], one)

    ws1 = (s1, wx1, wl1, wr1, zl1, zr1)
    ws2 = (s2, wx2, wl2, wr2, zl2, zr2)
    ws3 = (s3, wx3, wl3, wr3, zl3, zr3)
    rows1, rows2, rows3 = (8, 56), (8, 40), (8, 48)

    h_c1.arrive()
    setup(c1, j1, i1, wx1, wl1, wr1, zl1, zr1, (1, 15), rows1, 1, 0.25)
    h_c2.arrive()
    setup(c2, j2, i2, wx2, wl2, wr2, zl2, zr2, (1, 15), rows2, 2, 0.0625)
    h_c3.arrive()
    setup(c3, j3, i3, wx3, wl3, wr3, zl3, zr3, (1, 17), rows3, 4, 0.015625)

    m_s1.arrive()
    first(va1, d1, s1, j1, (2, 14), rows1, FINE_STEPS[0][1])
    sweep(va1, vb1, d1, j1, ws1, (3, 13), rows1, 1, FINE_STEPS[1])
    sweep(vb1, va1, d1, j1, ws1, (4, 12), rows1, 1, FINE_STEPS[2])
    sweep(va1, vb1, d1, j1, ws1, (5, 11), rows1, 1, FINE_STEPS[3])

    def residual(src, a, ws, dn, rows, step):
        mid, total = gather_sum(src, a, *ws, rows, step)
        return total - dn[a, slice(*rows)] * mid

    for m in range(2):
        a = 6 + 2 * m
        tmp[0:32] = residual(vb1, a, ws1, i1, (16, 48), 1) + residual(vb1, a + 1, ws1, i1, (16, 48), 1)
        for t in range(2):
            s2[7 + m, 16 + 8 * t:24 + 8 * t] = 0.125 * fold_lanes(fold_rows(t), 1)
    m_s2.start()
    k1[6:10, 16:48] = vb1[6:10, 16:48]
    y_k1.start()
    y_pre.arrive()
    h_pre.start()

    m_s2.arrive()
    first(va2, d2, s2, j2, (3, 13), rows2, FINE_STEPS[0][1])
    sweep(va2, vb2, d2, j2, ws2, (4, 12), rows2, 2, FINE_STEPS[1])
    sweep(vb2, va2, d2, j2, ws2, (5, 11), rows2, 2, FINE_STEPS[2])
    sweep(va2, vb2, d2, j2, ws2, (6, 10), rows2, 2, FINE_STEPS[3])
    tmp[0:16] = residual(vb2, 7, ws2, i2, (16, 32), 2) + residual(vb2, 8, ws2, i2, (16, 32), 2)
    s3[p + 1, 24:32] = 0.125 * fold_lanes(fold_rows(0), 2)
    y_s3.start()
    k2[7:9, 16:32] = vb2[7:9, 16:32]
    y_k2.start()
    y_k1.arrive()
    h_k1.start()
    y_s3.arrive()
    h_s3.start()
    y_k2.arrive()
    h_k2.start()

    h_s3.arrive()
    first(va3, d3, s3, j3, (1, 17), rows3, BOTTOM_STEPS[0][1])
    here, there = va3, vb3
    for at in range(1, BOTTOM):
        halo = BOTTOM + 3 - at
        planes = (jnp.maximum(1, p + 1 - halo), jnp.minimum(17, p + 2 + halo))
        sweep(here, there, d3, j3, ws3, planes, rows3 if halo > 8 else (16, 40), 4, BOTTOM_STEPS[at])
        here, there = there, here

    h_k2.arrive()

    def finish2(a):
        up = jnp.clip(p - 3 + (a + 1) // 2, 0, 17)
        for t in range(2):
            e = here[up, 20 + 8 * t:28 + 8 * t]
            for odd in range(2):
                at = pl.ds(8 + 16 * t + odd, 8, stride=2)
                va2[a, at] = k2[a, at] + e

    loop(0, 16, finish2)
    sweep(va2, vb2, d2, j2, ws2, (1, 15), rows2, 2, FINE_STEPS[0])
    sweep(vb2, va2, d2, j2, ws2, (2, 14), rows2, 2, FINE_STEPS[1])
    sweep(va2, vb2, d2, j2, ws2, (3, 13), rows2, 2, FINE_STEPS[2])
    sweep(vb2, va2, d2, j2, ws2, (4, 12), rows2, 2, FINE_STEPS[3])

    h_k1.arrive()

    def finish1(a):
        up = 4 + a // 2
        for t in range(3):
            e = va2[up, 12 + 8 * t:20 + 8 * t]
            for odd in range(2):
                at = pl.ds(8 + 16 * t + odd, 8, stride=2)
                va1[a, at] = k1[a, at] + e

    loop(0, 16, finish1)
    sweep(va1, vb1, d1, j1, ws1, (1, 15), rows1, 1, FINE_STEPS[0])
    sweep(vb1, va1, d1, j1, ws1, (2, 14), rows1, 1, FINE_STEPS[1])
    sweep(va1, vb1, d1, j1, ws1, (3, 13), rows1, 1, FINE_STEPS[2])
    sweep(vb1, va1, d1, j1, ws1, (4, 12), rows1, 1, FINE_STEPS[3])

    h_pre.arrive()

    def finish0(m):
        for t in range(5):
            e = va1[4 + m, 14 + 8 * t:22 + 8 * t]
            for x in range(2):
                a = 1 + 2 * m + x
                for h in range(2):
                    for odd in range(2):
                        got = pre[a, h, pl.ds(12 + 16 * t + odd, 8, stride=2)]
                        va[a, h, pl.ds(8 + 16 * t + odd, 8, stride=2)] = got + e

    loop(0, 8, finish0)
    fine_sweep(va, vb, 0, 3)
    fine_sweep(vb, va, 1, 2)
    fine_sweep(va, vb, 2, 1)
    fine_sweep(vb, va, 3, 0)

    def join(x):
        left, right = shuffle(va[5 + x, 0, 12:76], va[5 + x, 1, 12:76], back)
        obuf[0, x] = left
        obuf[1, x] = right

    loop(0, 8, join)
    give = pltpu.make_async_remote_copy(
        src_ref=obuf.at[1 - k],
        dst_ref=out.at[pl.ds(8 * k, 8)],
        send_sem=o_send,
        recv_sem=o_recv,
        device_id=(i, j, 1 - k),
        device_id_type=MESH,
    )
    give.start()
    out[pl.ds(8 * k, 8)] = obuf[k]
    give.wait_send()
    pltpu.make_async_remote_copy(
        src_ref=obuf.at[k],
        dst_ref=out.at[pl.ds(8 * (1 - k), 8)],
        send_sem=o_send,
        recv_sem=o_recv,
        device_id=(i, j, 1 - k),
        device_id_type=MESH,
    ).wait_recv()

    for moves in (moves_c, moves_v, moves_g):
        moves[2]()
    for moves in (y_c1, y_c2, y_c3, h_c1, h_c2, h_c3, m_s1, y_pre, h_pre, m_s2, y_k1, h_k1, y_s3, h_s3, y_k2, h_k2):
        moves.drain()


def on_device(iterate, right_side, diffusion):
    def buf(*shape):
        return pltpu.VMEM(shape, F32)

    fine = [buf(18, 2, 88, 128)] * 10
    scratch = [buf(18, 2, 80, 128)] * 3
    scratch += [pltpu.VMEM((256, 256), jnp.bfloat16)] * 2 + [buf(64, 128)]
    scratch += fine + [buf(18, 88, 128), buf(18, 2, 88, 128), buf(18, 2, 96, 128), buf(2, 8, 64, 128)]
    scratch += [buf(16, 64, 128)] * 13
    scratch += [buf(16, 48, 128)] * 13
    scratch += [buf(18, 56, 128)] * 12
    dma = pltpu.SemaphoreType.DMA
    scratch += [dma((3, 11)), dma((3, 11)), dma((3,))]
    scratch += [dma((14,)), dma((14,)), dma((20,)), dma((20,))]
    scratch += [dma((7, 4)), dma((7, 4)), dma((5, 8)), dma((5, 8)), dma((2, NP)), dma((2, NP)), dma, dma]
    return pl.pallas_call(
        kernel,
        out_shape=jax.ShapeDtypeStruct((16, 64, 128), F32),
        in_specs=[pl.BlockSpec(memory_space=pl.ANY)] * 3,
        out_specs=pl.BlockSpec(memory_space=pltpu.VMEM),
        scratch_shapes=scratch,
        compiler_params=pltpu.CompilerParams(
            collective_id=0, has_side_effects=True, vmem_limit_bytes=60 * 2**20
        ),
        cost_estimate=pl.CostEstimate(flops=10**8, bytes_accessed=2 * 10**6, transcendentals=0),
        name="vcycle",
    )(iterate, right_side, diffusion)


def solution(mesh):
    placed = (P("gx", "gy", "gz"), P("gx", "gy", "gz"), P("gx", "gy", "gz"))
    return jax.shard_map(
        on_device, mesh=mesh, in_specs=placed, out_specs=P("gx", "gy", "gz"), check_vma=False
    )
```

```python
import jax
import jax.numpy as jnp
from jax import lax
from jax.experimental import pallas as pl
from jax.experimental.pallas import tpu as pltpu
from jax.sharding import PartitionSpec as P

DEGREE = 4
BOTTOM = 8
SMOOTH_LOW = 0.25
SMOOTH_HIGH = 2.0
BOTTOM_LOW = 0.05

F32 = jnp.float32
MESH = pl.DeviceIdType.MESH
NP = 16
NJ = 8


def chebyshev_steps(sweeps, low_end, high_end):
    center = 0.5 * (high_end + low_end)
    radius = 0.5 * (high_end - low_end)
    sigma_ratio = center / radius
    rho_old = 1.0 / sigma_ratio
    steps_out = [(0.0, 1.0 / center)]
    for sweep_index in range(1, sweeps):
        rho_new = 1.0 / (2.0 * sigma_ratio - rho_old)
        steps_out.append((rho_new * rho_old, 2.0 * rho_new / radius))
        rho_old = rho_new
    return steps_out


FINE_STEPS = chebyshev_steps(DEGREE, SMOOTH_LOW, SMOOTH_HIGH)
BOTTOM_STEPS = chebyshev_steps(BOTTOM, BOTTOM_LOW, SMOOTH_HIGH)


def loop(low, high, body):
    def step(index, carry):
        body(index)
        return carry

    lax.fori_loop(low, high, step, 0)


def spread(low, count, most, body):
    runs = -(-count // most)
    each = -(-count // runs)
    full = count // each
    if full > 1:
        loop(0, full, lambda r: body(low + r * each, each))
    elif full == 1:
        body(low, each)
    if count % each:
        body(low + full * each, count % each)


def lanes(shape):
    return lax.broadcasted_iota(jnp.int32, shape, len(shape) - 1)


class Moves:
    def __init__(self, place, ref, send, recv, dirs):
        self.place, self.ref, self.send, self.recv, self.dirs = place, ref, send, recv, dirs

    def copy(self, at):
        p, j = self.place
        dp, dj, src, dst = self.dirs[at]
        to = p + dp
        return pltpu.make_async_remote_copy(
            src_ref=self.ref.at[src],
            dst_ref=self.ref.at[dst],
            send_sem=self.send.at[at],
            recv_sem=self.recv.at[at],
            device_id=(to // 2, j + dj, to % 2),
            device_id_type=MESH,
        )

    def each(self, sign, act):
        p, j = self.place
        for at, (dp, dj, src, dst) in enumerate(self.dirs):
            ok = None
            for value, count, shift in ((p, NP, sign * dp), (j, NJ, sign * dj)):
                if shift > 0:
                    good = value < count - shift
                elif shift < 0:
                    good = value >= -shift
                else:
                    continue
                ok = good if ok is None else jnp.logical_and(ok, good)

            @pl.when(ok)
            def _():
                act(self.copy(at))

    def start(self):
        self.each(1, lambda c: c.start())

    def arrive(self):
        self.each(-1, lambda c: c.wait_recv())

    def drain(self):
        self.each(1, lambda c: c.wait_send())


def block_dirs(planes, first, halo, row, rows, dps, djs, wide, mid=()):
    out = []
    for dj in djs:
        for dp in dps:
            if dp == 0 and dj == 0:
                continue
            if dp > 0:
                x0 = max(0, planes * dp - halo)
                count = planes - x0
            elif dp < 0:
                x0 = 0
                count = min(planes, planes + halo + planes * dp)
            else:
                x0, count = 0, planes
            if dj == 0:
                low, size = (row - 8, rows + 16) if wide else (row, rows)
                to = low
            elif dj > 0:
                low, size, to = row + rows - 8, 8, row - 8
            else:
                low, size, to = row, 8, row + rows
            a = first + x0
            src = (pl.ds(a, count),) + mid + (pl.ds(low, size),)
            dst = (pl.ds(a - planes * dp, count),) + mid + (pl.ds(to, size),)
            out.append((dp, dj, src, dst))
    return out


def line(ref, start):
    return ref[pl.ds(start, 8, stride=2)]


def kernel(
    iterate, right_side, diffusion, out,
    va, cc, gg, tmp,
    vb, dd, jj, di, wx, wl, wr, zl, zr, pre,
    s1, c1, k1, va1, vb1, d1, j1, i1, wx1, wl1, wr1, zl1, zr1,
    s2, c2, k2, va2, vb2, d2, j2, i2, wx2, wl2, wr2, zl2, zr2,
    s3, c3, va3, vb3, d3, j3, i3, wx3, wl3, wr3, zl3, zr3,
    x_send, x_recv, self_sem,
    s1_send, s1_recv, s2_send, s2_recv,
    y_send, y_recv, h_send, h_recv, g_send, g_recv, o_send, o_recv,
):
    i = lax.axis_index("gx")
    j = lax.axis_index("gy")
    k = lax.axis_index("gz")
    p = 2 * i + k
    place = (p, j)

    barrier = pltpu.get_barrier_semaphore()

    def greet(to, tj):
        pl.semaphore_signal(
            barrier, inc=1, device_id=(to // 2, tj, to % 2), device_id_type=MESH
        )

    loop(1, NP, lambda q: greet((p + q) % NP, j))
    count = NP - 1
    for dj in (-1, 1, -2, 2):
        okj = jnp.logical_and(j + dj >= 0, j + dj < NJ)
        for dp in range(-3, 4) if abs(dj) == 1 else (0,):
            ok = jnp.logical_and(okj, jnp.logical_and(p + dp >= 0, p + dp < NP))
            count = count + ok.astype(jnp.int32)

            @pl.when(ok)
            def _():
                greet(p + dp, j + dj)

    pl.semaphore_wait(barrier, count)

    def fine_moves(at, src, dst, halo):
        n = 8 + halo
        sends = []

        def copy(slot_s, slot_r, x0, nx, a0, low, size, to, zh, dev):
            return pltpu.make_async_remote_copy(
                src_ref=src.at[pl.ds(x0, nx), pl.ds(low, size)],
                dst_ref=dst.at[pl.ds(a0, nx), zh, pl.ds(to, size)],
                send_sem=x_send.at[at, slot_s],
                recv_sem=x_recv.at[at, slot_r],
                device_id=dev,
                device_id_type=MESH,
            )

        mine = pltpu.make_async_copy(
            src.at[pl.ds(k * (8 - halo), n)],
            dst.at[pl.ds(5 - halo * k, n), k, pl.ds(16, 64)],
            self_sem.at[at],
        )
        other = 1 - k
        sends.append((None, copy(0, 0, other * (8 - halo), n, 5 - halo * other, 0, 64, 16, k, (i, j, other))))
        rows = [(0, 0, 64, 16), (1, 56, 8, 8), (-1, 0, 8, 80)]
        for dj, low, size, to in rows:
            okj = jnp.logical_and(j + dj >= 0, j + dj < NJ)
            turn = {0: 0, 1: 1, -1: 2}[dj]
            up = jnp.logical_and(i < 7, okj)
            down = jnp.logical_and(i > 0, okj)
            slot = 1 + 2 * turn + k
            sends.append((up, copy(1 + 2 * turn, slot, 16 - halo, halo, 5 - halo, low, size, to, k, (i + 1, j + dj, 0))))
            sends.append((down, copy(2 + 2 * turn, slot, 0, halo, 13, low, size, to, k, (i - 1, j + dj, 1))))
            if dj != 0:
                for half in (0, 1):
                    sends.append(
                        (okj, copy(5 + 2 * turn + half, 5 + 2 * turn + k, half * (8 - halo), n, 5 - halo * half, low, size, to, k, (i, j + dj, half)))
                    )

        def start():
            mine.start()
            for ok, c in sends:
                if ok is None:
                    c.start()
                else:
                    pl.when(ok)(c.start)

        def arrive():
            mine.wait()
            copy(0, 0, 0, n, 5 - halo * k, 0, 64, 16, other, (i, j, other)).wait_recv()
            beside = jnp.logical_or(jnp.logical_and(k == 0, i > 0), jnp.logical_and(k == 1, i < 7))
            a0 = (5 - halo) * (1 - k) + 13 * k
            for dj, low, size, to in rows:
                turn = {0: 0, 1: 1, -1: 2}[dj]
                okj = jnp.logical_and(j - dj >= 0, j - dj < NJ)
                ok = jnp.logical_and(beside, okj)
                for half in (0, 1):
                    pl.when(ok)(copy(0, 1 + 2 * turn + half, 0, halo, a0, low, size, to, half, (i, j, other)).wait_recv)
                    if dj != 0:
                        pl.when(okj)(copy(0, 5 + 2 * turn + half, 0, n, 5 - halo * k, low, size, to, half, (i, j, other)).wait_recv)

        def drain():
            for ok, c in sends:
                if ok is None:
                    c.wait_send()
                else:
                    pl.when(ok)(c.wait_send)

        return start, arrive, drain

    moves_c = fine_moves(0, diffusion, cc, 5)
    moves_v = fine_moves(1, iterate, va, 5)
    moves_g = fine_moves(2, right_side, gg, 4)
    moves_c[0]()
    moves_v[0]()
    moves_g[0]()

    def clear(ref, planes, low_planes, high_from, edges, own=None):
        def wipe(a):
            ref[a] = jnp.zeros(ref.shape[1:], F32)

        loop(0, low_planes, wipe)
        loop(high_from, planes, wipe)

        def wipe_rows(low, size):
            def one(a):
                if len(ref.shape) == 4:
                    ref[a, :, low:low + size] = jnp.zeros((2, size, 128), F32)
                else:
                    ref[a, low:low + size] = jnp.zeros((size, 128), F32)

            loop(*(own or (0, planes)), one)

        for test, low, size in edges:
            pl.when(test)(lambda low=low, size=size: wipe_rows(low, size))

    def outer(first, planes, per, total):
        low = jnp.clip(first - per * p, 0, planes)
        high = jnp.clip(total - per * p + first, 0, planes)
        return low, high

    low, high = outer(5, 18, 8, 128)
    for ref in (va, cc, gg):
        clear(ref, 18, low, high, [(j == 0, 8, 8), (j == 7, 80, 8)])
    clear(pre, 18, low, high, [(j == 0, 8, 8), (j == 7, 80, 8)], (5, 13))
    low, high = outer(6, 16, 4, 64)
    for ref, own in ((s1, None), (c1, (6, 10)), (k1, (6, 10))):
        clear(ref, 16, low, high, [(j == 0, 8, 8), (j == 7, 48, 8)], own)
    low, high = outer(7, 16, 2, 32)
    for ref, own in ((s2, None), (c2, (7, 9)), (k2, (7, 9))):
        clear(ref, 16, low, high, [(j == 0, 8, 8), (j == 7, 32, 8)], own)
    for ref in (s3, c3):
        clear(ref, 18, 1, 17, [(j == 0, 8, 16), (j == 1, 8, 8), (j == 6, 40, 8), (j == 7, 32, 16)], (p + 1, p + 2))
    for ref in (va3, vb3):
        clear(ref, 18, 1, 17, [])

    def fold_rows(ref, at):
        return line(ref, 16 * at) + line(ref, 16 * at + 1)

    def fold_lanes(value, step):
        even = (lanes(value.shape) // step) % 2 == 0
        return value + jnp.where(even, pltpu.roll(value, 128 - step, 1), pltpu.roll(value, step, 1))

    def pack(halves, at):
        low, high = (fold_lanes(fold_rows(half, at), 1) for half in halves)
        from_lane = (2 * lanes((8, 128))) % 128
        low = jnp.take_along_axis(low, from_lane, axis=1)
        high = jnp.take_along_axis(high, from_lane, axis=1)
        return 0.125 * jnp.where(lanes((8, 128)) < 64, low, high)

    own = slice(16, 80)
    moves_c[1]()

    def coarsen_c(m):
        a = 5 + 2 * m
        for h in range(2):
            tmp[m, h] = cc[a, h, own] + cc[a + 1, h, own]
        for t in range(4):
            c1[6 + m, 16 + 8 * t:24 + 8 * t] = pack((tmp.at[m, 0], tmp.at[m, 1]), t)

    for m in range(4):
        coarsen_c(m)
    for m in range(2):
        tmp[m, 0, 0:32] = c1[6 + 2 * m, 16:48] + c1[7 + 2 * m, 16:48]
        for t in range(2):
            c2[7 + m, 16 + 8 * t:24 + 8 * t] = 0.125 * fold_lanes(fold_rows(tmp.at[m, 0], t), 1)
    tmp[2, 0, 0:16] = c2[7, 16:32] + c2[8, 16:32]
    c3[p + 1, 24:32] = 0.125 * fold_lanes(fold_rows(tmp.at[2, 0], 0), 2)

    def y_moves(at, ref, planes, first, row, rows, mid=()):
        dirs = block_dirs(planes, first, 0, row, rows, (0,), (-1, 1), False, mid)
        return Moves(place, ref, y_send.at[at], y_recv.at[at], dirs)

    def h_moves(at, ref, planes, first, halo, row, rows, reach, mid=()):
        dps = [d for d in range(-reach, reach + 1) if d != 0]
        dirs = block_dirs(planes, first, halo, row, rows, dps, (0,), True, mid)
        return Moves(place, ref, h_send.at[at], h_recv.at[at], dirs)

    def column_moves(at, ref):
        here = (p + 1, pl.ds(24, 8))
        dirs = [(0, dj, here, (p + 1, pl.ds(24 - 8 * dj, 8))) for dj in (-2, -1, 1, 2)]
        return Moves(place, ref, y_send.at[at], y_recv.at[at], dirs)

    class Around:
        def __init__(self, at, ref):
            self.at, self.ref = at, ref

        def copy(self, q, plane):
            to = (p + q) % NP
            return pltpu.make_async_remote_copy(
                src_ref=self.ref.at[plane, pl.ds(8, 40)],
                dst_ref=self.ref.at[plane, pl.ds(8, 40)],
                send_sem=g_send.at[self.at, q],
                recv_sem=g_recv.at[self.at, q],
                device_id=(to // 2, j, to % 2),
                device_id_type=MESH,
            )

        def start(self):
            loop(1, NP, lambda q: self.copy(q, p + 1).start())

        def arrive(self):
            loop(1, NP, lambda q: self.copy(q, (p - q + NP) % NP + 1).wait_recv())

        def drain(self):
            loop(1, NP, lambda q: self.copy(q, p + 1).wait_send())

    y_c1 = y_moves(0, c1, 4, 6, 16, 32)
    y_c2 = y_moves(1, c2, 2, 7, 16, 16)
    y_c3 = column_moves(2, c3)
    h_c1 = h_moves(0, c1, 4, 6, 6, 16, 32, 2)
    h_c2 = h_moves(1, c2, 2, 7, 7, 16, 16, 4)
    h_c3 = Around(0, c3)
    y_pre = y_moves(3, pre, 8, 5, 16, 64, (slice(None),))
    h_pre = h_moves(2, pre, 8, 5, 4, 16, 64, 1, (slice(None),))
    y_k1 = y_moves(4, k1, 4, 6, 16, 32)
    h_k1 = h_moves(3, k1, 4, 6, 6, 16, 32, 2)
    y_k2 = y_moves(5, k2, 2, 7, 16, 16)
    h_k2 = h_moves(4, k2, 2, 7, 7, 16, 16, 4)
    y_s3 = column_moves(6, s3)
    h_s3 = Around(1, s3)
    m_s1 = Moves(place, s1, s1_send, s1_recv, block_dirs(4, 6, 5, 16, 32, range(-2, 3), (0, -1, 1), False))
    m_s2 = Moves(place, s2, s2_send, s2_recv, block_dirs(2, 7, 6, 16, 16, range(-3, 4), (0, -1, 1), False))

    y_c1.start()
    y_c2.start()
    y_c3.start()

    wide = slice(12, 84)
    lane = lanes((72, 128))

    def fine_setup(low, n):
        for a in [low + u for u in range(n)]:
            mid = [cc[a, h, wide] for h in range(2)]
            prev = [pltpu.roll(m, 1, 1) for m in mid]
            foll = [pltpu.roll(m, 127, 1) for m in mid]
            left = (jnp.where(lane == 0, 0.0, prev[0]), jnp.where(lane == 0, prev[0], prev[1]))
            right = (jnp.where(lane == 127, foll[1], foll[0]), jnp.where(lane == 127, 0.0, foll[1]))
            for h in range(2):
                ahead = cc[a + 1, h, wide]
                yl = cc[a, h, 11:83]
                yr = cc[a, h, 13:85]
                wx[a, h, wide] = 0.5 * (mid[h] + ahead)
                wl[a, h, wide] = 0.5 * (mid[h] + yl)
                wr[a, h, wide] = 0.5 * (mid[h] + yr)
                low_edge = 0.5 * (mid[h] + left[h])
                high_edge = 0.5 * (mid[h] + right[h])
                zl[a, h, wide] = jnp.where(lane == 0, 0.0, low_edge) if h == 0 else low_edge
                zr[a, h, wide] = jnp.where(lane == 127, 0.0, high_edge) if h == 1 else high_edge
                diag = 0.5 * (6.0 * mid[h] + (cc[a - 1, h, wide] + ahead) + (yl + yr) + (left[h] + right[h]))
                di[a, h, wide] = diag
                jj[a, h, wide] = jnp.where(mid[h] > 0.0, 1.0 / diag, 0.0)

    wx[0, :, wide] = 0.5 * (cc[0, :, wide] + cc[1, :, wide])
    spread(1, 16, 2, fine_setup)

    moves_v[1]()
    moves_g[1]()

    def fine_sum(src, low, n, r0, r1):
        for r in range(r0, r1, 24 if (r1 - r0) % 24 == 0 else 32):
            e = r + (24 if (r1 - r0) % 24 == 0 else 32)
            w = slice(r, e)
            spot = lanes((e - r, 128))
            v = [[src[low + u, h, w] for h in range(2)] for u in range(-1, n + 1)]
            x = [[wx[low + u, h, w] for h in range(2)] for u in range(-1, n)]
            for u in range(n):
                a = low + u
                mid = v[u + 1]
                prev = [pltpu.roll(m, 1, 1) for m in mid]
                foll = [pltpu.roll(m, 127, 1) for m in mid]
                left = (prev[0], jnp.where(spot == 0, prev[0], prev[1]))
                right = (jnp.where(spot == 127, foll[1], foll[0]), foll[1])
                for h in range(2):
                    total = gg[a, h, w] + x[u][h] * v[u][h] + x[u + 1][h] * v[u + 2][h]
                    total = total + wl[a, h, w] * src[a, h, r - 1:e - 1] + wr[a, h, w] * src[a, h, r + 1:e + 1]
                    total = total + zl[a, h, w] * left[h] + zr[a, h, w] * right[h]
                    yield u, a, h, w, mid[h], total

    def fine_sweep(src, dst, step, halo):
        keep, new = FINE_STEPS[step]

        def run(low, n):
            for u, a, h, w, mid, total in fine_sum(src, low, n, 12, 84):
                move = new * (jj[a, h, w] * total - mid)
                if step > 0:
                    move = move + keep * dd[a, h, w]
                dd[a, h, w] = move
                dst[a, h, w] = mid + move

        spread(5 - halo, 8 + 2 * halo, 4, run)

    fine_sweep(va, vb, 0, 4)
    fine_sweep(vb, va, 1, 3)
    y_c1.arrive()
    y_c2.arrive()
    y_c3.arrive()
    h_c1.start()
    h_c2.start()
    h_c3.start()
    fine_sweep(va, vb, 2, 2)
    fine_sweep(vb, va, 3, 1)

    for m in range(4):
        for u, a, h, w, mid, total in fine_sum(va, 5 + 2 * m, 2, 16, 80):
            part = total - di[a, h, w] * mid
            spot = slice(w.start - 16, w.stop - 16)
            tmp[m, h, spot] = part if u == 0 else tmp[m, h, spot] + part
        for t in range(4):
            s1[6 + m, 16 + 8 * t:24 + 8 * t] = pack((tmp.at[m, 0], tmp.at[m, 1]), t)

    m_s1.start()

    def keep_fine(a):
        pre[a, :, own] = va[a, :, own]

    loop(5, 13, keep_fine)
    y_pre.start()

    def setup(c, jn, dn, wxn, wln, wrn, zln, zrn, planes, rows, step, scale):
        low, high = planes
        r0, r1 = rows
        w = slice(r0, r1)
        spot = lanes((r1 - r0, 128))
        half = 0.5 * scale

        def run(first_plane, n):
            for a in [first_plane + u for u in range(n)]:
                mid = c[a, w]
                ahead = c[a + 1, w]
                left = jnp.where(spot < step, 0.0, pltpu.roll(mid, step, 1))
                right = jnp.where(spot >= 128 - step, 0.0, pltpu.roll(mid, 128 - step, 1))
                yl = c[a, r0 - 1:r1 - 1]
                yr = c[a, r0 + 1:r1 + 1]
                wxn[a, w] = half * (mid + ahead)
                wln[a, w] = half * (mid + yl)
                wrn[a, w] = half * (mid + yr)
                zln[a, w] = jnp.where(spot < step, 0.0, half * (mid + left))
                zrn[a, w] = jnp.where(spot >= 128 - step, 0.0, half * (mid + right))
                diag = half * (6.0 * mid + (c[a - 1, w] + ahead) + (yl + yr) + (left + right))
                dn[a, w] = diag
                jn[a, w] = jnp.where(mid > 0.0, 1.0 / diag, 0.0)

        wxn[low - 1, w] = half * (c[low - 1, w] + c[low, w])
        spread(low, high - low, 7 if high - low == 14 else 8, run)

    def gather_sum(src, low, n, g, wxn, wln, wrn, zln, zrn, rows, step):
        r0, r1 = rows
        w = slice(r0, r1)
        v = [src[low + u, w] for u in range(-1, n + 1)]
        x = [wxn[low + u, w] for u in range(-1, n)]
        for u in range(n):
            a = low + u
            mid = v[u + 1]
            total = g[a, w] + x[u] * v[u] + x[u + 1] * v[u + 2]
            total = total + wln[a, w] * src[a, r0 - 1:r1 - 1] + wrn[a, w] * src[a, r0 + 1:r1 + 1]
            total = total + zln[a, w] * pltpu.roll(mid, step, 1) + zrn[a, w] * pltpu.roll(mid, 128 - step, 1)
            yield a, mid, total

    def sweep(src, dst, d, jn, ws, planes, rows, step, pair):
        keep, new = pair
        w = slice(*rows)

        def run(low, n):
            for a, mid, total in gather_sum(src, low, n, *ws, rows, step):
                move = new * (jn[a, w] * total - mid)
                if keep != 0.0:
                    move = move + keep * d[a, w]
                d[a, w] = move
                dst[a, w] = mid + move

        spread(planes[0], planes[1] - planes[0], 8, run)

    def first(dst, d, g, jn, planes, rows, new):
        w = slice(*rows)

        for a in range(*planes):
            move = new * (jn[a, w] * g[a, w])
            d[a, w] = move
            dst[a, w] = move

    ws1 = (s1, wx1, wl1, wr1, zl1, zr1)
    ws2 = (s2, wx2, wl2, wr2, zl2, zr2)
    ws3 = (s3, wx3, wl3, wr3, zl3, zr3)
    rows1, rows2, rows3 = (8, 56), (8, 40), (8, 48)

    h_c1.arrive()
    setup(c1, j1, i1, wx1, wl1, wr1, zl1, zr1, (1, 15), rows1, 1, 0.25)
    h_c2.arrive()
    setup(c2, j2, i2, wx2, wl2, wr2, zl2, zr2, (1, 15), rows2, 2, 0.0625)
    h_c3.arrive()
    setup(c3, j3, i3, wx3, wl3, wr3, zl3, zr3, (1, 17), rows3, 4, 0.015625)

    m_s1.arrive()
    first(va1, d1, s1, j1, (2, 14), rows1, FINE_STEPS[0][1])
    sweep(va1, vb1, d1, j1, ws1, (3, 13), rows1, 1, FINE_STEPS[1])
    sweep(vb1, va1, d1, j1, ws1, (4, 12), rows1, 1, FINE_STEPS[2])
    sweep(va1, vb1, d1, j1, ws1, (5, 11), rows1, 1, FINE_STEPS[3])

    def residual(src, low, ws, dn, rows, step):
        parts = [total - dn[a, slice(*rows)] * mid for a, mid, total in gather_sum(src, low, 2, *ws, rows, step)]
        return parts[0] + parts[1]

    for m in range(2):
        tmp[m, 0, 0:32] = residual(vb1, 6 + 2 * m, ws1, i1, (16, 48), 1)
    for m in range(2):
        for t in range(2):
            s2[7 + m, 16 + 8 * t:24 + 8 * t] = 0.125 * fold_lanes(fold_rows(tmp.at[m, 0], t), 1)
    m_s2.start()
    k1[6:10, 16:48] = vb1[6:10, 16:48]
    y_k1.start()
    y_pre.arrive()
    h_pre.start()

    m_s2.arrive()
    first(va2, d2, s2, j2, (3, 13), rows2, FINE_STEPS[0][1])
    sweep(va2, vb2, d2, j2, ws2, (4, 12), rows2, 2, FINE_STEPS[1])
    sweep(vb2, va2, d2, j2, ws2, (5, 11), rows2, 2, FINE_STEPS[2])
    sweep(va2, vb2, d2, j2, ws2, (6, 10), rows2, 2, FINE_STEPS[3])
    tmp[2, 0, 0:16] = residual(vb2, 7, ws2, i2, (16, 32), 2)
    s3[p + 1, 24:32] = 0.125 * fold_lanes(fold_rows(tmp.at[2, 0], 0), 2)
    y_s3.start()
    k2[7:9, 16:32] = vb2[7:9, 16:32]
    y_k2.start()
    y_k1.arrive()
    h_k1.start()
    y_s3.arrive()
    h_s3.start()
    y_k2.arrive()
    h_k2.start()

    h_s3.arrive()
    first(va3, d3, s3, j3, (1, 17), rows3, BOTTOM_STEPS[0][1])
    here, there = va3, vb3
    for at in range(1, BOTTOM):
        halo = BOTTOM + 3 - at
        rows = (12, 44) if halo > 8 else (16, 40)
        sweep(here, there, d3, j3, ws3, (1, 17), rows, 4, BOTTOM_STEPS[at])
        here, there = there, here

    h_k2.arrive()

    def finish2(a):
        up = jnp.clip(p - 3 + (a + 1) // 2, 0, 17)
        for t in range(2):
            e = here[up, 20 + 8 * t:28 + 8 * t]
            for odd in range(2):
                at = pl.ds(8 + 16 * t + odd, 8, stride=2)
                va2[a, at] = k2[a, at] + e

    for a in range(16):
        finish2(a)
    sweep(va2, vb2, d2, j2, ws2, (1, 15), rows2, 2, FINE_STEPS[0])
    sweep(vb2, va2, d2, j2, ws2, (2, 14), rows2, 2, FINE_STEPS[1])
    sweep(va2, vb2, d2, j2, ws2, (3, 13), rows2, 2, FINE_STEPS[2])
    sweep(vb2, va2, d2, j2, ws2, (4, 12), rows2, 2, FINE_STEPS[3])

    h_k1.arrive()

    def finish1(a):
        up = 4 + a // 2
        for t in range(3):
            e = va2[up, 12 + 8 * t:20 + 8 * t]
            for odd in range(2):
                at = pl.ds(8 + 16 * t + odd, 8, stride=2)
                va1[a, at] = k1[a, at] + e

    for a in range(16):
        finish1(a)
    sweep(va1, vb1, d1, j1, ws1, (1, 15), rows1, 1, FINE_STEPS[0])
    sweep(vb1, va1, d1, j1, ws1, (2, 14), rows1, 1, FINE_STEPS[1])
    sweep(va1, vb1, d1, j1, ws1, (3, 13), rows1, 1, FINE_STEPS[2])
    sweep(vb1, va1, d1, j1, ws1, (4, 12), rows1, 1, FINE_STEPS[3])

    h_pre.arrive()

    def finish0(m):
        for t in range(5):
            e = va1[4 + m, 14 + 8 * t:22 + 8 * t]
            to_lane = lanes((8, 128)) // 2
            for h in range(2):
                half = jnp.take_along_axis(e, to_lane + 64 * h, axis=1)
                for x in range(2):
                    a = 1 + 2 * m + x
                    for odd in range(2):
                        at = pl.ds(12 + 16 * t + odd, 8, stride=2)
                        va[a, h, at] = pre[a, h, at] + half

    loop(0, 8, finish0)
    fine_sweep(va, vb, 0, 3)
    fine_sweep(vb, va, 1, 2)
    fine_sweep(va, vb, 2, 1)
    fine_sweep(vb, va, 3, 0)

    give = pltpu.make_async_remote_copy(
        src_ref=va.at[pl.ds(5, 8), 1 - k, pl.ds(16, 64)],
        dst_ref=out.at[pl.ds(8 * k, 8)],
        send_sem=o_send,
        recv_sem=o_recv,
        device_id=(i, j, 1 - k),
        device_id_type=MESH,
    )
    give.start()
    out[pl.ds(8 * k, 8)] = va[5:13, k, own]
    give.wait_send()
    pltpu.make_async_remote_copy(
        src_ref=va.at[pl.ds(5, 8), k, pl.ds(16, 64)],
        dst_ref=out.at[pl.ds(8 * (1 - k), 8)],
        send_sem=o_send,
        recv_sem=o_recv,
        device_id=(i, j, 1 - k),
        device_id_type=MESH,
    ).wait_recv()

    for moves in (moves_c, moves_v, moves_g):
        moves[2]()
    for moves in (y_c1, y_c2, y_c3, h_c1, h_c2, h_c3, m_s1, y_pre, h_pre, m_s2, y_k1, h_k1, y_s3, h_s3, y_k2, h_k2):
        moves.drain()


def on_device(iterate, right_side, diffusion):
    def buf(*shape):
        return pltpu.VMEM(shape, F32)

    scratch = [buf(18, 2, 96, 128)] * 3 + [buf(4, 2, 64, 128)] + [buf(18, 2, 96, 128)] * 10
    scratch += [buf(16, 64, 128)] * 13
    scratch += [buf(16, 48, 128)] * 13
    scratch += [buf(18, 56, 128)] * 12
    dma = pltpu.SemaphoreType.DMA
    scratch += [dma((3, 11)), dma((3, 11)), dma((3,))]
    scratch += [dma((14,)), dma((14,)), dma((20,)), dma((20,))]
    scratch += [dma((7, 4)), dma((7, 4)), dma((5, 8)), dma((5, 8)), dma((2, NP)), dma((2, NP)), dma, dma]
    return pl.pallas_call(
        kernel,
        out_shape=jax.ShapeDtypeStruct((16, 64, 128), F32),
        in_specs=[pl.BlockSpec(memory_space=pl.ANY)] * 3,
        out_specs=pl.BlockSpec(memory_space=pltpu.VMEM),
        scratch_shapes=scratch,
        compiler_params=pltpu.CompilerParams(
            collective_id=0, has_side_effects=True, vmem_limit_bytes=60 * 2**20
        ),
        cost_estimate=pl.CostEstimate(flops=10**8, bytes_accessed=2 * 10**6, transcendentals=0),
        name="vcycle",
    )(iterate, right_side, diffusion)


def solution(mesh):
    placed = (P("gx", "gy", "gz"), P("gx", "gy", "gz"), P("gx", "gy", "gz"))
    return jax.shard_map(
        on_device, mesh=mesh, in_specs=placed, out_specs=P("gx", "gy", "gz"), check_vma=False
    )
```

```python
import jax
import jax.numpy as jnp
from jax import lax
from jax.experimental import pallas as pl
from jax.experimental.pallas import tpu as pltpu
from jax.sharding import PartitionSpec as P

DEGREE = 4
BOTTOM = 8
SMOOTH_LOW = 0.25
SMOOTH_HIGH = 2.0
BOTTOM_LOW = 0.05

F32 = jnp.float32
MESH = pl.DeviceIdType.MESH
NP = 16
NJ = 8
FINE_SEND = 0
FINE_RECV = 107
SEMS = 107 + 33 + 8 + 27 + 8 + 4 + 14 + 6 + 4 + 4 + 15 + 2 + 8 + 1


def chebyshev_steps(sweeps, low_end, high_end):
    center = 0.5 * (high_end + low_end)
    radius = 0.5 * (high_end - low_end)
    sigma_ratio = center / radius
    rho_old = 1.0 / sigma_ratio
    steps_out = [(0.0, 1.0 / center)]
    for sweep_index in range(1, sweeps):
        rho_new = 1.0 / (2.0 * sigma_ratio - rho_old)
        steps_out.append((rho_new * rho_old, 2.0 * rho_new / radius))
        rho_old = rho_new
    return steps_out


FINE_STEPS = chebyshev_steps(DEGREE, SMOOTH_LOW, SMOOTH_HIGH)
BOTTOM_STEPS = chebyshev_steps(BOTTOM, BOTTOM_LOW, SMOOTH_HIGH)


def loop(low, high, body):
    def step(index, carry):
        body(index)
        return carry

    lax.fori_loop(low, high, step, 0)


def spread(low, count, most, body):
    runs = -(-count // most)
    each = -(-count // runs)
    full = count // each
    if full > 1:
        loop(0, full, lambda r: body(low + r * each, each))
    elif full == 1:
        body(low, each)
    if count % each:
        body(low + full * each, count % each)


def lanes(shape):
    return lax.broadcasted_iota(jnp.int32, shape, len(shape) - 1)


class Moves:
    def __init__(self, place, ref, sem, send, recv, dirs):
        self.place, self.ref, self.sem, self.dirs = place, ref, sem, dirs
        self.send, self.recv = send, recv

    def copy(self, at):
        p, j = self.place
        dp, dj, src, dst = self.dirs[at]
        to = p + dp
        return pltpu.make_async_remote_copy(
            src_ref=self.ref.at[src],
            dst_ref=self.ref.at[dst],
            send_sem=self.sem.at[self.send + at],
            recv_sem=self.sem.at[self.recv + at],
            device_id=(to // 2, j + dj, to % 2),
            device_id_type=MESH,
        )

    def each(self, sign, act):
        p, j = self.place
        for at, (dp, dj, src, dst) in enumerate(self.dirs):
            ok = None
            for value, count, shift in ((p, NP, sign * dp), (j, NJ, sign * dj)):
                if shift > 0:
                    good = value < count - shift
                elif shift < 0:
                    good = value >= -shift
                else:
                    continue
                ok = good if ok is None else jnp.logical_and(ok, good)

            @pl.when(ok)
            def _():
                act(self.copy(at))

    def start(self):
        self.each(1, lambda c: c.start())

    def arrive(self):
        self.each(-1, lambda c: c.wait_recv())

    def drain(self):
        self.each(1, lambda c: c.wait_send())


def block_dirs(planes, first, halo, row, rows, dps, djs, wide, mid=()):
    out = []
    for dj in djs:
        for dp in dps:
            if dp == 0 and dj == 0:
                continue
            if dp > 0:
                x0 = max(0, planes * dp - halo)
                count = planes - x0
            elif dp < 0:
                x0 = 0
                count = min(planes, planes + halo + planes * dp)
            else:
                x0, count = 0, planes
            if dj == 0:
                low, size = (row - 8, rows + 16) if wide else (row, rows)
                to = low
            elif dj > 0:
                low, size, to = row + rows - 8, 8, row - 8
            else:
                low, size, to = row, 8, row + rows
            a = first + x0
            src = (pl.ds(a, count),) + mid + (pl.ds(low, size),)
            dst = (pl.ds(a - planes * dp, count),) + mid + (pl.ds(to, size),)
            out.append((dp, dj, src, dst))
    return out


def line(ref, start):
    return ref[pl.ds(start, 8, stride=2)]


def kernel(
    iterate, right_side, diffusion, out,
    va, cc, gg, tmp, vb, vc, vd, ve,
    dd, jj, di, wx, wl, wr, zl, zr, pre,
    s1, c1, k1, va1, vb1, d1, j1, i1, wx1, wl1, wr1, zl1, zr1,
    s2, c2, k2, va2, vb2, d2, j2, i2, wx2, wl2, wr2, zl2, zr2, pc2, pk2,
    s3, c3, va3, vb3, d3, j3, i3, wx3, wl3, wr3, zl3, zr3, pc3, ps3,
    sem, self_sem,
):
    i = lax.axis_index("gx")
    j = lax.axis_index("gy")
    k = lax.axis_index("gz")
    p = 2 * i + k
    place = (p, j)

    barrier = pltpu.get_barrier_semaphore()

    def greet(to, tj):
        pl.semaphore_signal(
            barrier, inc=1, device_id=(to // 2, tj, to % 2), device_id_type=MESH
        )

    loop(1, NP, lambda q: greet((p + q) % NP, j))
    count = NP - 1
    for dj in (-1, 1, -2, 2):
        okj = jnp.logical_and(j + dj >= 0, j + dj < NJ)
        for dp in range(-2, 3) if abs(dj) == 1 else (0,):
            ok = jnp.logical_and(okj, jnp.logical_and(p + dp >= 0, p + dp < NP))
            count = count + ok.astype(jnp.int32)

            @pl.when(ok)
            def _():
                greet(p + dp, j + dj)

    pl.semaphore_wait(barrier, count)

    def fine_moves(at, src, dst, halo):
        n = 8 + halo

        def copy(slot_s, slot_r, x0, nx, a0, low, size, to, zh, dev):
            return pltpu.make_async_remote_copy(
                src_ref=src.at[pl.ds(x0, nx), pl.ds(low, size)],
                dst_ref=dst.at[pl.ds(a0, nx), zh, pl.ds(to, size)],
                send_sem=sem.at[FINE_SEND + 11 * at + slot_s],
                recv_sem=sem.at[FINE_RECV + 11 * at + slot_r],
                device_id=dev,
                device_id_type=MESH,
            )

        mine = pltpu.make_async_copy(
            src.at[pl.ds(k * (8 - halo), n)],
            dst.at[pl.ds(5 - halo * k, n), k, pl.ds(16, 64)],
            self_sem.at[at],
        )
        other = 1 - k
        corner = halo - 1
        ny = 8 + corner
        sends = []
        rows = [(0, 0, 64, 16), (1, 56, 8, 8), (-1, 0, 8, 80)]
        for dj, low, size, to in rows:
            okj = jnp.logical_and(j + dj >= 0, j + dj < NJ)
            turn = {0: 0, 1: 1, -1: 2}[dj]
            up = jnp.logical_and(i < 7, okj)
            down = jnp.logical_and(i > 0, okj)
            slot = 1 + 2 * turn + k
            w = halo if dj == 0 else corner
            sends.append((up, copy(1 + 2 * turn, slot, 16 - w, w, 5 - w, low, size, to, k, (i + 1, j + dj, 0))))
            sends.append((down, copy(2 + 2 * turn, slot, 0, w, 13, low, size, to, k, (i - 1, j + dj, 1))))
            if dj != 0:
                for half in (0, 1):
                    sends.append(
                        (okj, copy(5 + 2 * turn + half, 5 + 2 * turn + k, half * (8 - corner), ny, 5 - corner * half, low, size, to, k, (i, j + dj, half)))
                    )
        sends.append((None, copy(0, 0, other * (8 - halo), n, 5 - halo * other, 0, 64, 16, k, (i, j, other))))

        def start():
            mine.start()
            for ok, c in sends:
                if ok is None:
                    c.start()
                else:
                    pl.when(ok)(c.start)

        def arrive_inner():
            mine.wait()
            copy(0, 0, 0, n, 5 - halo * k, 0, 64, 16, other, (i, j, other)).wait_recv()
            for dj, low, size, to in rows[1:]:
                turn = {1: 1, -1: 2}[dj]
                okj = jnp.logical_and(j - dj >= 0, j - dj < NJ)
                for half in (0, 1):
                    pl.when(okj)(copy(0, 5 + 2 * turn + half, 0, ny, 5 - corner * k, low, size, to, half, (i, j, other)).wait_recv)

        def arrive_outer():
            beside = jnp.logical_or(jnp.logical_and(k == 0, i > 0), jnp.logical_and(k == 1, i < 7))
            for dj, low, size, to in rows:
                turn = {0: 0, 1: 1, -1: 2}[dj]
                okj = jnp.logical_and(j - dj >= 0, j - dj < NJ)
                ok = jnp.logical_and(beside, okj)
                w = halo if dj == 0 else corner
                a0 = (5 - w) * (1 - k) + 13 * k
                for half in (0, 1):
                    pl.when(ok)(copy(0, 1 + 2 * turn + half, 0, w, a0, low, size, to, half, (i, j, other)).wait_recv)

        def drain():
            for ok, c in sends:
                if ok is None:
                    c.wait_send()
                else:
                    pl.when(ok)(c.wait_send)

        return start, arrive_inner, arrive_outer, drain

    moves_c = fine_moves(0, diffusion, cc, 5)
    moves_v = fine_moves(1, iterate, va, 5)
    moves_g = fine_moves(2, right_side, gg, 4)
    moves_c[0]()
    moves_v[0]()
    moves_g[0]()

    def clear(ref, planes, low_planes, high_from, edges, own=None):
        def wipe(a):
            ref[a] = jnp.zeros(ref.shape[1:], F32)

        loop(0, low_planes, wipe)
        loop(high_from, planes, wipe)

        def wipe_rows(low, size):
            def one(a):
                if len(ref.shape) == 4:
                    ref[a, :, low:low + size] = jnp.zeros((2, size, 128), F32)
                else:
                    ref[a, low:low + size] = jnp.zeros((size, 128), F32)

            loop(*(own or (0, planes)), one)

        for test, low, size in edges:
            pl.when(test)(lambda low=low, size=size: wipe_rows(low, size))

    def outer(first, planes, per, total):
        low = jnp.clip(first - per * p, 0, planes)
        high = jnp.clip(total - per * p + first, 0, planes)
        return low, high

    low, high = outer(5, 18, 8, 128)
    for ref in (va, cc, gg):
        clear(ref, 18, low, high, [(j == 0, 8, 8), (j == 7, 80, 8)])
    clear(pre, 18, low, high, [(j == 0, 8, 8), (j == 7, 80, 8)], (5, 13))
    low, high = outer(6, 16, 4, 64)
    for ref, owned in ((s1, None), (c1, (6, 10)), (k1, (6, 10))):
        clear(ref, 16, low, high, [(j == 0, 8, 8), (j == 7, 48, 8)], owned)
    low, high = outer(7, 16, 2, 32)
    for ref, owned in ((s2, None), (c2, (7, 9)), (k2, (7, 9))):
        clear(ref, 16, low, high, [(j == 0, 8, 8), (j == 7, 32, 8)], owned)
    for ref in (pc2, pk2):
        clear(ref, 16, low, high, [])
    for ref in (s3, c3):
        clear(ref, 18, 1, 17, [(j == 0, 8, 16), (j == 1, 8, 8), (j == 6, 40, 8), (j == 7, 32, 16)], (p + 1, p + 2))
    for ref in (va3, vb3):
        clear(ref, 18, 1, 17, [])

    def fold_rows(ref, at):
        return line(ref, 16 * at) + line(ref, 16 * at + 1)

    def fold_lanes(value, step):
        even = (lanes(value.shape) // step) % 2 == 0
        return value + jnp.where(even, pltpu.roll(value, 128 - step, 1), pltpu.roll(value, step, 1))

    def pack(halves, at):
        low, high = (fold_lanes(fold_rows(half, at), 1) for half in halves)
        from_lane = (2 * lanes((8, 128))) % 128
        low = jnp.take_along_axis(low, from_lane, axis=1)
        high = jnp.take_along_axis(high, from_lane, axis=1)
        return 0.125 * jnp.where(lanes((8, 128)) < 64, low, high)

    def squeeze(ref, a, row, rows, parts):
        size = rows // parts
        spot = lanes((size, 128)) % parts
        res = ref[a, row:row + size]
        for q in range(1, parts):
            res = jnp.where(spot == q, ref[a, row + q * size:row + (q + 1) * size], res)
        return res

    def widen(src, dst, planes, row, rows, parts):
        size = rows // parts
        spot = lanes((8, 128))
        spot = spot - spot % parts
        for a in planes:
            for r in range(0, size, 8):
                value = src[a, r:r + 8]
                for q in range(parts):
                    at = row + q * size + r
                    dst[a, at:at + 8] = jnp.take_along_axis(value, spot + q, axis=1)

    own = slice(16, 80)
    moves_c[1]()

    def coarsen_c(m):
        a = 5 + 2 * m
        for h in range(2):
            tmp[m, h] = cc[a, h, own] + cc[a + 1, h, own]
        for t in range(4):
            c1[6 + m, 16 + 8 * t:24 + 8 * t] = pack((tmp.at[m, 0], tmp.at[m, 1]), t)

    for m in range(4):
        coarsen_c(m)
    for m in range(2):
        tmp[m, 0, 0:32] = c1[6 + 2 * m, 16:48] + c1[7 + 2 * m, 16:48]
        for t in range(2):
            c2[7 + m, 16 + 8 * t:24 + 8 * t] = 0.125 * fold_lanes(fold_rows(tmp.at[m, 0], t), 1)
    tmp[2, 0, 0:16] = c2[7, 16:32] + c2[8, 16:32]
    c3[p + 1, 24:32] = 0.125 * fold_lanes(fold_rows(tmp.at[2, 0], 0), 2)

    used = {"recv": FINE_RECV + 33, "send": 0}

    def moves(ref, send, dirs):
        recv = used["recv"]
        used["recv"] = recv + len(dirs)
        return Moves(place, ref, sem, send, recv, dirs)

    def y_moves(send, ref, planes, first, row, rows, mid=()):
        return moves(ref, send, block_dirs(planes, first, 0, row, rows, (0,), (-1, 1), False, mid))

    def h_moves(send, ref, planes, first, halo, row, rows, dps, mid=()):
        return moves(ref, send, block_dirs(planes, first, halo, row, rows, dps, (0,), True, mid))

    def column_moves(send, ref):
        here = (p + 1, pl.ds(24, 8))
        return moves(ref, send, [(0, dj, here, (p + 1, pl.ds(24 - 8 * dj, 8))) for dj in (-2, -1, 1, 2)])

    class Around:
        def __init__(self, send, ref):
            self.send, self.ref, self.recv = send, ref, used["recv"]
            used["recv"] += NP - 1

        def copy(self, q, plane):
            to = (p + q) % NP
            return pltpu.make_async_remote_copy(
                src_ref=self.ref.at[plane],
                dst_ref=self.ref.at[plane],
                send_sem=sem.at[self.send + q - 1],
                recv_sem=sem.at[self.recv + q - 1],
                device_id=(to // 2, j, to % 2),
                device_id_type=MESH,
            )

        def start(self):
            loop(1, NP, lambda q: self.copy(q, p + 1).start())

        def arrive(self):
            loop(1, NP, lambda q: self.copy(q, (p - q + NP) % NP + 1).wait_recv())

        def drain(self):
            loop(1, NP, lambda q: self.copy(q, p + 1).wait_send())

    y_c1 = y_moves(33, c1, 4, 6, 16, 32)
    y_c2 = y_moves(35, c2, 2, 7, 16, 16)
    y_c3 = column_moves(37, c3)
    h_c1 = h_moves(0, c1, 4, 6, 6, 16, 32, (-2, -1, 1, 2))
    h_c2 = h_moves(4, pc2, 2, 7, 7, 8, 0, (-4, -3, -2, -1, 1, 2, 3, 4))
    h_c3 = Around(12, pc3)
    m_s1 = moves(s1, 41, block_dirs(4, 6, 4, 16, 32, (-1, 0, 1), (0, -1, 1), False))
    y_pre = y_moves(49, pre, 8, 5, 16, 64, (slice(None),))
    h_pre = h_moves(51, pre, 8, 5, 4, 16, 64, (-1, 1), (slice(None),))
    m_s2 = moves(s2, 53, block_dirs(2, 7, 4, 16, 16, (-2, -1, 0, 1, 2), (0, -1, 1), False))
    y_k1 = y_moves(67, k1, 4, 6, 16, 32)
    h_k1 = h_moves(69, k1, 4, 6, 6, 16, 32, (-2, -1, 1, 2))
    h_s1 = h_moves(73, s1, 4, 6, 5, 16, 32, (-2, 2))
    h_s2 = h_moves(75, s2, 2, 7, 6, 16, 16, (-3, 3))
    y_s3 = column_moves(77, s3)
    h_s3 = Around(81, ps3)
    y_k2 = y_moves(96, k2, 2, 7, 16, 16)
    h_k2 = h_moves(98, pk2, 2, 7, 7, 8, 0, (-4, -3, -2, -1, 1, 2, 3, 4))
    out_send, out_recv = 106, used["recv"]
    assert out_recv < SEMS, out_recv

    y_c1.start()
    y_c2.start()
    y_c3.start()

    wide = slice(12, 84)
    lane = lanes((72, 128))

    def fine_setup(low, n):
        for a in [low + u for u in range(n)]:
            mid = [cc[a, h, wide] for h in range(2)]
            prev = [pltpu.roll(m, 1, 1) for m in mid]
            foll = [pltpu.roll(m, 127, 1) for m in mid]
            left = (jnp.where(lane == 0, 0.0, prev[0]), jnp.where(lane == 0, prev[0], prev[1]))
            right = (jnp.where(lane == 127, foll[1], foll[0]), jnp.where(lane == 127, 0.0, foll[1]))
            for h in range(2):
                ahead = cc[a + 1, h, wide]
                yl = cc[a, h, 11:83]
                yr = cc[a, h, 13:85]
                wx[a, h, wide] = 0.5 * (mid[h] + ahead)
                wl[a, h, wide] = 0.5 * (mid[h] + yl)
                wr[a, h, wide] = 0.5 * (mid[h] + yr)
                low_edge = 0.5 * (mid[h] + left[h])
                high_edge = 0.5 * (mid[h] + right[h])
                zl[a, h, wide] = jnp.where(lane == 0, 0.0, low_edge) if h == 0 else low_edge
                zr[a, h, wide] = jnp.where(lane == 127, 0.0, high_edge) if h == 1 else high_edge
                diag = 0.5 * (6.0 * mid[h] + (cc[a - 1, h, wide] + ahead) + (yl + yr) + (left[h] + right[h]))
                di[a, h, wide] = diag
                jj[a, h, wide] = jnp.where(mid[h] > 0.0, 1.0 / diag, 0.0)

    def fine_setups(low, count):
        wx[low - 1, :, wide] = 0.5 * (cc[low - 1, :, wide] + cc[low, :, wide])
        spread(low, count, 3, fine_setup)

    fine_setups(6 - 5 * k, 11)
    moves_v[1]()
    moves_g[1]()

    def fine_sum(src, low, n, r0, r1):
        for r in range(r0, r1, 24 if (r1 - r0) % 24 == 0 else 32):
            e = r + (24 if (r1 - r0) % 24 == 0 else 32)
            w = slice(r, e)
            spot = lanes((e - r, 128))
            v = [[src[low + u, h, w] for h in range(2)] for u in range(-1, n + 1)]
            x = [[wx[low + u, h, w] for h in range(2)] for u in range(-1, n)]
            for u in range(n):
                a = low + u
                mid = v[u + 1]
                prev = [pltpu.roll(m, 1, 1) for m in mid]
                foll = [pltpu.roll(m, 127, 1) for m in mid]
                left = (prev[0], jnp.where(spot == 0, prev[0], prev[1]))
                right = (jnp.where(spot == 127, foll[1], foll[0]), foll[1])
                for h in range(2):
                    total = gg[a, h, w] + x[u][h] * v[u][h] + x[u + 1][h] * v[u + 2][h]
                    total = total + wl[a, h, w] * src[a, h, r - 1:e - 1] + wr[a, h, w] * src[a, h, r + 1:e + 1]
                    total = total + zl[a, h, w] * left[h] + zr[a, h, w] * right[h]
                    yield u, a, h, w, mid[h], total

    def fine_sweep(src, dst, step, low_plane, count, most=4):
        keep, new = FINE_STEPS[step]

        def run(low, n):
            for u, a, h, w, mid, total in fine_sum(src, low, n, 12, 84):
                move = new * (jj[a, h, w] * total - mid)
                if step > 0:
                    move = move + keep * dd[a, h, w]
                dd[a, h, w] = move
                dst[a, h, w] = mid + move

        spread(low_plane, count, most, run)

    rounds = ((va, vb), (vb, vc), (vc, vd), (vd, ve))
    for step, (src, dst) in enumerate(rounds):
        fine_sweep(src, dst, step, 6 + step - 5 * k, 11 - 2 * step)
    moves_c[2]()
    fine_setups(1 + 11 * k, 5)
    moves_v[2]()
    moves_g[2]()
    for moved in (moves_c, moves_v, moves_g):
        moved[3]()
    y_c1.arrive()
    h_c1.start()
    for step, (src, dst) in enumerate(rounds):
        fine_sweep(src, dst, step, 1 + step + (11 - 2 * step) * k, 5, 5)

    for m in range(4):
        for u, a, h, w, mid, total in fine_sum(ve, 5 + 2 * m, 2, 16, 80):
            part = total - di[a, h, w] * mid
            spot = slice(w.start - 16, w.stop - 16)
            tmp[m, h, spot] = part if u == 0 else tmp[m, h, spot] + part
        for t in range(4):
            s1[6 + m, 16 + 8 * t:24 + 8 * t] = pack((tmp.at[m, 0], tmp.at[m, 1]), t)

    m_s1.start()

    def keep_fine(a):
        pre[a, :, own] = ve[a, :, own]

    loop(5, 13, keep_fine)
    y_pre.start()
    y_c2.arrive()
    for a in (7, 8):
        pc2[a] = squeeze(c2, a, 8, 32, 2)
    h_c2.start()
    y_c3.arrive()
    pc3[p + 1] = squeeze(c3, p + 1, 12, 32, 4)
    h_c3.start()

    def setup(c, jn, dn, wxn, wln, wrn, zln, zrn, planes, rows, step, scale):
        low, high = planes
        r0, r1 = rows
        w = slice(r0, r1)
        spot = lanes((r1 - r0, 128))
        half = 0.5 * scale

        def run(first_plane, n):
            for a in [first_plane + u for u in range(n)]:
                mid = c[a, w]
                ahead = c[a + 1, w]
                left = jnp.where(spot < step, 0.0, pltpu.roll(mid, step, 1))
                right = jnp.where(spot >= 128 - step, 0.0, pltpu.roll(mid, 128 - step, 1))
                yl = c[a, r0 - 1:r1 - 1]
                yr = c[a, r0 + 1:r1 + 1]
                wxn[a, w] = half * (mid + ahead)
                wln[a, w] = half * (mid + yl)
                wrn[a, w] = half * (mid + yr)
                zln[a, w] = jnp.where(spot < step, 0.0, half * (mid + left))
                zrn[a, w] = jnp.where(spot >= 128 - step, 0.0, half * (mid + right))
                diag = half * (6.0 * mid + (c[a - 1, w] + ahead) + (yl + yr) + (left + right))
                dn[a, w] = diag
                jn[a, w] = jnp.where(mid > 0.0, 1.0 / diag, 0.0)

        wxn[low - 1, w] = half * (c[low - 1, w] + c[low, w])
        spread(low, high - low, 7 if high - low == 14 else 8, run)

    def gather_sum(src, low, n, g, wxn, wln, wrn, zln, zrn, rows, step):
        r0, r1 = rows
        w = slice(r0, r1)
        v = [src[low + u, w] for u in range(-1, n + 1)]
        x = [wxn[low + u, w] for u in range(-1, n)]
        for u in range(n):
            a = low + u
            mid = v[u + 1]
            total = g[a, w] + x[u] * v[u] + x[u + 1] * v[u + 2]
            total = total + wln[a, w] * src[a, r0 - 1:r1 - 1] + wrn[a, w] * src[a, r0 + 1:r1 + 1]
            total = total + zln[a, w] * pltpu.roll(mid, step, 1) + zrn[a, w] * pltpu.roll(mid, 128 - step, 1)
            yield a, mid, total

    def sweep(src, dst, d, jn, ws, planes, rows, step, pair):
        keep, new = pair
        w = slice(*rows)

        def run(low, n):
            for a, mid, total in gather_sum(src, low, n, *ws, rows, step):
                move = new * (jn[a, w] * total - mid)
                if keep != 0.0:
                    move = move + keep * d[a, w]
                d[a, w] = move
                dst[a, w] = mid + move

        spread(planes[0], planes[1] - planes[0], 8, run)

    def first(dst, d, g, jn, planes, rows, new):
        w = slice(*rows)

        for a in range(*planes):
            move = new * (jn[a, w] * g[a, w])
            d[a, w] = move
            dst[a, w] = move

    ws1 = (s1, wx1, wl1, wr1, zl1, zr1)
    ws2 = (s2, wx2, wl2, wr2, zl2, zr2)
    ws3 = (s3, wx3, wl3, wr3, zl3, zr3)
    rows1, rows2, rows3 = (8, 56), (8, 40), (8, 48)

    h_c1.arrive()
    setup(c1, j1, i1, wx1, wl1, wr1, zl1, zr1, (1, 15), rows1, 1, 0.25)
    m_s1.arrive()
    y_pre.arrive()
    h_pre.start()
    first(va1, d1, s1, j1, (2, 14), rows1, FINE_STEPS[0][1])
    sweep(va1, vb1, d1, j1, ws1, (3, 13), rows1, 1, FINE_STEPS[1])
    sweep(vb1, va1, d1, j1, ws1, (4, 12), rows1, 1, FINE_STEPS[2])
    sweep(va1, vb1, d1, j1, ws1, (5, 11), rows1, 1, FINE_STEPS[3])

    def residual(src, low, ws, dn, rows, step):
        parts = [total - dn[a, slice(*rows)] * mid for a, mid, total in gather_sum(src, low, 2, *ws, rows, step)]
        return parts[0] + parts[1]

    for m in range(2):
        tmp[m, 0, 0:32] = residual(vb1, 6 + 2 * m, ws1, i1, (16, 48), 1)
    for m in range(2):
        for t in range(2):
            s2[7 + m, 16 + 8 * t:24 + 8 * t] = 0.125 * fold_lanes(fold_rows(tmp.at[m, 0], t), 1)
    m_s2.start()
    k1[6:10, 16:48] = vb1[6:10, 16:48]
    y_k1.start()
    h_s1.start()
    h_c2.arrive()
    others2 = tuple(range(7)) + tuple(range(9, 16))
    widen(pc2, c2, others2, 8, 32, 2)
    setup(c2, j2, i2, wx2, wl2, wr2, zl2, zr2, (1, 15), rows2, 2, 0.0625)

    m_s2.arrive()
    first(va2, d2, s2, j2, (3, 13), rows2, FINE_STEPS[0][1])
    sweep(va2, vb2, d2, j2, ws2, (4, 12), rows2, 2, FINE_STEPS[1])
    sweep(vb2, va2, d2, j2, ws2, (5, 11), rows2, 2, FINE_STEPS[2])
    sweep(va2, vb2, d2, j2, ws2, (6, 10), rows2, 2, FINE_STEPS[3])
    tmp[2, 0, 0:16] = residual(vb2, 7, ws2, i2, (16, 32), 2)
    s3[p + 1, 24:32] = 0.125 * fold_lanes(fold_rows(tmp.at[2, 0], 0), 2)
    y_s3.start()
    k2[7:9, 16:32] = vb2[7:9, 16:32]
    y_k2.start()
    y_k1.arrive()
    h_k1.start()
    y_s3.arrive()
    ps3[p + 1] = squeeze(s3, p + 1, 12, 32, 4)
    h_s3.start()
    y_k2.arrive()
    for a in (7, 8):
        pk2[a] = squeeze(k2, a, 8, 32, 2)
    h_k2.start()
    h_s2.start()
    h_c3.arrive()
    y_c3.drain()
    widen(pc3, c3, range(1, 17), 12, 32, 4)
    setup(c3, j3, i3, wx3, wl3, wr3, zl3, zr3, (1, 17), rows3, 4, 0.015625)

    h_s3.arrive()
    y_s3.drain()
    widen(ps3, s3, range(1, 17), 12, 32, 4)
    first(va3, d3, s3, j3, (1, 17), rows3, BOTTOM_STEPS[0][1])
    here, there = va3, vb3
    for at in range(1, BOTTOM):
        halo = BOTTOM + 3 - at
        rows = (12, 44) if halo > 8 else (16, 40)
        sweep(here, there, d3, j3, ws3, (1, 17), rows, 4, BOTTOM_STEPS[at])
        here, there = there, here

    h_k2.arrive()
    widen(pk2, k2, others2, 8, 32, 2)
    h_s2.arrive()

    def finish2(a):
        up = jnp.clip(p - 3 + (a + 1) // 2, 0, 17)
        for t in range(2):
            e = here[up, 20 + 8 * t:28 + 8 * t]
            for odd in range(2):
                at = pl.ds(8 + 16 * t + odd, 8, stride=2)
                va2[a, at] = k2[a, at] + e

    for a in range(16):
        finish2(a)
    sweep(va2, vb2, d2, j2, ws2, (1, 15), rows2, 2, FINE_STEPS[0])
    sweep(vb2, va2, d2, j2, ws2, (2, 14), rows2, 2, FINE_STEPS[1])
    sweep(va2, vb2, d2, j2, ws2, (3, 13), rows2, 2, FINE_STEPS[2])
    sweep(vb2, va2, d2, j2, ws2, (4, 12), rows2, 2, FINE_STEPS[3])

    h_k1.arrive()
    h_s1.arrive()

    def finish1(a):
        up = 4 + a // 2
        for t in range(3):
            e = va2[up, 12 + 8 * t:20 + 8 * t]
            for odd in range(2):
                at = pl.ds(8 + 16 * t + odd, 8, stride=2)
                va1[a, at] = k1[a, at] + e

    for a in range(16):
        finish1(a)
    sweep(va1, vb1, d1, j1, ws1, (1, 15), rows1, 1, FINE_STEPS[0])
    sweep(vb1, va1, d1, j1, ws1, (2, 14), rows1, 1, FINE_STEPS[1])
    sweep(va1, vb1, d1, j1, ws1, (3, 13), rows1, 1, FINE_STEPS[2])
    sweep(vb1, va1, d1, j1, ws1, (4, 12), rows1, 1, FINE_STEPS[3])

    h_pre.arrive()

    def finish0(m):
        for t in range(5):
            e = va1[4 + m, 14 + 8 * t:22 + 8 * t]
            to_lane = lanes((8, 128)) // 2
            for h in range(2):
                half = jnp.take_along_axis(e, to_lane + 64 * h, axis=1)
                for x in range(2):
                    a = 1 + 2 * m + x
                    for odd in range(2):
                        at = pl.ds(12 + 16 * t + odd, 8, stride=2)
                        va[a, h, at] = pre[a, h, at] + half

    loop(0, 8, finish0)
    fine_sweep(va, vb, 0, 2, 14)
    fine_sweep(vb, va, 1, 3, 12)
    fine_sweep(va, vb, 2, 4, 10)
    fine_sweep(vb, va, 3, 5, 8)
    give = pltpu.make_async_remote_copy(
        src_ref=va.at[pl.ds(5, 8), 1 - k, pl.ds(16, 64)],
        dst_ref=out.at[pl.ds(8 * k, 8)],
        send_sem=sem.at[out_send],
        recv_sem=sem.at[out_recv],
        device_id=(i, j, 1 - k),
        device_id_type=MESH,
    )
    give.start()
    out[pl.ds(8 * k, 8)] = va[5:13, k, own]
    give.wait_send()
    pltpu.make_async_remote_copy(
        src_ref=va.at[pl.ds(5, 8), k, pl.ds(16, 64)],
        dst_ref=out.at[pl.ds(8 * (1 - k), 8)],
        send_sem=sem.at[out_send],
        recv_sem=sem.at[out_recv],
        device_id=(i, j, 1 - k),
        device_id_type=MESH,
    ).wait_recv()

    for moved in (y_c1, y_c2, h_c1, h_c2, h_c3, m_s1, y_pre, h_pre, m_s2, y_k1, h_k1, h_s1, h_s2, h_s3, y_k2, h_k2):
        moved.drain()


def on_device(iterate, right_side, diffusion):
    def buf(*shape):
        return pltpu.VMEM(shape, F32)

    scratch = [buf(18, 2, 96, 128)] * 3 + [buf(4, 2, 64, 128)] + [buf(18, 2, 96, 128)] * 13
    scratch += [buf(16, 64, 128)] * 13
    scratch += [buf(16, 48, 128)] * 13 + [buf(16, 16, 128)] * 2
    scratch += [buf(18, 56, 128)] * 12 + [buf(18, 8, 128)] * 2
    dma = pltpu.SemaphoreType.DMA
    scratch += [dma((SEMS,)), dma((3,))]
    return pl.pallas_call(
        kernel,
        out_shape=pltpu.VMEM((16, 64, 128), F32),
        in_specs=[pl.BlockSpec(memory_space=pl.ANY)] * 3,
        out_specs=pl.BlockSpec(memory_space=pltpu.VMEM),
        scratch_shapes=scratch,
        compiler_params=pltpu.CompilerParams(
            collective_id=0, has_side_effects=True, vmem_limit_bytes=60 * 2**20
        ),
        cost_estimate=pl.CostEstimate(flops=10**8, bytes_accessed=2 * 10**6, transcendentals=0),
        name="vcycle",
    )(iterate, right_side, diffusion)


def solution(mesh):
    placed = (P("gx", "gy", "gz"), P("gx", "gy", "gz"), P("gx", "gy", "gz"))
    return jax.shard_map(
        on_device, mesh=mesh, in_specs=placed, out_specs=P("gx", "gy", "gz"), check_vma=False
    )
```

```python
import jax
import jax.numpy as jnp
from jax import lax
from jax.experimental import pallas as pl
from jax.experimental.pallas import tpu as pltpu
from jax.sharding import PartitionSpec as P

DEGREE = 4
BOTTOM = 8
SMOOTH_LOW = 0.25
SMOOTH_HIGH = 2.0
BOTTOM_LOW = 0.05

F32 = jnp.float32
MESH = pl.DeviceIdType.MESH
NP = 16
NJ = 8
FINE_SEND = 0
FINE_RECV = 111
SEMS = 111 + 33 + 6 + 27 + 8 + 4 + 24 + 6 + 4 + 15 + 2 + 8 + 1


def chebyshev_steps(sweeps, low_end, high_end):
    center = 0.5 * (high_end + low_end)
    radius = 0.5 * (high_end - low_end)
    sigma_ratio = center / radius
    rho_old = 1.0 / sigma_ratio
    steps_out = [(0.0, 1.0 / center)]
    for sweep_index in range(1, sweeps):
        rho_new = 1.0 / (2.0 * sigma_ratio - rho_old)
        steps_out.append((rho_new * rho_old, 2.0 * rho_new / radius))
        rho_old = rho_new
    return steps_out


FINE_STEPS = chebyshev_steps(DEGREE, SMOOTH_LOW, SMOOTH_HIGH)
BOTTOM_STEPS = chebyshev_steps(BOTTOM, BOTTOM_LOW, SMOOTH_HIGH)


def loop(low, high, body):
    def step(index, carry):
        body(index)
        return carry

    lax.fori_loop(low, high, step, 0)


def spread(low, count, most, body):
    runs = -(-count // most)
    each = -(-count // runs)
    full = count // each
    if full > 1:
        loop(0, full, lambda r: body(low + r * each, each))
    elif full == 1:
        body(low, each)
    if count % each:
        body(low + full * each, count % each)


def lanes(shape):
    return lax.broadcasted_iota(jnp.int32, shape, len(shape) - 1)


class Moves:
    def __init__(self, place, ref, sem, send, recv, dirs):
        self.place, self.ref, self.sem, self.dirs = place, ref, sem, dirs
        self.send, self.recv = send, recv

    def copy(self, at):
        p, j = self.place
        dp, dj, src, dst = self.dirs[at]
        to = p + dp
        return pltpu.make_async_remote_copy(
            src_ref=self.ref.at[src],
            dst_ref=self.ref.at[dst],
            send_sem=self.sem.at[self.send + at],
            recv_sem=self.sem.at[self.recv + at],
            device_id=(to // 2, j + dj, to % 2),
            device_id_type=MESH,
        )

    def each(self, sign, act):
        p, j = self.place
        for at, (dp, dj, src, dst) in enumerate(self.dirs):
            ok = None
            for value, count, shift in ((p, NP, sign * dp), (j, NJ, sign * dj)):
                if shift > 0:
                    good = value < count - shift
                elif shift < 0:
                    good = value >= -shift
                else:
                    continue
                ok = good if ok is None else jnp.logical_and(ok, good)

            @pl.when(ok)
            def _():
                act(self.copy(at))

    def start(self):
        self.each(1, lambda c: c.start())

    def arrive(self):
        self.each(-1, lambda c: c.wait_recv())

    def drain(self):
        self.each(1, lambda c: c.wait_send())


def block_dirs(planes, first, halo, row, rows, dps, djs, wide, mid=()):
    out = []
    for dj in djs:
        for dp in dps:
            if dp == 0 and dj == 0:
                continue
            if dp > 0:
                x0 = max(0, planes * dp - halo)
                count = planes - x0
            elif dp < 0:
                x0 = 0
                count = min(planes, planes + halo + planes * dp)
            else:
                x0, count = 0, planes
            if dj == 0:
                low, size = (row - 8, rows + 16) if wide else (row, rows)
                to = low
            elif dj > 0:
                low, size, to = row + rows - 8, 8, row - 8
            else:
                low, size, to = row, 8, row + rows
            a = first + x0
            src = (pl.ds(a, count),) + mid + (pl.ds(low, size),)
            dst = (pl.ds(a - planes * dp, count),) + mid + (pl.ds(to, size),)
            out.append((dp, dj, src, dst))
    return out


def line(ref, start):
    return ref[pl.ds(start, 8, stride=2)]


def kernel(
    iterate, right_side, diffusion, out,
    va, cc, gg, tmp, vb, vc, vd, ve,
    dd, jj, di, wx, wl, wr, zl, zr, pre,
    s1, c1, k1, va1, vb1, d1, j1, i1, wx1, wl1, wr1, zl1, zr1,
    s2, c2, k2, va2, vb2, d2, j2, i2, wx2, wl2, wr2, zl2, zr2, pc2, pk2,
    s3, c3, va3, vb3, d3, j3, i3, wx3, wl3, wr3, zl3, zr3, pc3, ps3,
    sem, self_sem,
):
    i = lax.axis_index("gx")
    j = lax.axis_index("gy")
    k = lax.axis_index("gz")
    p = 2 * i + k
    place = (p, j)

    barrier = pltpu.get_barrier_semaphore()

    def greet(to, tj):
        pl.semaphore_signal(
            barrier, inc=1, device_id=(to // 2, tj, to % 2), device_id_type=MESH
        )

    loop(1, NP, lambda q: greet((p + q) % NP, j))
    count = NP - 1
    for dj in (-1, 1, -2, 2):
        okj = jnp.logical_and(j + dj >= 0, j + dj < NJ)
        for dp in range(-2, 3):
            ok = jnp.logical_and(okj, jnp.logical_and(p + dp >= 0, p + dp < NP))
            count = count + ok.astype(jnp.int32)

            @pl.when(ok)
            def _():
                greet(p + dp, j + dj)

    pl.semaphore_wait(barrier, count)

    def fine_moves(at, src, dst, halo):
        n = 8 + halo

        def copy(slot_s, slot_r, x0, nx, a0, low, size, to, zh, dev):
            return pltpu.make_async_remote_copy(
                src_ref=src.at[pl.ds(x0, nx), pl.ds(low, size)],
                dst_ref=dst.at[pl.ds(a0, nx), zh, pl.ds(to, size)],
                send_sem=sem.at[FINE_SEND + 11 * at + slot_s],
                recv_sem=sem.at[FINE_RECV + 11 * at + slot_r],
                device_id=dev,
                device_id_type=MESH,
            )

        mine = pltpu.make_async_copy(
            src.at[pl.ds(k * (8 - halo), n)],
            dst.at[pl.ds(5 - halo * k, n), k, pl.ds(16, 64)],
            self_sem.at[at],
        )
        other = 1 - k
        corner = halo - 1
        ny = 8 + corner
        inner = [(None, copy(0, 0, other * (8 - halo), n, 5 - halo * other, 0, 64, 16, k, (i, j, other)))]
        sends = []
        rows = [(0, 0, 64, 16), (1, 56, 8, 8), (-1, 0, 8, 80)]
        for dj, low, size, to in rows:
            okj = jnp.logical_and(j + dj >= 0, j + dj < NJ)
            turn = {0: 0, 1: 1, -1: 2}[dj]
            up = jnp.logical_and(i < 7, okj)
            down = jnp.logical_and(i > 0, okj)
            slot = 1 + 2 * turn + k
            w = halo if dj == 0 else corner
            sends.append((up, copy(1 + 2 * turn, slot, 16 - w, w, 5 - w, low, size, to, k, (i + 1, j + dj, 0))))
            sends.append((down, copy(2 + 2 * turn, slot, 0, w, 13, low, size, to, k, (i - 1, j + dj, 1))))
            if dj != 0:
                for half in (0, 1):
                    inner.append(
                        (okj, copy(5 + 2 * turn + half, 5 + 2 * turn + k, half * (8 - corner), ny, 5 - corner * half, low, size, to, k, (i, j + dj, half)))
                    )

        def start(part):
            if part == 0:
                mine.start()
            for ok, c in (inner, sends)[part]:
                if ok is None:
                    c.start()
                else:
                    pl.when(ok)(c.start)

        def arrive_inner():
            mine.wait()
            copy(0, 0, 0, n, 5 - halo * k, 0, 64, 16, other, (i, j, other)).wait_recv()
            for dj, low, size, to in rows[1:]:
                turn = {1: 1, -1: 2}[dj]
                okj = jnp.logical_and(j - dj >= 0, j - dj < NJ)
                for half in (0, 1):
                    pl.when(okj)(copy(0, 5 + 2 * turn + half, 0, ny, 5 - corner * k, low, size, to, half, (i, j, other)).wait_recv)

        def arrive_outer():
            beside = jnp.logical_or(jnp.logical_and(k == 0, i > 0), jnp.logical_and(k == 1, i < 7))
            for dj, low, size, to in rows:
                turn = {0: 0, 1: 1, -1: 2}[dj]
                okj = jnp.logical_and(j - dj >= 0, j - dj < NJ)
                ok = jnp.logical_and(beside, okj)
                w = halo if dj == 0 else corner
                a0 = (5 - w) * (1 - k) + 13 * k
                for half in (0, 1):
                    pl.when(ok)(copy(0, 1 + 2 * turn + half, 0, w, a0, low, size, to, half, (i, j, other)).wait_recv)

        def drain():
            for ok, c in inner + sends:
                if ok is None:
                    c.wait_send()
                else:
                    pl.when(ok)(c.wait_send)

        return start, arrive_inner, arrive_outer, drain

    moves_c = fine_moves(0, diffusion, cc, 5)
    moves_v = fine_moves(1, iterate, va, 5)
    moves_g = fine_moves(2, right_side, gg, 4)
    for part in range(2):
        for moved in (moves_c, moves_v, moves_g):
            moved[0](part)

    def clear(ref, planes, low_planes, high_from, edges, own=None):
        def wipe(a):
            ref[a] = jnp.zeros(ref.shape[1:], F32)

        loop(0, low_planes, wipe)
        loop(high_from, planes, wipe)

        def wipe_rows(low, size):
            def one(a):
                if len(ref.shape) == 4:
                    ref[a, :, low:low + size] = jnp.zeros((2, size, 128), F32)
                else:
                    ref[a, low:low + size] = jnp.zeros((size, 128), F32)

            loop(*(own or (0, planes)), one)

        for test, low, size in edges:
            pl.when(test)(lambda low=low, size=size: wipe_rows(low, size))

    def outer(first, planes, per, total):
        low = jnp.clip(first - per * p, 0, planes)
        high = jnp.clip(total - per * p + first, 0, planes)
        return low, high

    low, high = outer(5, 18, 8, 128)
    for ref in (va, cc, gg):
        clear(ref, 18, low, high, [(j == 0, 8, 8), (j == 7, 80, 8)])
    clear(pre, 18, low, high, [(j == 0, 8, 8), (j == 7, 80, 8)], (5, 13))
    low, high = outer(6, 16, 4, 64)
    for ref, owned in ((s1, None), (c1, (6, 10)), (k1, (6, 10))):
        clear(ref, 16, low, high, [(j == 0, 8, 8), (j == 7, 48, 8)], owned)
    low, high = outer(7, 16, 2, 32)
    for ref, owned in ((s2, None), (c2, (7, 9))):
        clear(ref, 16, low, high, [(j == 0, 8, 32), (j == 1, 8, 16), (j == 6, 72, 16), (j == 7, 56, 32)], owned)
    clear(k2, 16, low, high, [(j == 0, 32, 8), (j == 7, 56, 8)], (7, 9))
    for ref in (pc2, pk2):
        clear(ref, 16, low, high, [])
    for ref in (c3, va3, vb3):
        clear(ref, 18, 1, 17, [])

    def fold_rows(ref, at):
        return line(ref, 16 * at) + line(ref, 16 * at + 1)

    def fold_lanes(value, step):
        even = (lanes(value.shape) // step) % 2 == 0
        return value + jnp.where(even, pltpu.roll(value, 128 - step, 1), pltpu.roll(value, step, 1))

    def pack(halves, at):
        low, high = (fold_lanes(fold_rows(half, at), 1) for half in halves)
        from_lane = (2 * lanes((8, 128))) % 128
        low = jnp.take_along_axis(low, from_lane, axis=1)
        high = jnp.take_along_axis(high, from_lane, axis=1)
        return 0.125 * jnp.where(lanes((8, 128)) < 64, low, high)

    def squeeze(ref, a, row, rows, parts):
        size = rows // parts
        spot = lanes((size, 128)) % parts
        res = ref[a, row:row + size]
        for q in range(1, parts):
            res = jnp.where(spot == q, ref[a, row + q * size:row + (q + 1) * size], res)
        return res

    def widen(src, dst, planes, row, rows, parts):
        size = rows // parts
        spot = lanes((8, 128))
        spot = spot - spot % parts
        for a in planes:
            for r in range(0, size, 8):
                value = src[a, r:r + 8]
                for q in range(parts):
                    at = row + q * size + r
                    dst[a, at:at + 8] = jnp.take_along_axis(value, spot + q, axis=1)

    own = slice(16, 80)
    moves_c[1]()

    def coarsen_c(m):
        a = 5 + 2 * m
        for h in range(2):
            tmp[m, h] = cc[a, h, own] + cc[a + 1, h, own]
        for t in range(4):
            c1[6 + m, 16 + 8 * t:24 + 8 * t] = pack((tmp.at[m, 0], tmp.at[m, 1]), t)

    for m in range(4):
        coarsen_c(m)
    for m in range(2):
        tmp[m, 0, 0:32] = c1[6 + 2 * m, 16:48] + c1[7 + 2 * m, 16:48]
        for t in range(2):
            c2[7 + m, 40 + 8 * t:48 + 8 * t] = 0.125 * fold_lanes(fold_rows(tmp.at[m, 0], t), 1)

    used = {"recv": FINE_RECV + 33, "send": 0}

    def moves(ref, send, dirs):
        recv = used["recv"]
        used["recv"] = recv + len(dirs)
        return Moves(place, ref, sem, send, recv, dirs)

    def y_moves(send, ref, planes, first, row, rows, mid=()):
        return moves(ref, send, block_dirs(planes, first, 0, row, rows, (0,), (-1, 1), False, mid))

    def h_moves(send, ref, planes, first, halo, row, rows, dps, mid=()):
        return moves(ref, send, block_dirs(planes, first, halo, row, rows, dps, (0,), True, mid))

    def column_moves(send, ref, dps, djs):
        dirs = []
        for dp, dj, src, dst in block_dirs(2, 7, 4, 40, 16, dps, (0,), False):
            dirs.append((dp, 0, src, dst))
        for dj in djs:
            for dp in (0,) + tuple(dps):
                row = pl.ds(40 - 16 * dj, 16)
                dirs.append((dp, dj, (pl.ds(7, 2), pl.ds(40, 16)), (pl.ds(7 - 2 * dp, 2), row)))
        return moves(ref, send, dirs)

    class Around:
        def __init__(self, send, ref):
            self.send, self.ref, self.recv = send, ref, used["recv"]
            used["recv"] += NP - 1

        def copy(self, q, plane):
            to = (p + q) % NP
            return pltpu.make_async_remote_copy(
                src_ref=self.ref.at[plane],
                dst_ref=self.ref.at[plane],
                send_sem=sem.at[self.send + q - 1],
                recv_sem=sem.at[self.recv + q - 1],
                device_id=(to // 2, j, to % 2),
                device_id_type=MESH,
            )

        def start(self):
            loop(1, NP, lambda q: self.copy(q, p + 1).start())

        def arrive(self):
            loop(1, NP, lambda q: self.copy(q, (p - q + NP) % NP + 1).wait_recv())

        def drain(self):
            loop(1, NP, lambda q: self.copy(q, p + 1).wait_send())

    y_c1 = y_moves(33, c1, 4, 6, 16, 32)
    y_c2 = column_moves(35, c2, (), (-2, -1, 1, 2))
    h_c1 = h_moves(0, c1, 4, 6, 6, 16, 32, (-2, -1, 1, 2))
    h_c2 = h_moves(4, pc2, 2, 7, 7, 8, 24, (-4, -3, -2, -1, 1, 2, 3, 4))
    h_c3 = Around(12, pc3)
    m_s1 = moves(s1, 39, block_dirs(4, 6, 4, 16, 32, (-1, 0, 1), (0, -1, 1), False))
    y_pre = y_moves(47, pre, 8, 5, 16, 64, (slice(None),))
    h_pre = h_moves(49, pre, 8, 5, 4, 16, 64, (-1, 1), (slice(None),))
    m_s2 = column_moves(51, s2, (-2, -1, 1, 2), (-2, -1, 1, 2))
    y_k1 = y_moves(75, k1, 4, 6, 16, 32)
    h_k1 = h_moves(77, k1, 4, 6, 6, 16, 32, (-2, -1, 1, 2))
    h_s1 = h_moves(81, s1, 4, 6, 5, 16, 32, (-2, 2))
    h_s2 = h_moves(83, s2, 2, 7, 6, 40, 16, (-3, 3))
    h_s3 = Around(85, ps3)
    y_k2 = y_moves(100, k2, 2, 7, 40, 16)
    h_k2 = h_moves(102, pk2, 2, 7, 7, 8, 0, (-4, -3, -2, -1, 1, 2, 3, 4))
    out_send, out_recv = 110, used["recv"]
    assert out_recv < SEMS, out_recv

    y_c1.start()
    y_c2.start()

    wide = slice(12, 84)
    lane = lanes((72, 128))

    def fine_setup(low, n):
        for a in [low + u for u in range(n)]:
            mid = [cc[a, h, wide] for h in range(2)]
            prev = [pltpu.roll(m, 1, 1) for m in mid]
            foll = [pltpu.roll(m, 127, 1) for m in mid]
            left = (jnp.where(lane == 0, 0.0, prev[0]), jnp.where(lane == 0, prev[0], prev[1]))
            right = (jnp.where(lane == 127, foll[1], foll[0]), jnp.where(lane == 127, 0.0, foll[1]))
            for h in range(2):
                ahead = cc[a + 1, h, wide]
                yl = cc[a, h, 11:83]
                yr = cc[a, h, 13:85]
                wx[a, h, wide] = 0.5 * (mid[h] + ahead)
                wl[a, h, wide] = 0.5 * (mid[h] + yl)
                wr[a, h, wide] = 0.5 * (mid[h] + yr)
                low_edge = 0.5 * (mid[h] + left[h])
                high_edge = 0.5 * (mid[h] + right[h])
                zl[a, h, wide] = jnp.where(lane == 0, 0.0, low_edge) if h == 0 else low_edge
                zr[a, h, wide] = jnp.where(lane == 127, 0.0, high_edge) if h == 1 else high_edge
                diag = 0.5 * (6.0 * mid[h] + (cc[a - 1, h, wide] + ahead) + (yl + yr) + (left[h] + right[h]))
                di[a, h, wide] = diag
                jj[a, h, wide] = jnp.where(mid[h] > 0.0, 1.0 / diag, 0.0)

    def fine_setups(low, count):
        wx[low - 1, :, wide] = 0.5 * (cc[low - 1, :, wide] + cc[low, :, wide])
        spread(low, count, 3, fine_setup)

    fine_setups(6 - 5 * k, 11)
    moves_v[1]()
    moves_g[1]()

    def fine_sum(src, low, n, r0, r1):
        for r in range(r0, r1, 24 if (r1 - r0) % 24 == 0 else 32):
            e = r + (24 if (r1 - r0) % 24 == 0 else 32)
            w = slice(r, e)
            spot = lanes((e - r, 128))
            v = [[src[low + u, h, w] for h in range(2)] for u in range(-1, n + 1)]
            x = [[wx[low + u, h, w] for h in range(2)] for u in range(-1, n)]
            for u in range(n):
                a = low + u
                mid = v[u + 1]
                prev = [pltpu.roll(m, 1, 1) for m in mid]
                foll = [pltpu.roll(m, 127, 1) for m in mid]
                left = (prev[0], jnp.where(spot == 0, prev[0], prev[1]))
                right = (jnp.where(spot == 127, foll[1], foll[0]), foll[1])
                for h in range(2):
                    total = gg[a, h, w] + x[u][h] * v[u][h] + x[u + 1][h] * v[u + 2][h]
                    total = total + wl[a, h, w] * src[a, h, r - 1:e - 1] + wr[a, h, w] * src[a, h, r + 1:e + 1]
                    total = total + zl[a, h, w] * left[h] + zr[a, h, w] * right[h]
                    yield u, a, h, w, mid[h], total

    def fine_sweep(src, dst, step, low_plane, count, most=4):
        keep, new = FINE_STEPS[step]

        def run(low, n):
            for u, a, h, w, mid, total in fine_sum(src, low, n, 12, 84):
                move = new * (jj[a, h, w] * total - mid)
                if step > 0:
                    move = move + keep * dd[a, h, w]
                dd[a, h, w] = move
                dst[a, h, w] = mid + move

        spread(low_plane, count, most, run)

    rounds = ((va, vb), (vb, vc), (vc, vd), (vd, ve))
    for step, (src, dst) in enumerate(rounds):
        fine_sweep(src, dst, step, 6 + step - 5 * k, 11 - 2 * step)
    moves_c[2]()
    fine_setups(1 + 11 * k, 5)
    moves_v[2]()
    moves_g[2]()
    for moved in (moves_c, moves_v, moves_g):
        moved[3]()
    y_c1.arrive()
    h_c1.start()
    for step, (src, dst) in enumerate(rounds):
        fine_sweep(src, dst, step, 1 + step + (11 - 2 * step) * k, 5, 5)

    for m in range(4):
        for u, a, h, w, mid, total in fine_sum(ve, 5 + 2 * m, 2, 16, 80):
            part = total - di[a, h, w] * mid
            spot = slice(w.start - 16, w.stop - 16)
            tmp[m, h, spot] = part if u == 0 else tmp[m, h, spot] + part
        for t in range(4):
            s1[6 + m, 16 + 8 * t:24 + 8 * t] = pack((tmp.at[m, 0], tmp.at[m, 1]), t)

    m_s1.start()

    def keep_fine(a):
        pre[a, :, own] = ve[a, :, own]

    loop(5, 13, keep_fine)
    y_pre.start()
    y_c2.arrive()
    for a in (7, 8):
        pc2[a] = squeeze(c2, a, 8, 80, 2)
    h_c2.start()
    tmp[2, 0] = c2[7, 16:80] + c2[8, 16:80]
    for t in range(4):
        c3[p + 1, 12 + 8 * t:20 + 8 * t] = 0.125 * fold_lanes(fold_rows(tmp.at[2, 0], t), 2)
    pc3[p + 1] = squeeze(c3, p + 1, 12, 32, 4)
    h_c3.start()

    def setup(c, jn, dn, wxn, wln, wrn, zln, zrn, planes, rows, step, scale):
        low, high = planes
        r0, r1 = rows
        w = slice(r0, r1)
        spot = lanes((r1 - r0, 128))
        half = 0.5 * scale

        def run(first_plane, n):
            for a in [first_plane + u for u in range(n)]:
                mid = c[a, w]
                ahead = c[a + 1, w]
                left = jnp.where(spot < step, 0.0, pltpu.roll(mid, step, 1))
                right = jnp.where(spot >= 128 - step, 0.0, pltpu.roll(mid, 128 - step, 1))
                yl = c[a, r0 - 1:r1 - 1]
                yr = c[a, r0 + 1:r1 + 1]
                wxn[a, w] = half * (mid + ahead)
                wln[a, w] = half * (mid + yl)
                wrn[a, w] = half * (mid + yr)
                zln[a, w] = jnp.where(spot < step, 0.0, half * (mid + left))
                zrn[a, w] = jnp.where(spot >= 128 - step, 0.0, half * (mid + right))
                diag = half * (6.0 * mid + (c[a - 1, w] + ahead) + (yl + yr) + (left + right))
                dn[a, w] = diag
                jn[a, w] = jnp.where(mid > 0.0, 1.0 / diag, 0.0)

        wxn[low - 1, w] = half * (c[low - 1, w] + c[low, w])
        spread(low, high - low, 7 if high - low == 14 else 8, run)

    def gather_sum(src, low, n, g, wxn, wln, wrn, zln, zrn, rows, step):
        r0, r1 = rows
        w = slice(r0, r1)
        v = [src[low + u, w] for u in range(-1, n + 1)]
        x = [wxn[low + u, w] for u in range(-1, n)]
        for u in range(n):
            a = low + u
            mid = v[u + 1]
            total = g[a, w] + x[u] * v[u] + x[u + 1] * v[u + 2]
            total = total + wln[a, w] * src[a, r0 - 1:r1 - 1] + wrn[a, w] * src[a, r0 + 1:r1 + 1]
            total = total + zln[a, w] * pltpu.roll(mid, step, 1) + zrn[a, w] * pltpu.roll(mid, 128 - step, 1)
            yield a, mid, total

    def sweep(src, dst, d, jn, ws, planes, rows, step, pair):
        keep, new = pair
        w = slice(*rows)

        def run(low, n):
            for a, mid, total in gather_sum(src, low, n, *ws, rows, step):
                move = new * (jn[a, w] * total - mid)
                if keep != 0.0:
                    move = move + keep * d[a, w]
                d[a, w] = move
                dst[a, w] = mid + move

        spread(planes[0], planes[1] - planes[0], 8, run)

    def first(dst, d, g, jn, planes, rows, new):
        w = slice(*rows)

        for a in range(*planes):
            move = new * (jn[a, w] * g[a, w])
            d[a, w] = move
            dst[a, w] = move

    ws1 = (s1, wx1, wl1, wr1, zl1, zr1)
    ws2 = (s2, wx2, wl2, wr2, zl2, zr2)
    ws3 = (s3, wx3, wl3, wr3, zl3, zr3)
    rows1, wide2, rows2, rows3 = (8, 56), (8, 88), (32, 64), (8, 48)

    h_c1.arrive()
    setup(c1, j1, i1, wx1, wl1, wr1, zl1, zr1, (1, 15), rows1, 1, 0.25)
    m_s1.arrive()
    first(va1, d1, s1, j1, (2, 14), rows1, FINE_STEPS[0][1])
    sweep(va1, vb1, d1, j1, ws1, (3, 13), rows1, 1, FINE_STEPS[1])
    sweep(vb1, va1, d1, j1, ws1, (4, 12), rows1, 1, FINE_STEPS[2])
    sweep(va1, vb1, d1, j1, ws1, (5, 11), rows1, 1, FINE_STEPS[3])

    def residual(src, low, ws, dn, rows, step):
        parts = [total - dn[a, slice(*rows)] * mid for a, mid, total in gather_sum(src, low, 2, *ws, rows, step)]
        return parts[0] + parts[1]

    for m in range(2):
        tmp[m, 0, 0:32] = residual(vb1, 6 + 2 * m, ws1, i1, (16, 48), 1)
    for m in range(2):
        for t in range(2):
            s2[7 + m, 40 + 8 * t:48 + 8 * t] = 0.125 * fold_lanes(fold_rows(tmp.at[m, 0], t), 1)
    m_s2.start()
    k1[6:10, 16:48] = vb1[6:10, 16:48]
    y_k1.start()
    h_s1.start()
    y_pre.arrive()
    h_pre.start()
    h_c2.arrive()
    others2 = tuple(range(7)) + tuple(range(9, 16))
    widen(pc2, c2, others2, 8, 80, 2)
    setup(c2, j2, i2, wx2, wl2, wr2, zl2, zr2, (1, 15), wide2, 2, 0.0625)
    for moved in (y_c1, y_c2, h_c1, h_c2, m_s1, y_pre):
        moved.drain()

    m_s2.arrive()
    first(va2, d2, s2, j2, (3, 13), wide2, FINE_STEPS[0][1])
    sweep(va2, vb2, d2, j2, ws2, (4, 12), wide2, 2, FINE_STEPS[1])
    sweep(vb2, va2, d2, j2, ws2, (5, 11), wide2, 2, FINE_STEPS[2])
    sweep(va2, vb2, d2, j2, ws2, (6, 10), wide2, 2, FINE_STEPS[3])
    tmp[2, 0] = residual(vb2, 7, ws2, i2, (16, 80), 2)
    for t in range(4):
        s3[p + 1, 12 + 8 * t:20 + 8 * t] = 0.125 * fold_lanes(fold_rows(tmp.at[2, 0], t), 2)
    ps3[p + 1] = squeeze(s3, p + 1, 12, 32, 4)
    h_s3.start()
    k2[7:9, 40:56] = vb2[7:9, 40:56]
    y_k2.start()
    y_k1.arrive()
    h_k1.start()
    h_s2.start()
    h_c3.arrive()
    widen(pc3, c3, range(1, 17), 12, 32, 4)
    setup(c3, j3, i3, wx3, wl3, wr3, zl3, zr3, (1, 17), rows3, 4, 0.015625)
    y_k2.arrive()
    for a in (7, 8):
        pk2[a] = squeeze(k2, a, 32, 32, 2)
    h_k2.start()
    for moved in (h_c3, h_pre, m_s2, y_k1, h_s1, y_k2):
        moved.drain()

    h_s3.arrive()
    widen(ps3, s3, range(1, 17), 12, 32, 4)
    first(va3, d3, s3, j3, (1, 17), rows3, BOTTOM_STEPS[0][1])
    here, there = va3, vb3
    for at in range(1, BOTTOM):
        halo = BOTTOM + 3 - at
        rows = (12, 44) if halo > 8 else (16, 40)
        sweep(here, there, d3, j3, ws3, (1, 17), rows, 4, BOTTOM_STEPS[at])
        here, there = there, here

    h_k2.arrive()
    widen(pk2, k2, others2, 32, 32, 2)
    h_s2.arrive()

    def finish2(a):
        up = jnp.clip(p - 3 + (a + 1) // 2, 0, 17)
        for t in range(2):
            e = here[up, 20 + 8 * t:28 + 8 * t]
            for odd in range(2):
                at = pl.ds(32 + 16 * t + odd, 8, stride=2)
                va2[a, at] = k2[a, at] + e

    for a in range(16):
        finish2(a)
    sweep(va2, vb2, d2, j2, ws2, (1, 15), rows2, 2, FINE_STEPS[0])
    sweep(vb2, va2, d2, j2, ws2, (2, 14), rows2, 2, FINE_STEPS[1])
    sweep(va2, vb2, d2, j2, ws2, (3, 13), rows2, 2, FINE_STEPS[2])
    sweep(vb2, va2, d2, j2, ws2, (4, 12), rows2, 2, FINE_STEPS[3])

    h_k1.arrive()
    h_s1.arrive()

    def finish1(a):
        up = 4 + a // 2
        for t in range(3):
            e = va2[up, 36 + 8 * t:44 + 8 * t]
            for odd in range(2):
                at = pl.ds(8 + 16 * t + odd, 8, stride=2)
                va1[a, at] = k1[a, at] + e

    for a in range(16):
        finish1(a)
    sweep(va1, vb1, d1, j1, ws1, (1, 15), rows1, 1, FINE_STEPS[0])
    sweep(vb1, va1, d1, j1, ws1, (2, 14), rows1, 1, FINE_STEPS[1])
    sweep(va1, vb1, d1, j1, ws1, (3, 13), rows1, 1, FINE_STEPS[2])
    sweep(vb1, va1, d1, j1, ws1, (4, 12), rows1, 1, FINE_STEPS[3])

    h_pre.arrive()
    for moved in (h_k1, h_s2, h_s3, h_k2):
        moved.drain()

    def finish0(m):
        for t in range(5):
            e = va1[4 + m, 14 + 8 * t:22 + 8 * t]
            to_lane = lanes((8, 128)) // 2
            for h in range(2):
                half = jnp.take_along_axis(e, to_lane + 64 * h, axis=1)
                for x in range(2):
                    a = 1 + 2 * m + x
                    for odd in range(2):
                        at = pl.ds(12 + 16 * t + odd, 8, stride=2)
                        va[a, h, at] = pre[a, h, at] + half

    loop(0, 8, finish0)
    fine_sweep(va, vb, 0, 2, 14)
    fine_sweep(vb, va, 1, 3, 12)
    fine_sweep(va, vb, 2, 4, 10)
    fine_sweep(vb, va, 3, 5, 8)
    give = pltpu.make_async_remote_copy(
        src_ref=va.at[pl.ds(5, 8), 1 - k, pl.ds(16, 64)],
        dst_ref=out.at[pl.ds(8 * k, 8)],
        send_sem=sem.at[out_send],
        recv_sem=sem.at[out_recv],
        device_id=(i, j, 1 - k),
        device_id_type=MESH,
    )
    give.start()
    out[pl.ds(8 * k, 8)] = va[5:13, k, own]
    give.wait_send()
    pltpu.make_async_remote_copy(
        src_ref=va.at[pl.ds(5, 8), k, pl.ds(16, 64)],
        dst_ref=out.at[pl.ds(8 * (1 - k), 8)],
        send_sem=sem.at[out_send],
        recv_sem=sem.at[out_recv],
        device_id=(i, j, 1 - k),
        device_id_type=MESH,
    ).wait_recv()


def on_device(iterate, right_side, diffusion):
    def buf(*shape):
        return pltpu.VMEM(shape, F32)

    scratch = [buf(18, 2, 96, 128)] * 3 + [buf(4, 2, 64, 128)] + [buf(18, 2, 96, 128)] * 13
    scratch += [buf(16, 64, 128)] * 13
    scratch += [buf(16, 96, 128)] * 13 + [buf(16, 40, 128), buf(16, 16, 128)]
    scratch += [buf(18, 56, 128)] * 12 + [buf(18, 8, 128)] * 2
    dma = pltpu.SemaphoreType.DMA
    scratch += [dma((SEMS,)), dma((3,))]
    return pl.pallas_call(
        kernel,
        out_shape=pltpu.VMEM((16, 64, 128), F32),
        in_specs=[pl.BlockSpec(memory_space=pl.ANY)] * 3,
        out_specs=pl.BlockSpec(memory_space=pltpu.VMEM),
        scratch_shapes=scratch,
        compiler_params=pltpu.CompilerParams(
            collective_id=0, has_side_effects=True, vmem_limit_bytes=60 * 2**20
        ),
        cost_estimate=pl.CostEstimate(flops=10**8, bytes_accessed=2 * 10**6, transcendentals=0),
        name="vcycle",
    )(iterate, right_side, diffusion)


def solution(mesh):
    placed = (P("gx", "gy", "gz"), P("gx", "gy", "gz"), P("gx", "gy", "gz"))
    return jax.shard_map(
        on_device, mesh=mesh, in_specs=placed, out_specs=P("gx", "gy", "gz"), check_vma=False
    )
```

```python
import jax
import jax.numpy as jnp
from jax import lax
from jax.experimental import pallas as pl
from jax.experimental.pallas import tpu as pltpu
from jax.sharding import PartitionSpec as P

DEGREE = 4
BOTTOM = 8
SMOOTH_LOW = 0.25
SMOOTH_HIGH = 2.0
BOTTOM_LOW = 0.05

F32 = jnp.float32
MESH = pl.DeviceIdType.MESH
NP = 16
NJ = 8
FINE_SEND = 0
FINE_RECV = 95
SEMS = 95 + 33 + 6 + 13 + 8 + 4 + 24 + 6 + 4 + 1 + 8 + 1


def chebyshev_steps(sweeps, low_end, high_end):
    center = 0.5 * (high_end + low_end)
    radius = 0.5 * (high_end - low_end)
    sigma_ratio = center / radius
    rho_old = 1.0 / sigma_ratio
    steps_out = [(0.0, 1.0 / center)]
    for sweep_index in range(1, sweeps):
        rho_new = 1.0 / (2.0 * sigma_ratio - rho_old)
        steps_out.append((rho_new * rho_old, 2.0 * rho_new / radius))
        rho_old = rho_new
    return steps_out


FINE_STEPS = chebyshev_steps(DEGREE, SMOOTH_LOW, SMOOTH_HIGH)
BOTTOM_STEPS = chebyshev_steps(BOTTOM, BOTTOM_LOW, SMOOTH_HIGH)


def loop(low, high, body):
    def step(index, carry):
        body(index)
        return carry

    lax.fori_loop(low, high, step, 0)


def spread(low, count, most, body):
    runs = -(-count // most)
    each = -(-count // runs)
    full = count // each
    if full > 1:
        loop(0, full, lambda r: body(low + r * each, each))
    elif full == 1:
        body(low, each)
    if count % each:
        body(low + full * each, count % each)


def lanes(shape):
    return lax.broadcasted_iota(jnp.int32, shape, len(shape) - 1)


class Moves:
    def __init__(self, place, ref, sem, send, recv, dirs):
        self.place, self.ref, self.sem, self.dirs = place, ref, sem, dirs
        self.send, self.recv = send, recv

    def copy(self, at):
        p, j = self.place
        dp, dj, src, dst = self.dirs[at]
        to = p + dp
        return pltpu.make_async_remote_copy(
            src_ref=self.ref.at[src],
            dst_ref=self.ref.at[dst],
            send_sem=self.sem.at[self.send + at],
            recv_sem=self.sem.at[self.recv + at],
            device_id=(to // 2, j + dj, to % 2),
            device_id_type=MESH,
        )

    def each(self, sign, act):
        p, j = self.place
        for at, (dp, dj, src, dst) in enumerate(self.dirs):
            ok = None
            for value, count, shift in ((p, NP, sign * dp), (j, NJ, sign * dj)):
                if shift > 0:
                    good = value < count - shift
                elif shift < 0:
                    good = value >= -shift
                else:
                    continue
                ok = good if ok is None else jnp.logical_and(ok, good)

            @pl.when(ok)
            def _():
                act(self.copy(at))

    def start(self):
        self.each(1, lambda c: c.start())

    def arrive(self):
        self.each(-1, lambda c: c.wait_recv())

    def drain(self):
        self.each(1, lambda c: c.wait_send())


def block_dirs(planes, first, halo, row, rows, dps, djs, wide, mid=()):
    out = []
    for dj in djs:
        for dp in dps:
            if dp == 0 and dj == 0:
                continue
            if dp > 0:
                x0 = max(0, planes * dp - halo)
                count = planes - x0
            elif dp < 0:
                x0 = 0
                count = min(planes, planes + halo + planes * dp)
            else:
                x0, count = 0, planes
            if dj == 0:
                low, size = (row - 8, rows + 16) if wide else (row, rows)
                to = low
            elif dj > 0:
                low, size, to = row + rows - 8, 8, row - 8
            else:
                low, size, to = row, 8, row + rows
            a = first + x0
            src = (pl.ds(a, count),) + mid + (pl.ds(low, size),)
            dst = (pl.ds(a - planes * dp, count),) + mid + (pl.ds(to, size),)
            out.append((dp, dj, src, dst))
    return out


def line(ref, start):
    return ref[pl.ds(start, 8, stride=2)]


def kernel(
    iterate, right_side, diffusion, out,
    va, cc, gg, tmp, vb, vc, vd, ve,
    dd, jj, di, wx, wl, wr, zl, zr, pre,
    s1, c1, k1, va1, vb1, d1, j1, i1, wx1, wl1, wr1, zl1, zr1,
    s2, c2, k2, va2, vb2, d2, j2, i2, wx2, wl2, wr2, zl2, zr2, pc2, pk2,
    s3, c3, va3, vb3, d3, j3, i3, wx3, wl3, wr3, zl3, zr3, pc3, ps3,
    sem, self_sem,
):
    i = lax.axis_index("gx")
    j = lax.axis_index("gy")
    k = lax.axis_index("gz")
    p = 2 * i + k
    place = (p, j)

    barrier = pltpu.get_barrier_semaphore()

    def greet(to, tj):
        pl.semaphore_signal(
            barrier, inc=1, device_id=(to // 2, tj, to % 2), device_id_type=MESH
        )

    loop(1, NP, lambda q: greet((p + q) % NP, j))
    count = NP - 1
    for dj in (-1, 1, -2, 2):
        okj = jnp.logical_and(j + dj >= 0, j + dj < NJ)
        for dp in range(-2, 3):
            ok = jnp.logical_and(okj, jnp.logical_and(p + dp >= 0, p + dp < NP))
            count = count + ok.astype(jnp.int32)

            @pl.when(ok)
            def _():
                greet(p + dp, j + dj)

    pl.semaphore_wait(barrier, count)

    def fine_moves(at, src, dst, halo):
        n = 8 + halo

        def copy(slot_s, slot_r, x0, nx, a0, low, size, to, zh, dev):
            return pltpu.make_async_remote_copy(
                src_ref=src.at[pl.ds(x0, nx), pl.ds(low, size)],
                dst_ref=dst.at[pl.ds(a0, nx), zh, pl.ds(to, size)],
                send_sem=sem.at[FINE_SEND + 11 * at + slot_s],
                recv_sem=sem.at[FINE_RECV + 11 * at + slot_r],
                device_id=dev,
                device_id_type=MESH,
            )

        mine = pltpu.make_async_copy(
            src.at[pl.ds(k * (8 - halo), n)],
            dst.at[pl.ds(5 - halo * k, n), k, pl.ds(16, 64)],
            self_sem.at[at],
        )
        other = 1 - k
        corner = halo - 1
        ny = 8 + corner
        inner = [(None, copy(0, 0, other * (8 - halo), n, 5 - halo * other, 0, 64, 16, k, (i, j, other)))]
        sends = []
        rows = [(0, 0, 64, 16), (1, 56, 8, 8), (-1, 0, 8, 80)]
        for dj, low, size, to in rows:
            okj = jnp.logical_and(j + dj >= 0, j + dj < NJ)
            turn = {0: 0, 1: 1, -1: 2}[dj]
            up = jnp.logical_and(i < 7, okj)
            down = jnp.logical_and(i > 0, okj)
            slot = 1 + 2 * turn + k
            w = halo if dj == 0 else corner
            sends.append((up, copy(1 + 2 * turn, slot, 16 - w, w, 5 - w, low, size, to, k, (i + 1, j + dj, 0))))
            sends.append((down, copy(2 + 2 * turn, slot, 0, w, 13, low, size, to, k, (i - 1, j + dj, 1))))
            if dj != 0:
                for half in (0, 1):
                    inner.append(
                        (okj, copy(5 + 2 * turn + half, 5 + 2 * turn + k, half * (8 - corner), ny, 5 - corner * half, low, size, to, k, (i, j + dj, half)))
                    )

        def start(part):
            if part == 0:
                mine.start()
            for ok, c in (inner, sends)[part]:
                if ok is None:
                    c.start()
                else:
                    pl.when(ok)(c.start)

        def arrive_inner():
            mine.wait()
            copy(0, 0, 0, n, 5 - halo * k, 0, 64, 16, other, (i, j, other)).wait_recv()
            for dj, low, size, to in rows[1:]:
                turn = {1: 1, -1: 2}[dj]
                okj = jnp.logical_and(j - dj >= 0, j - dj < NJ)
                for half in (0, 1):
                    pl.when(okj)(copy(0, 5 + 2 * turn + half, 0, ny, 5 - corner * k, low, size, to, half, (i, j, other)).wait_recv)

        def arrive_outer():
            beside = jnp.logical_or(jnp.logical_and(k == 0, i > 0), jnp.logical_and(k == 1, i < 7))
            for dj, low, size, to in rows:
                turn = {0: 0, 1: 1, -1: 2}[dj]
                okj = jnp.logical_and(j - dj >= 0, j - dj < NJ)
                ok = jnp.logical_and(beside, okj)
                w = halo if dj == 0 else corner
                a0 = (5 - w) * (1 - k) + 13 * k
                for half in (0, 1):
                    pl.when(ok)(copy(0, 1 + 2 * turn + half, 0, w, a0, low, size, to, half, (i, j, other)).wait_recv)

        def drain():
            for ok, c in inner + sends:
                if ok is None:
                    c.wait_send()
                else:
                    pl.when(ok)(c.wait_send)

        return start, arrive_inner, arrive_outer, drain

    moves_c = fine_moves(0, diffusion, cc, 5)
    moves_v = fine_moves(1, iterate, va, 5)
    moves_g = fine_moves(2, right_side, gg, 4)
    for part in range(2):
        for moved in (moves_c, moves_v, moves_g):
            moved[0](part)

    def clear(ref, planes, low_planes, high_from, edges, own=None):
        def wipe(a):
            ref[a] = jnp.zeros(ref.shape[1:], F32)

        loop(0, low_planes, wipe)
        loop(high_from, planes, wipe)

        def wipe_rows(low, size):
            def one(a):
                if len(ref.shape) == 4:
                    ref[a, :, low:low + size] = jnp.zeros((2, size, 128), F32)
                else:
                    ref[a, low:low + size] = jnp.zeros((size, 128), F32)

            loop(*(own or (0, planes)), one)

        for test, low, size in edges:
            pl.when(test)(lambda low=low, size=size: wipe_rows(low, size))

    def outer(first, planes, per, total):
        low = jnp.clip(first - per * p, 0, planes)
        high = jnp.clip(total - per * p + first, 0, planes)
        return low, high

    low, high = outer(5, 18, 8, 128)
    for ref in (va, cc, gg):
        clear(ref, 18, low, high, [(j == 0, 8, 8), (j == 7, 80, 8)])
    clear(pre, 18, low, high, [(j == 0, 8, 8), (j == 7, 80, 8)], (5, 13))
    low, high = outer(6, 16, 4, 64)
    for ref, owned in ((s1, None), (c1, (6, 10)), (k1, (6, 10))):
        clear(ref, 16, low, high, [(j == 0, 8, 8), (j == 7, 48, 8)], owned)
    low, high = outer(7, 16, 2, 32)
    for ref, owned in ((s2, None), (c2, (7, 9))):
        clear(ref, 16, low, high, [(j == 0, 8, 32), (j == 1, 8, 16), (j == 6, 72, 16), (j == 7, 56, 32)], owned)
    for ref in (pc2, pk2):
        clear(ref, 16, low, high, [])
    for ref in (c3, va3, vb3):
        clear(ref, 18, 1, 17, [])

    def fold_rows(ref, at):
        return line(ref, 16 * at) + line(ref, 16 * at + 1)

    def fold_lanes(value, step):
        even = (lanes(value.shape) // step) % 2 == 0
        return value + jnp.where(even, pltpu.roll(value, 128 - step, 1), pltpu.roll(value, step, 1))

    def pack(halves, at):
        low, high = (fold_lanes(fold_rows(half, at), 1) for half in halves)
        from_lane = (2 * lanes((8, 128))) % 128
        low = jnp.take_along_axis(low, from_lane, axis=1)
        high = jnp.take_along_axis(high, from_lane, axis=1)
        return 0.125 * jnp.where(lanes((8, 128)) < 64, low, high)

    def squeeze(ref, a, row, rows, parts):
        size = rows // parts
        spot = lanes((size, 128)) % parts
        res = ref[a, row:row + size]
        for q in range(1, parts):
            res = jnp.where(spot == q, ref[a, row + q * size:row + (q + 1) * size], res)
        return res

    def widen(src, dst, planes, row, rows, parts):
        size = rows // parts
        spot = lanes((8, 128))
        spot = spot - spot % parts
        for a in planes:
            for r in range(0, size, 8):
                value = src[a, r:r + 8]
                for q in range(parts):
                    at = row + q * size + r
                    dst[a, at:at + 8] = jnp.take_along_axis(value, spot + q, axis=1)

    own = slice(16, 80)
    moves_c[1]()

    def coarsen_c(m):
        a = 5 + 2 * m
        for h in range(2):
            tmp[m, h] = cc[a, h, own] + cc[a + 1, h, own]
        for t in range(4):
            c1[6 + m, 16 + 8 * t:24 + 8 * t] = pack((tmp.at[m, 0], tmp.at[m, 1]), t)

    for m in range(4):
        coarsen_c(m)
    for m in range(2):
        tmp[m, 0, 0:32] = c1[6 + 2 * m, 16:48] + c1[7 + 2 * m, 16:48]
        for t in range(2):
            c2[7 + m, 40 + 8 * t:48 + 8 * t] = 0.125 * fold_lanes(fold_rows(tmp.at[m, 0], t), 1)

    used = {"recv": FINE_RECV + 33, "send": 0}

    def moves(ref, send, dirs):
        recv = used["recv"]
        used["recv"] = recv + len(dirs)
        return Moves(place, ref, sem, send, recv, dirs)

    def y_moves(send, ref, planes, first, row, rows, mid=()):
        return moves(ref, send, block_dirs(planes, first, 0, row, rows, (0,), (-1, 1), False, mid))

    def h_moves(send, ref, planes, first, halo, row, rows, dps, mid=()):
        return moves(ref, send, block_dirs(planes, first, halo, row, rows, dps, (0,), True, mid))

    def column_moves(send, ref, dps, djs):
        dirs = []
        for dp, dj, src, dst in block_dirs(2, 7, 4, 40, 16, dps, (0,), False):
            dirs.append((dp, 0, src, dst))
        for dj in djs:
            for dp in (0,) + tuple(dps):
                row = pl.ds(40 - 16 * dj, 16)
                dirs.append((dp, dj, (pl.ds(7, 2), pl.ds(40, 16)), (pl.ds(7 - 2 * dp, 2), row)))
        return moves(ref, send, dirs)

    class Around:
        def __init__(self, send, ref):
            self.send, self.ref, self.recv = send, ref, used["recv"]
            used["recv"] += 1

        def copy(self, q, src, dst):
            to = (p + q) % NP
            return pltpu.make_async_remote_copy(
                src_ref=self.ref.at[src],
                dst_ref=self.ref.at[dst],
                send_sem=sem.at[self.send],
                recv_sem=sem.at[self.recv],
                device_id=(to // 2, j, to % 2),
                device_id_type=MESH,
            )

        def start(self):
            loop(1, NP, lambda q: self.copy(q, p + 1, p + 1).start())

        def all(self):
            planes = pl.ds(1, NP - 1)
            return self.copy(1, planes, planes)

        def arrive(self):
            self.all().wait_recv()

        def drain(self):
            self.all().wait_send()

    y_c1 = y_moves(33, c1, 4, 6, 16, 32)
    y_c2 = column_moves(35, c2, (), (-2, -1, 1, 2))
    h_c1 = h_moves(0, c1, 4, 6, 6, 16, 32, (-2, -1, 1, 2))
    h_c2 = h_moves(4, pc2, 2, 7, 7, 8, 24, (-4, -3, -2, -1, 1, 2, 3, 4))
    h_c3 = Around(12, pc3)
    m_s1 = moves(s1, 39, block_dirs(4, 6, 4, 16, 32, (-1, 0, 1), (0, -1, 1), False))
    y_pre = y_moves(47, pre, 8, 5, 16, 64, (slice(None),))
    h_pre = h_moves(49, pre, 8, 5, 4, 16, 64, (-1, 1), (slice(None),))
    m_s2 = column_moves(51, s2, (-2, -1, 1, 2), (-2, -1, 1, 2))
    y_k1 = y_moves(75, k1, 4, 6, 16, 32)
    h_k1 = h_moves(77, k1, 4, 6, 6, 16, 32, (-2, -1, 1, 2))
    h_s1 = h_moves(81, s1, 4, 6, 5, 16, 32, (-2, 2))
    h_s2 = h_moves(83, s2, 2, 7, 6, 40, 16, (-3, 3))
    h_s3 = Around(85, ps3)
    h_k2 = h_moves(86, pk2, 2, 7, 7, 8, 0, (-4, -3, -2, -1, 1, 2, 3, 4))
    out_send, out_recv = 94, used["recv"]
    assert out_recv < SEMS, out_recv

    y_c1.start()
    y_c2.start()

    wide = slice(12, 84)
    lane = lanes((72, 128))

    def fine_setup(low, n):
        for a in [low + u for u in range(n)]:
            mid = [cc[a, h, wide] for h in range(2)]
            prev = [pltpu.roll(m, 1, 1) for m in mid]
            foll = [pltpu.roll(m, 127, 1) for m in mid]
            left = (jnp.where(lane == 0, 0.0, prev[0]), jnp.where(lane == 0, prev[0], prev[1]))
            right = (jnp.where(lane == 127, foll[1], foll[0]), jnp.where(lane == 127, 0.0, foll[1]))
            for h in range(2):
                ahead = cc[a + 1, h, wide]
                yl = cc[a, h, 11:83]
                yr = cc[a, h, 13:85]
                wx[a, h, wide] = 0.5 * (mid[h] + ahead)
                wl[a, h, wide] = 0.5 * (mid[h] + yl)
                wr[a, h, wide] = 0.5 * (mid[h] + yr)
                low_edge = 0.5 * (mid[h] + left[h])
                high_edge = 0.5 * (mid[h] + right[h])
                zl[a, h, wide] = jnp.where(lane == 0, 0.0, low_edge) if h == 0 else low_edge
                zr[a, h, wide] = jnp.where(lane == 127, 0.0, high_edge) if h == 1 else high_edge
                diag = 0.5 * (6.0 * mid[h] + (cc[a - 1, h, wide] + ahead) + (yl + yr) + (left[h] + right[h]))
                di[a, h, wide] = diag
                jj[a, h, wide] = jnp.where(mid[h] > 0.0, 1.0 / diag, 0.0)

    def fine_setups(low, count):
        wx[low - 1, :, wide] = 0.5 * (cc[low - 1, :, wide] + cc[low, :, wide])
        spread(low, count, 3, fine_setup)

    fine_setups(6 - 5 * k, 11)
    moves_v[1]()
    moves_g[1]()

    def fine_sum(src, low, n, r0, r1):
        for r in range(r0, r1, 24 if (r1 - r0) % 24 == 0 else 32):
            e = r + (24 if (r1 - r0) % 24 == 0 else 32)
            w = slice(r, e)
            spot = lanes((e - r, 128))
            v = [[src[low + u, h, w] for h in range(2)] for u in range(-1, n + 1)]
            x = [[wx[low + u, h, w] for h in range(2)] for u in range(-1, n)]
            for u in range(n):
                a = low + u
                mid = v[u + 1]
                prev = [pltpu.roll(m, 1, 1) for m in mid]
                foll = [pltpu.roll(m, 127, 1) for m in mid]
                left = (prev[0], jnp.where(spot == 0, prev[0], prev[1]))
                right = (jnp.where(spot == 127, foll[1], foll[0]), foll[1])
                for h in range(2):
                    total = gg[a, h, w] + x[u][h] * v[u][h] + x[u + 1][h] * v[u + 2][h]
                    total = total + wl[a, h, w] * src[a, h, r - 1:e - 1] + wr[a, h, w] * src[a, h, r + 1:e + 1]
                    total = total + zl[a, h, w] * left[h] + zr[a, h, w] * right[h]
                    yield u, a, h, w, mid[h], total

    def fine_sweep(src, dst, step, low_plane, count, most=4):
        keep, new = FINE_STEPS[step]

        def run(low, n):
            for u, a, h, w, mid, total in fine_sum(src, low, n, 12, 84):
                move = new * (jj[a, h, w] * total - mid)
                if step > 0:
                    move = move + keep * dd[a, h, w]
                dd[a, h, w] = move
                dst[a, h, w] = mid + move

        spread(low_plane, count, most, run)

    rounds = ((va, vb), (vb, vc), (vc, vd), (vd, ve))
    for step, (src, dst) in enumerate(rounds):
        fine_sweep(src, dst, step, 6 + step - 5 * k, 11 - 2 * step)
    moves_c[2]()
    fine_setups(1 + 11 * k, 5)
    moves_v[2]()
    moves_g[2]()
    for moved in (moves_c, moves_v, moves_g):
        moved[3]()
    y_c1.arrive()
    h_c1.start()
    for step, (src, dst) in enumerate(rounds):
        fine_sweep(src, dst, step, 1 + step + (11 - 2 * step) * k, 5, 5)

    for m in range(4):
        for u, a, h, w, mid, total in fine_sum(ve, 5 + 2 * m, 2, 16, 80):
            part = total - di[a, h, w] * mid
            spot = slice(w.start - 16, w.stop - 16)
            tmp[m, h, spot] = part if u == 0 else tmp[m, h, spot] + part
        for t in range(4):
            s1[6 + m, 16 + 8 * t:24 + 8 * t] = pack((tmp.at[m, 0], tmp.at[m, 1]), t)

    m_s1.start()

    def keep_fine(a):
        pre[a, :, own] = ve[a, :, own]

    loop(5, 13, keep_fine)
    y_pre.start()
    y_c2.arrive()
    for a in (7, 8):
        pc2[a] = squeeze(c2, a, 8, 80, 2)
    h_c2.start()
    tmp[2, 0] = c2[7, 16:80] + c2[8, 16:80]
    for t in range(4):
        c3[p + 1, 12 + 8 * t:20 + 8 * t] = 0.125 * fold_lanes(fold_rows(tmp.at[2, 0], t), 2)
    pc3[p + 1] = squeeze(c3, p + 1, 12, 32, 4)
    h_c3.start()

    def setup(c, jn, dn, wxn, wln, wrn, zln, zrn, planes, rows, step, scale):
        low, high = planes
        r0, r1 = rows
        w = slice(r0, r1)
        spot = lanes((r1 - r0, 128))
        half = 0.5 * scale

        def run(first_plane, n):
            for a in [first_plane + u for u in range(n)]:
                mid = c[a, w]
                ahead = c[a + 1, w]
                left = jnp.where(spot < step, 0.0, pltpu.roll(mid, step, 1))
                right = jnp.where(spot >= 128 - step, 0.0, pltpu.roll(mid, 128 - step, 1))
                yl = c[a, r0 - 1:r1 - 1]
                yr = c[a, r0 + 1:r1 + 1]
                wxn[a, w] = half * (mid + ahead)
                wln[a, w] = half * (mid + yl)
                wrn[a, w] = half * (mid + yr)
                zln[a, w] = jnp.where(spot < step, 0.0, half * (mid + left))
                zrn[a, w] = jnp.where(spot >= 128 - step, 0.0, half * (mid + right))
                diag = half * (6.0 * mid + (c[a - 1, w] + ahead) + (yl + yr) + (left + right))
                dn[a, w] = diag
                jn[a, w] = jnp.where(mid > 0.0, 1.0 / diag, 0.0)

        wxn[low - 1, w] = half * (c[low - 1, w] + c[low, w])
        spread(low, high - low, 7 if high - low == 14 else 8, run)

    def gather_sum(src, low, n, g, wxn, wln, wrn, zln, zrn, rows, step):
        r0, r1 = rows
        w = slice(r0, r1)
        v = [src[low + u, w] for u in range(-1, n + 1)]
        x = [wxn[low + u, w] for u in range(-1, n)]
        for u in range(n):
            a = low + u
            mid = v[u + 1]
            total = g[a, w] + x[u] * v[u] + x[u + 1] * v[u + 2]
            total = total + wln[a, w] * src[a, r0 - 1:r1 - 1] + wrn[a, w] * src[a, r0 + 1:r1 + 1]
            total = total + zln[a, w] * pltpu.roll(mid, step, 1) + zrn[a, w] * pltpu.roll(mid, 128 - step, 1)
            yield a, mid, total

    def sweep(src, dst, d, jn, ws, planes, rows, step, pair):
        keep, new = pair
        w = slice(*rows)

        def run(low, n):
            for a, mid, total in gather_sum(src, low, n, *ws, rows, step):
                move = new * (jn[a, w] * total - mid)
                if keep != 0.0:
                    move = move + keep * d[a, w]
                d[a, w] = move
                dst[a, w] = mid + move

        spread(planes[0], planes[1] - planes[0], 8, run)

    def first(dst, d, g, jn, planes, rows, new):
        w = slice(*rows)

        for a in range(*planes):
            move = new * (jn[a, w] * g[a, w])
            d[a, w] = move
            dst[a, w] = move

    ws1 = (s1, wx1, wl1, wr1, zl1, zr1)
    ws2 = (s2, wx2, wl2, wr2, zl2, zr2)
    ws3 = (s3, wx3, wl3, wr3, zl3, zr3)
    rows1, wide2, rows2, rows3 = (8, 56), (8, 88), (32, 64), (8, 48)

    h_c1.arrive()
    setup(c1, j1, i1, wx1, wl1, wr1, zl1, zr1, (1, 15), rows1, 1, 0.25)
    m_s1.arrive()
    first(va1, d1, s1, j1, (2, 14), rows1, FINE_STEPS[0][1])
    sweep(va1, vb1, d1, j1, ws1, (3, 13), rows1, 1, FINE_STEPS[1])
    sweep(vb1, va1, d1, j1, ws1, (4, 12), rows1, 1, FINE_STEPS[2])
    sweep(va1, vb1, d1, j1, ws1, (5, 11), rows1, 1, FINE_STEPS[3])

    def residual(src, low, ws, dn, rows, step):
        parts = [total - dn[a, slice(*rows)] * mid for a, mid, total in gather_sum(src, low, 2, *ws, rows, step)]
        return parts[0] + parts[1]

    for m in range(2):
        tmp[m, 0, 0:32] = residual(vb1, 6 + 2 * m, ws1, i1, (16, 48), 1)
    for m in range(2):
        for t in range(2):
            s2[7 + m, 40 + 8 * t:48 + 8 * t] = 0.125 * fold_lanes(fold_rows(tmp.at[m, 0], t), 1)
    m_s2.start()
    k1[6:10, 16:48] = vb1[6:10, 16:48]
    y_k1.start()
    h_s1.start()
    y_pre.arrive()
    h_pre.start()
    h_c2.arrive()
    others2 = tuple(range(7)) + tuple(range(9, 16))
    widen(pc2, c2, others2, 8, 80, 2)
    setup(c2, j2, i2, wx2, wl2, wr2, zl2, zr2, (1, 15), wide2, 2, 0.0625)
    for moved in (y_c1, y_c2, h_c1, h_c2, m_s1, y_pre):
        moved.drain()

    m_s2.arrive()
    first(va2, d2, s2, j2, (3, 13), wide2, FINE_STEPS[0][1])
    sweep(va2, vb2, d2, j2, ws2, (4, 12), wide2, 2, FINE_STEPS[1])
    sweep(vb2, va2, d2, j2, ws2, (5, 11), wide2, 2, FINE_STEPS[2])
    sweep(va2, vb2, d2, j2, ws2, (6, 10), wide2, 2, FINE_STEPS[3])
    tmp[2, 0] = residual(vb2, 7, ws2, i2, (16, 80), 2)
    for t in range(4):
        s3[p + 1, 12 + 8 * t:20 + 8 * t] = 0.125 * fold_lanes(fold_rows(tmp.at[2, 0], t), 2)
    ps3[p + 1] = squeeze(s3, p + 1, 12, 32, 4)
    h_s3.start()
    k2[7:9, 32:64] = vb2[7:9, 32:64]
    for a in (7, 8):
        pk2[a] = squeeze(vb2, a, 32, 32, 2)
    h_k2.start()
    y_k1.arrive()
    h_k1.start()
    h_s2.start()
    h_c3.arrive()
    widen(pc3, c3, range(1, 17), 12, 32, 4)
    setup(c3, j3, i3, wx3, wl3, wr3, zl3, zr3, (1, 17), rows3, 4, 0.015625)
    for moved in (h_c3, h_pre, m_s2, y_k1, h_s1):
        moved.drain()

    h_s3.arrive()
    widen(ps3, s3, range(1, 17), 12, 32, 4)
    first(va3, d3, s3, j3, (1, 17), rows3, BOTTOM_STEPS[0][1])
    here, there = va3, vb3
    for at in range(1, BOTTOM):
        halo = BOTTOM + 3 - at
        rows = (12, 44) if halo > 8 else (16, 40)
        sweep(here, there, d3, j3, ws3, (1, 17), rows, 4, BOTTOM_STEPS[at])
        here, there = there, here

    h_k2.arrive()
    widen(pk2, k2, others2, 32, 32, 2)
    h_s2.arrive()

    def finish2(a):
        up = jnp.clip(p - 3 + (a + 1) // 2, 0, 17)
        for t in range(2):
            e = here[up, 20 + 8 * t:28 + 8 * t]
            for odd in range(2):
                at = pl.ds(32 + 16 * t + odd, 8, stride=2)
                va2[a, at] = k2[a, at] + e

    for a in range(16):
        finish2(a)
    sweep(va2, vb2, d2, j2, ws2, (1, 15), rows2, 2, FINE_STEPS[0])
    sweep(vb2, va2, d2, j2, ws2, (2, 14), rows2, 2, FINE_STEPS[1])
    sweep(va2, vb2, d2, j2, ws2, (3, 13), rows2, 2, FINE_STEPS[2])
    sweep(vb2, va2, d2, j2, ws2, (4, 12), rows2, 2, FINE_STEPS[3])

    h_k1.arrive()
    h_s1.arrive()

    def finish1(a):
        up = 4 + a // 2
        for t in range(3):
            e = va2[up, 36 + 8 * t:44 + 8 * t]
            for odd in range(2):
                at = pl.ds(8 + 16 * t + odd, 8, stride=2)
                va1[a, at] = k1[a, at] + e

    for a in range(16):
        finish1(a)
    sweep(va1, vb1, d1, j1, ws1, (1, 15), rows1, 1, FINE_STEPS[0])
    sweep(vb1, va1, d1, j1, ws1, (2, 14), rows1, 1, FINE_STEPS[1])
    sweep(va1, vb1, d1, j1, ws1, (3, 13), rows1, 1, FINE_STEPS[2])
    sweep(vb1, va1, d1, j1, ws1, (4, 12), rows1, 1, FINE_STEPS[3])

    h_pre.arrive()
    for moved in (h_k1, h_s2, h_s3, h_k2):
        moved.drain()

    def finish0(m):
        for t in range(5):
            e = va1[4 + m, 14 + 8 * t:22 + 8 * t]
            to_lane = lanes((8, 128)) // 2
            for h in range(2):
                half = jnp.take_along_axis(e, to_lane + 64 * h, axis=1)
                for x in range(2):
                    a = 1 + 2 * m + x
                    for odd in range(2):
                        at = pl.ds(12 + 16 * t + odd, 8, stride=2)
                        va[a, h, at] = pre[a, h, at] + half

    loop(0, 8, finish0)
    fine_sweep(va, vb, 0, 2, 14)
    fine_sweep(vb, va, 1, 3, 12)
    fine_sweep(va, vb, 2, 4, 10)
    fine_sweep(vb, va, 3, 5, 8)
    give = pltpu.make_async_remote_copy(
        src_ref=va.at[pl.ds(5, 8), 1 - k, pl.ds(16, 64)],
        dst_ref=out.at[pl.ds(8 * k, 8)],
        send_sem=sem.at[out_send],
        recv_sem=sem.at[out_recv],
        device_id=(i, j, 1 - k),
        device_id_type=MESH,
    )
    give.start()
    out[pl.ds(8 * k, 8)] = va[5:13, k, own]
    give.wait_send()
    pltpu.make_async_remote_copy(
        src_ref=va.at[pl.ds(5, 8), k, pl.ds(16, 64)],
        dst_ref=out.at[pl.ds(8 * (1 - k), 8)],
        send_sem=sem.at[out_send],
        recv_sem=sem.at[out_recv],
        device_id=(i, j, 1 - k),
        device_id_type=MESH,
    ).wait_recv()


def on_device(iterate, right_side, diffusion):
    def buf(*shape):
        return pltpu.VMEM(shape, F32)

    scratch = [buf(18, 2, 96, 128)] * 3 + [buf(4, 2, 64, 128)] + [buf(18, 2, 96, 128)] * 13
    scratch += [buf(16, 64, 128)] * 13
    scratch += [buf(16, 96, 128)] * 13 + [buf(16, 40, 128), buf(16, 16, 128)]
    scratch += [buf(18, 56, 128)] * 12 + [buf(18, 8, 128)] * 2
    dma = pltpu.SemaphoreType.DMA
    scratch += [dma((SEMS,)), dma((3,))]
    return pl.pallas_call(
        kernel,
        out_shape=pltpu.VMEM((16, 64, 128), F32),
        in_specs=[pl.BlockSpec(memory_space=pl.ANY)] * 3,
        out_specs=pl.BlockSpec(memory_space=pltpu.VMEM),
        scratch_shapes=scratch,
        compiler_params=pltpu.CompilerParams(
            collective_id=0, has_side_effects=True, vmem_limit_bytes=60 * 2**20
        ),
        cost_estimate=pl.CostEstimate(flops=10**8, bytes_accessed=2 * 10**6, transcendentals=0),
        name="vcycle",
    )(iterate, right_side, diffusion)


def solution(mesh):
    placed = (P("gx", "gy", "gz"), P("gx", "gy", "gz"), P("gx", "gy", "gz"))
    return jax.shard_map(
        on_device, mesh=mesh, in_specs=placed, out_specs=P("gx", "gy", "gz"), check_vma=False
    )
```

```python
import jax
import jax.numpy as jnp
from jax import lax
from jax.experimental import pallas as pl
from jax.experimental.pallas import tpu as pltpu
from jax.sharding import PartitionSpec as P

DEGREE = 4
BOTTOM = 8
SMOOTH_LOW = 0.25
SMOOTH_HIGH = 2.0
BOTTOM_LOW = 0.05

F32 = jnp.float32
MESH = pl.DeviceIdType.MESH
NP = 16
NJ = 8
FINE_SEND = 0
FINE_RECV = 95
SEMS = 95 + 33 + 6 + 13 + 8 + 4 + 24 + 6 + 4 + 1 + 8 + 1


def chebyshev_steps(sweeps, low_end, high_end):
    center = 0.5 * (high_end + low_end)
    radius = 0.5 * (high_end - low_end)
    sigma_ratio = center / radius
    rho_old = 1.0 / sigma_ratio
    steps_out = [(0.0, 1.0 / center)]
    for sweep_index in range(1, sweeps):
        rho_new = 1.0 / (2.0 * sigma_ratio - rho_old)
        steps_out.append((rho_new * rho_old, 2.0 * rho_new / radius))
        rho_old = rho_new
    return steps_out


FINE_STEPS = chebyshev_steps(DEGREE, SMOOTH_LOW, SMOOTH_HIGH)
BOTTOM_STEPS = chebyshev_steps(BOTTOM, BOTTOM_LOW, SMOOTH_HIGH)


def loop(low, high, body):
    def step(index, carry):
        body(index)
        return carry

    lax.fori_loop(low, high, step, 0)


def spread(low, count, most, body):
    runs = -(-count // most)
    each = -(-count // runs)
    full = count // each
    if full > 1:
        loop(0, full, lambda r: body(low + r * each, each))
    elif full == 1:
        body(low, each)
    if count % each:
        body(low + full * each, count % each)


def lanes(shape):
    return lax.broadcasted_iota(jnp.int32, shape, len(shape) - 1)


class Moves:
    def __init__(self, place, ref, sem, send, recv, dirs):
        self.place, self.ref, self.sem, self.dirs = place, ref, sem, dirs
        self.send, self.recv = send, recv

    def copy(self, at):
        p, j = self.place
        dp, dj, src, dst = self.dirs[at]
        to = p + dp
        return pltpu.make_async_remote_copy(
            src_ref=self.ref.at[src],
            dst_ref=self.ref.at[dst],
            send_sem=self.sem.at[self.send + at],
            recv_sem=self.sem.at[self.recv + at],
            device_id=(to // 2, j + dj, to % 2),
            device_id_type=MESH,
        )

    def each(self, sign, act):
        p, j = self.place
        for at, (dp, dj, src, dst) in enumerate(self.dirs):
            ok = None
            for value, count, shift in ((p, NP, sign * dp), (j, NJ, sign * dj)):
                if shift > 0:
                    good = value < count - shift
                elif shift < 0:
                    good = value >= -shift
                else:
                    continue
                ok = good if ok is None else jnp.logical_and(ok, good)

            @pl.when(ok)
            def _():
                act(self.copy(at))

    def start(self):
        self.each(1, lambda c: c.start())

    def arrive(self):
        self.each(-1, lambda c: c.wait_recv())

    def drain(self):
        self.each(1, lambda c: c.wait_send())


def block_dirs(planes, first, halo, row, rows, dps, djs, wide, mid=()):
    out = []
    for dj in djs:
        for dp in dps:
            if dp == 0 and dj == 0:
                continue
            if dp > 0:
                x0 = max(0, planes * dp - halo)
                count = planes - x0
            elif dp < 0:
                x0 = 0
                count = min(planes, planes + halo + planes * dp)
            else:
                x0, count = 0, planes
            if dj == 0:
                low, size = (row - 8, rows + 16) if wide else (row, rows)
                to = low
            elif dj > 0:
                low, size, to = row + rows - 8, 8, row - 8
            else:
                low, size, to = row, 8, row + rows
            a = first + x0
            src = (pl.ds(a, count),) + mid + (pl.ds(low, size),)
            dst = (pl.ds(a - planes * dp, count),) + mid + (pl.ds(to, size),)
            out.append((dp, dj, src, dst))
    return out


def line(ref, start):
    return ref[pl.ds(start, 8, stride=2)]


def kernel(
    iterate, right_side, diffusion, out,
    va, cc, gg, tmp, vb, vc, vd, ve,
    dd, jj, di, wx, wl, wr, zl, zr, pre,
    s1, c1, k1, va1, vb1, d1, j1, i1, wx1, wl1, wr1, zl1, zr1,
    s2, c2, k2, va2, vb2, d2, j2, i2, wx2, wl2, wr2, zl2, zr2, pc2, pk2,
    s3, c3, va3, vb3, d3, j3, i3, wx3, wl3, wr3, zl3, zr3, pc3, ps3,
    face, yb, yd, ry, rd,
    sem, self_sem,
):
    i = lax.axis_index("gx")
    j = lax.axis_index("gy")
    k = lax.axis_index("gz")
    p = 2 * i + k
    place = (p, j)

    faces = []
    for at, src in enumerate((diffusion, iterate, right_side)):
        for t, low in enumerate((56, 0)):
            faces.append(pltpu.make_async_copy(src.at[pl.ds(0, 16), pl.ds(low, 8)], face.at[at, t], self_sem.at[3 + 2 * at + t]))
    for load in faces:
        load.start()

    barrier = pltpu.get_barrier_semaphore()

    def greet(to, tj):
        pl.semaphore_signal(
            barrier, inc=1, device_id=(to // 2, tj, to % 2), device_id_type=MESH
        )

    loop(1, NP, lambda q: greet((p + q) % NP, j))
    count = NP - 1
    for dj in (-1, 1, -2, 2):
        okj = jnp.logical_and(j + dj >= 0, j + dj < NJ)
        for dp in range(-2, 3):
            ok = jnp.logical_and(okj, jnp.logical_and(p + dp >= 0, p + dp < NP))
            count = count + ok.astype(jnp.int32)

            @pl.when(ok)
            def _():
                greet(p + dp, j + dj)

    for load in faces:
        load.wait()

    def pack_faces(at):
        for t, low in enumerate((3, 0)):
            for m in range(12):
                for half in range(2):
                    yb[at, t, half, 5 * m:5 * m + 5] = face[at, t, m + 4 * half, low:low + 5]
            for m in range(4):
                for end in range(2):
                    yd[at, t, end, 5 * m:5 * m + 5] = face[at, t, m + 12 * (1 - end), low:low + 5]

    loop(0, 3, pack_faces)
    pl.semaphore_wait(barrier, count)

    def fine_moves(at, src, dst, halo):
        n = 8 + halo

        def copy(slot_s, slot_r, x0, nx, a0, low, size, to, zh, dev):
            return pltpu.make_async_remote_copy(
                src_ref=src.at[pl.ds(x0, nx), pl.ds(low, size)],
                dst_ref=dst.at[pl.ds(a0, nx), zh, pl.ds(to, size)],
                send_sem=sem.at[FINE_SEND + 11 * at + slot_s],
                recv_sem=sem.at[FINE_RECV + 11 * at + slot_r],
                device_id=dev,
                device_id_type=MESH,
            )

        mine = pltpu.make_async_copy(
            src.at[pl.ds(k * (8 - halo), n)],
            dst.at[pl.ds(5 - halo * k, n), k, pl.ds(16, 64)],
            self_sem.at[at],
        )
        other = 1 - k
        def outer_rows(slot_s, slot_r, src_rows, dst_rows, dev):
            return pltpu.make_async_remote_copy(
                src_ref=src_rows,
                dst_ref=dst_rows,
                send_sem=sem.at[FINE_SEND + 11 * at + slot_s],
                recv_sem=sem.at[FINE_RECV + 11 * at + slot_r],
                device_id=dev,
                device_id_type=MESH,
            )

        inner = [(None, copy(0, 0, other * (8 - halo), n, 5 - halo * other, 0, 64, 16, k, (i, j, other)))]
        sends = []
        sends.append((i < 7, copy(1, 1 + k, 16 - halo, halo, 5 - halo, 0, 64, 16, k, (i + 1, j, 0))))
        sends.append((i > 0, copy(2, 1 + k, 0, halo, 13, 0, 64, 16, k, (i - 1, j, 1))))
        turns = ((0, 1, 11), (1, -1, 80))
        for t, dj, to in turns:
            okj = jnp.logical_and(j + dj >= 0, j + dj < NJ)
            up = jnp.logical_and(i < 7, okj)
            down = jnp.logical_and(i > 0, okj)
            slot = 3 + 2 * t
            sends.append((up, outer_rows(slot, slot + k, yd.at[at, t, 0], rd.at[at, t, k], (i + 1, j + dj, 0))))
            sends.append((down, outer_rows(slot + 1, slot + k, yd.at[at, t, 1], rd.at[at, t, k], (i - 1, j + dj, 1))))
            slot = 7 + 2 * t
            for half in (0, 1):
                inner.append((okj, outer_rows(slot + half, slot + k, yb.at[at, t, half], ry.at[at, t, k], (i, j + dj, half))))

        def start(part):
            if part == 0:
                mine.start()
            for ok, c in (inner, sends)[part]:
                if ok is None:
                    c.start()
                else:
                    pl.when(ok)(c.start)

        def unpack(buf, t, to, first, planes):
            for half in (0, 1):
                for m in range(planes):
                    dst[first + m, half, to:to + 5] = buf[at, t, half, 5 * m:5 * m + 5]

        def arrive_inner():
            mine.wait()
            copy(0, 0, 0, n, 5 - halo * k, 0, 64, 16, other, (i, j, other)).wait_recv()
            for t, dj, to in turns:

                @pl.when(jnp.logical_and(j - dj >= 0, j - dj < NJ))
                def _():
                    for half in (0, 1):
                        outer_rows(0, 7 + 2 * t + half, yb.at[at, t, 0], ry.at[at, t, half], (i, j, other)).wait_recv()
                    unpack(ry, t, to, 5 - 4 * k, 12)

        def arrive_outer():
            beside = jnp.logical_or(jnp.logical_and(k == 0, i > 0), jnp.logical_and(k == 1, i < 7))
            a0 = (5 - halo) * (1 - k) + 13 * k

            @pl.when(beside)
            def _():
                for half in (0, 1):
                    copy(0, 1 + half, 0, halo, a0, 0, 64, 16, half, (i, j, other)).wait_recv()

            for t, dj, to in turns:

                @pl.when(jnp.logical_and(beside, jnp.logical_and(j - dj >= 0, j - dj < NJ)))
                def _():
                    for half in (0, 1):
                        outer_rows(0, 3 + 2 * t + half, yd.at[at, t, 0], rd.at[at, t, half], (i, j, other)).wait_recv()
                    unpack(rd, t, to, 1 + 12 * k, 4)

        def drain():
            for ok, c in inner + sends:
                if ok is None:
                    c.wait_send()
                else:
                    pl.when(ok)(c.wait_send)

        return start, arrive_inner, arrive_outer, drain

    moves_c = fine_moves(0, diffusion, cc, 5)
    moves_v = fine_moves(1, iterate, va, 5)
    moves_g = fine_moves(2, right_side, gg, 4)
    for part in range(2):
        for moved in (moves_c, moves_v, moves_g):
            moved[0](part)

    def clear(ref, planes, low_planes, high_from, edges, own=None):
        def wipe(a):
            ref[a] = jnp.zeros(ref.shape[1:], F32)

        loop(0, low_planes, wipe)
        loop(high_from, planes, wipe)

        def wipe_rows(low, size):
            def one(a):
                if len(ref.shape) == 4:
                    ref[a, :, low:low + size] = jnp.zeros((2, size, 128), F32)
                else:
                    ref[a, low:low + size] = jnp.zeros((size, 128), F32)

            loop(*(own or (0, planes)), one)

        for test, low, size in edges:
            pl.when(test)(lambda low=low, size=size: wipe_rows(low, size))

    def outer(first, planes, per, total):
        low = jnp.clip(first - per * p, 0, planes)
        high = jnp.clip(total - per * p + first, 0, planes)
        return low, high

    low, high = outer(5, 18, 8, 128)
    for ref in (va, cc, gg):
        clear(ref, 18, low, high, [(j == 0, 8, 8), (j == 7, 80, 8)])
    clear(pre, 18, low, high, [(j == 0, 8, 8), (j == 7, 80, 8)], (5, 13))
    low, high = outer(6, 16, 4, 64)
    for ref, owned in ((s1, None), (c1, (6, 10)), (k1, (6, 10))):
        clear(ref, 16, low, high, [(j == 0, 8, 8), (j == 7, 48, 8)], owned)
    low, high = outer(7, 16, 2, 32)
    for ref, owned in ((s2, None), (c2, (7, 9))):
        clear(ref, 16, low, high, [(j == 0, 8, 32), (j == 1, 8, 16), (j == 6, 72, 16), (j == 7, 56, 32)], owned)
    for ref in (pc2, pk2):
        clear(ref, 16, low, high, [])
    for ref in (c3, va3, vb3):
        clear(ref, 18, 1, 17, [])

    def fold_rows(ref, at):
        return line(ref, 16 * at) + line(ref, 16 * at + 1)

    def fold_lanes(value, step):
        even = (lanes(value.shape) // step) % 2 == 0
        return value + jnp.where(even, pltpu.roll(value, 128 - step, 1), pltpu.roll(value, step, 1))

    def pack(halves, at):
        low, high = (fold_lanes(fold_rows(half, at), 1) for half in halves)
        from_lane = (2 * lanes((8, 128))) % 128
        low = jnp.take_along_axis(low, from_lane, axis=1)
        high = jnp.take_along_axis(high, from_lane, axis=1)
        return 0.125 * jnp.where(lanes((8, 128)) < 64, low, high)

    def squeeze(ref, a, row, rows, parts):
        size = rows // parts
        spot = lanes((size, 128)) % parts
        res = ref[a, row:row + size]
        for q in range(1, parts):
            res = jnp.where(spot == q, ref[a, row + q * size:row + (q + 1) * size], res)
        return res

    def widen(src, dst, planes, row, rows, parts):
        size = rows // parts
        spot = lanes((8, 128))
        spot = spot - spot % parts
        for a in planes:
            for r in range(0, size, 8):
                value = src[a, r:r + 8]
                for q in range(parts):
                    at = row + q * size + r
                    dst[a, at:at + 8] = jnp.take_along_axis(value, spot + q, axis=1)

    own = slice(16, 80)
    moves_c[1]()

    def coarsen_c(m):
        a = 5 + 2 * m
        for h in range(2):
            tmp[m, h] = cc[a, h, own] + cc[a + 1, h, own]
        for t in range(4):
            c1[6 + m, 16 + 8 * t:24 + 8 * t] = pack((tmp.at[m, 0], tmp.at[m, 1]), t)

    for m in range(4):
        coarsen_c(m)
    for m in range(2):
        tmp[m, 0, 0:32] = c1[6 + 2 * m, 16:48] + c1[7 + 2 * m, 16:48]
        for t in range(2):
            c2[7 + m, 40 + 8 * t:48 + 8 * t] = 0.125 * fold_lanes(fold_rows(tmp.at[m, 0], t), 1)

    used = {"recv": FINE_RECV + 33, "send": 0}

    def moves(ref, send, dirs):
        recv = used["recv"]
        used["recv"] = recv + len(dirs)
        return Moves(place, ref, sem, send, recv, dirs)

    def y_moves(send, ref, planes, first, row, rows, mid=()):
        return moves(ref, send, block_dirs(planes, first, 0, row, rows, (0,), (-1, 1), False, mid))

    def h_moves(send, ref, planes, first, halo, row, rows, dps, mid=()):
        return moves(ref, send, block_dirs(planes, first, halo, row, rows, dps, (0,), True, mid))

    def column_moves(send, ref, dps, djs):
        dirs = []
        for dp, dj, src, dst in block_dirs(2, 7, 4, 40, 16, dps, (0,), False):
            dirs.append((dp, 0, src, dst))
        for dj in djs:
            for dp in (0,) + tuple(dps):
                row = pl.ds(40 - 16 * dj, 16)
                dirs.append((dp, dj, (pl.ds(7, 2), pl.ds(40, 16)), (pl.ds(7 - 2 * dp, 2), row)))
        return moves(ref, send, dirs)

    class Around:
        def __init__(self, send, ref):
            self.send, self.ref, self.recv = send, ref, used["recv"]
            used["recv"] += 1

        def copy(self, q, src, dst):
            to = (p + q) % NP
            return pltpu.make_async_remote_copy(
                src_ref=self.ref.at[src],
                dst_ref=self.ref.at[dst],
                send_sem=sem.at[self.send],
                recv_sem=sem.at[self.recv],
                device_id=(to // 2, j, to % 2),
                device_id_type=MESH,
            )

        def start(self):
            loop(1, NP, lambda q: self.copy(q, p + 1, p + 1).start())

        def all(self):
            planes = pl.ds(1, NP - 1)
            return self.copy(1, planes, planes)

        def arrive(self):
            self.all().wait_recv()

        def drain(self):
            self.all().wait_send()

    y_c1 = y_moves(33, c1, 4, 6, 16, 32)
    y_c2 = column_moves(35, c2, (), (-2, -1, 1, 2))
    h_c1 = h_moves(0, c1, 4, 6, 6, 16, 32, (-2, -1, 1, 2))
    h_c2 = h_moves(4, pc2, 2, 7, 7, 8, 24, (-4, -3, -2, -1, 1, 2, 3, 4))
    h_c3 = Around(12, pc3)
    m_s1 = moves(s1, 39, block_dirs(4, 6, 4, 16, 32, (-1, 0, 1), (0, -1, 1), False))
    y_pre = y_moves(47, pre, 8, 5, 16, 64, (slice(None),))
    h_pre = h_moves(49, pre, 8, 5, 4, 16, 64, (-1, 1), (slice(None),))
    m_s2 = column_moves(51, s2, (-2, -1, 1, 2), (-2, -1, 1, 2))
    y_k1 = y_moves(75, k1, 4, 6, 16, 32)
    h_k1 = h_moves(77, k1, 4, 6, 6, 16, 32, (-2, -1, 1, 2))
    h_s1 = h_moves(81, s1, 4, 6, 5, 16, 32, (-2, 2))
    h_s2 = h_moves(83, s2, 2, 7, 6, 40, 16, (-3, 3))
    h_s3 = Around(85, ps3)
    h_k2 = h_moves(86, pk2, 2, 7, 7, 8, 0, (-4, -3, -2, -1, 1, 2, 3, 4))
    out_send, out_recv = 94, used["recv"]
    assert out_recv < SEMS, out_recv

    y_c1.start()
    y_c2.start()

    wide = slice(12, 84)
    lane = lanes((72, 128))

    def fine_setup(low, n):
        for a in [low + u for u in range(n)]:
            mid = [cc[a, h, wide] for h in range(2)]
            prev = [pltpu.roll(m, 1, 1) for m in mid]
            foll = [pltpu.roll(m, 127, 1) for m in mid]
            left = (jnp.where(lane == 0, 0.0, prev[0]), jnp.where(lane == 0, prev[0], prev[1]))
            right = (jnp.where(lane == 127, foll[1], foll[0]), jnp.where(lane == 127, 0.0, foll[1]))
            for h in range(2):
                ahead = cc[a + 1, h, wide]
                yl = cc[a, h, 11:83]
                yr = cc[a, h, 13:85]
                wx[a, h, wide] = 0.5 * (mid[h] + ahead)
                wl[a, h, wide] = 0.5 * (mid[h] + yl)
                wr[a, h, wide] = 0.5 * (mid[h] + yr)
                low_edge = 0.5 * (mid[h] + left[h])
                high_edge = 0.5 * (mid[h] + right[h])
                zl[a, h, wide] = jnp.where(lane == 0, 0.0, low_edge) if h == 0 else low_edge
                zr[a, h, wide] = jnp.where(lane == 127, 0.0, high_edge) if h == 1 else high_edge
                diag = 0.5 * (6.0 * mid[h] + (cc[a - 1, h, wide] + ahead) + (yl + yr) + (left[h] + right[h]))
                di[a, h, wide] = diag
                jj[a, h, wide] = jnp.where(mid[h] > 0.0, 1.0 / diag, 0.0)

    def fine_setups(low, count):
        wx[low - 1, :, wide] = 0.5 * (cc[low - 1, :, wide] + cc[low, :, wide])
        spread(low, count, 3, fine_setup)

    fine_setups(6 - 5 * k, 11)
    moves_v[1]()
    moves_g[1]()

    def fine_sum(src, low, n, r0, r1):
        for r in range(r0, r1, 24 if (r1 - r0) % 24 == 0 else 32):
            e = r + (24 if (r1 - r0) % 24 == 0 else 32)
            w = slice(r, e)
            spot = lanes((e - r, 128))
            v = [[src[low + u, h, w] for h in range(2)] for u in range(-1, n + 1)]
            x = [[wx[low + u, h, w] for h in range(2)] for u in range(-1, n)]
            for u in range(n):
                a = low + u
                mid = v[u + 1]
                prev = [pltpu.roll(m, 1, 1) for m in mid]
                foll = [pltpu.roll(m, 127, 1) for m in mid]
                left = (prev[0], jnp.where(spot == 0, prev[0], prev[1]))
                right = (jnp.where(spot == 127, foll[1], foll[0]), foll[1])
                for h in range(2):
                    total = gg[a, h, w] + x[u][h] * v[u][h] + x[u + 1][h] * v[u + 2][h]
                    total = total + wl[a, h, w] * src[a, h, r - 1:e - 1] + wr[a, h, w] * src[a, h, r + 1:e + 1]
                    total = total + zl[a, h, w] * left[h] + zr[a, h, w] * right[h]
                    yield u, a, h, w, mid[h], total

    def fine_sweep(src, dst, step, low_plane, count, most=4):
        keep, new = FINE_STEPS[step]

        def run(low, n):
            for u, a, h, w, mid, total in fine_sum(src, low, n, 12, 84):
                move = new * (jj[a, h, w] * total - mid)
                if step > 0:
                    move = move + keep * dd[a, h, w]
                dd[a, h, w] = move
                dst[a, h, w] = mid + move

        spread(low_plane, count, most, run)

    rounds = ((va, vb), (vb, vc), (vc, vd), (vd, ve))
    for step, (src, dst) in enumerate(rounds):
        fine_sweep(src, dst, step, 6 + step - 5 * k, 11 - 2 * step)
    moves_c[2]()
    fine_setups(1 + 11 * k, 5)
    moves_v[2]()
    moves_g[2]()
    for moved in (moves_c, moves_v, moves_g):
        moved[3]()
    y_c1.arrive()
    h_c1.start()
    for step, (src, dst) in enumerate(rounds):
        fine_sweep(src, dst, step, 1 + step + (11 - 2 * step) * k, 5, 5)

    for m in range(4):
        for u, a, h, w, mid, total in fine_sum(ve, 5 + 2 * m, 2, 16, 80):
            part = total - di[a, h, w] * mid
            spot = slice(w.start - 16, w.stop - 16)
            tmp[m, h, spot] = part if u == 0 else tmp[m, h, spot] + part
        for t in range(4):
            s1[6 + m, 16 + 8 * t:24 + 8 * t] = pack((tmp.at[m, 0], tmp.at[m, 1]), t)

    m_s1.start()

    def keep_fine(a):
        pre[a, :, own] = ve[a, :, own]

    loop(5, 13, keep_fine)
    y_pre.start()
    y_c2.arrive()
    for a in (7, 8):
        pc2[a] = squeeze(c2, a, 8, 80, 2)
    h_c2.start()
    tmp[2, 0] = c2[7, 16:80] + c2[8, 16:80]
    for t in range(4):
        c3[p + 1, 12 + 8 * t:20 + 8 * t] = 0.125 * fold_lanes(fold_rows(tmp.at[2, 0], t), 2)
    pc3[p + 1] = squeeze(c3, p + 1, 12, 32, 4)
    h_c3.start()

    def setup(c, jn, dn, wxn, wln, wrn, zln, zrn, planes, rows, step, scale):
        low, high = planes
        r0, r1 = rows
        w = slice(r0, r1)
        spot = lanes((r1 - r0, 128))
        half = 0.5 * scale

        def run(first_plane, n):
            for a in [first_plane + u for u in range(n)]:
                mid = c[a, w]
                ahead = c[a + 1, w]
                left = jnp.where(spot < step, 0.0, pltpu.roll(mid, step, 1))
                right = jnp.where(spot >= 128 - step, 0.0, pltpu.roll(mid, 128 - step, 1))
                yl = c[a, r0 - 1:r1 - 1]
                yr = c[a, r0 + 1:r1 + 1]
                wxn[a, w] = half * (mid + ahead)
                wln[a, w] = half * (mid + yl)
                wrn[a, w] = half * (mid + yr)
                zln[a, w] = jnp.where(spot < step, 0.0, half * (mid + left))
                zrn[a, w] = jnp.where(spot >= 128 - step, 0.0, half * (mid + right))
                diag = half * (6.0 * mid + (c[a - 1, w] + ahead) + (yl + yr) + (left + right))
                dn[a, w] = diag
                jn[a, w] = jnp.where(mid > 0.0, 1.0 / diag, 0.0)

        wxn[low - 1, w] = half * (c[low - 1, w] + c[low, w])
        spread(low, high - low, 7 if high - low == 14 else 8, run)

    def gather_sum(src, low, n, g, wxn, wln, wrn, zln, zrn, rows, step):
        r0, r1 = rows
        w = slice(r0, r1)
        v = [src[low + u, w] for u in range(-1, n + 1)]
        x = [wxn[low + u, w] for u in range(-1, n)]
        for u in range(n):
            a = low + u
            mid = v[u + 1]
            total = g[a, w] + x[u] * v[u] + x[u + 1] * v[u + 2]
            total = total + wln[a, w] * src[a, r0 - 1:r1 - 1] + wrn[a, w] * src[a, r0 + 1:r1 + 1]
            total = total + zln[a, w] * pltpu.roll(mid, step, 1) + zrn[a, w] * pltpu.roll(mid, 128 - step, 1)
            yield a, mid, total

    def sweep(src, dst, d, jn, ws, planes, rows, step, pair):
        keep, new = pair
        w = slice(*rows)

        def run(low, n):
            for a, mid, total in gather_sum(src, low, n, *ws, rows, step):
                move = new * (jn[a, w] * total - mid)
                if keep != 0.0:
                    move = move + keep * d[a, w]
                d[a, w] = move
                dst[a, w] = mid + move

        spread(planes[0], planes[1] - planes[0], 8, run)

    def first(dst, d, g, jn, planes, rows, new):
        w = slice(*rows)

        for a in range(*planes):
            move = new * (jn[a, w] * g[a, w])
            d[a, w] = move
            dst[a, w] = move

    ws1 = (s1, wx1, wl1, wr1, zl1, zr1)
    ws2 = (s2, wx2, wl2, wr2, zl2, zr2)
    ws3 = (s3, wx3, wl3, wr3, zl3, zr3)
    rows1, wide2, rows2, rows3 = (8, 56), (8, 88), (32, 64), (8, 48)

    h_c1.arrive()
    setup(c1, j1, i1, wx1, wl1, wr1, zl1, zr1, (1, 15), rows1, 1, 0.25)
    m_s1.arrive()
    first(va1, d1, s1, j1, (2, 14), rows1, FINE_STEPS[0][1])
    sweep(va1, vb1, d1, j1, ws1, (3, 13), rows1, 1, FINE_STEPS[1])
    sweep(vb1, va1, d1, j1, ws1, (4, 12), rows1, 1, FINE_STEPS[2])
    sweep(va1, vb1, d1, j1, ws1, (5, 11), rows1, 1, FINE_STEPS[3])

    def residual(src, low, ws, dn, rows, step):
        parts = [total - dn[a, slice(*rows)] * mid for a, mid, total in gather_sum(src, low, 2, *ws, rows, step)]
        return parts[0] + parts[1]

    for m in range(2):
        tmp[m, 0, 0:32] = residual(vb1, 6 + 2 * m, ws1, i1, (16, 48), 1)
    for m in range(2):
        for t in range(2):
            s2[7 + m, 40 + 8 * t:48 + 8 * t] = 0.125 * fold_lanes(fold_rows(tmp.at[m, 0], t), 1)
    m_s2.start()
    k1[6:10, 16:48] = vb1[6:10, 16:48]
    y_k1.start()
    h_s1.start()
    y_pre.arrive()
    h_pre.start()
    h_c2.arrive()
    others2 = tuple(range(7)) + tuple(range(9, 16))
    widen(pc2, c2, others2, 8, 80, 2)
    setup(c2, j2, i2, wx2, wl2, wr2, zl2, zr2, (1, 15), wide2, 2, 0.0625)
    for moved in (y_c1, y_c2, h_c1, h_c2, m_s1, y_pre):
        moved.drain()

    m_s2.arrive()
    first(va2, d2, s2, j2, (3, 13), wide2, FINE_STEPS[0][1])
    sweep(va2, vb2, d2, j2, ws2, (4, 12), wide2, 2, FINE_STEPS[1])
    sweep(vb2, va2, d2, j2, ws2, (5, 11), wide2, 2, FINE_STEPS[2])
    sweep(va2, vb2, d2, j2, ws2, (6, 10), wide2, 2, FINE_STEPS[3])
    tmp[2, 0] = residual(vb2, 7, ws2, i2, (16, 80), 2)
    for t in range(4):
        s3[p + 1, 12 + 8 * t:20 + 8 * t] = 0.125 * fold_lanes(fold_rows(tmp.at[2, 0], t), 2)
    ps3[p + 1] = squeeze(s3, p + 1, 12, 32, 4)
    h_s3.start()
    k2[7:9, 32:64] = vb2[7:9, 32:64]
    for a in (7, 8):
        pk2[a] = squeeze(vb2, a, 32, 32, 2)
    h_k2.start()
    y_k1.arrive()
    h_k1.start()
    h_s2.start()
    h_c3.arrive()
    widen(pc3, c3, range(1, 17), 12, 32, 4)
    setup(c3, j3, i3, wx3, wl3, wr3, zl3, zr3, (1, 17), rows3, 4, 0.015625)
    for moved in (h_c3, h_pre, m_s2, y_k1, h_s1):
        moved.drain()

    h_s3.arrive()
    widen(ps3, s3, range(1, 17), 12, 32, 4)
    first(va3, d3, s3, j3, (1, 17), rows3, BOTTOM_STEPS[0][1])
    here, there = va3, vb3
    for at in range(1, BOTTOM):
        halo = BOTTOM + 3 - at
        rows = (12, 44) if halo > 8 else (16, 40)
        sweep(here, there, d3, j3, ws3, (1, 17), rows, 4, BOTTOM_STEPS[at])
        here, there = there, here

    h_k2.arrive()
    widen(pk2, k2, others2, 32, 32, 2)
    h_s2.arrive()

    def finish2(a):
        up = jnp.clip(p - 3 + (a + 1) // 2, 0, 17)
        for t in range(2):
            e = here[up, 20 + 8 * t:28 + 8 * t]
            for odd in range(2):
                at = pl.ds(32 + 16 * t + odd, 8, stride=2)
                va2[a, at] = k2[a, at] + e

    for a in range(16):
        finish2(a)
    sweep(va2, vb2, d2, j2, ws2, (1, 15), rows2, 2, FINE_STEPS[0])
    sweep(vb2, va2, d2, j2, ws2, (2, 14), rows2, 2, FINE_STEPS[1])
    sweep(va2, vb2, d2, j2, ws2, (3, 13), rows2, 2, FINE_STEPS[2])
    sweep(vb2, va2, d2, j2, ws2, (4, 12), rows2, 2, FINE_STEPS[3])

    h_k1.arrive()
    h_s1.arrive()

    def finish1(a):
        up = 4 + a // 2
        for t in range(3):
            e = va2[up, 36 + 8 * t:44 + 8 * t]
            for odd in range(2):
                at = pl.ds(8 + 16 * t + odd, 8, stride=2)
                va1[a, at] = k1[a, at] + e

    for a in range(16):
        finish1(a)
    sweep(va1, vb1, d1, j1, ws1, (1, 15), rows1, 1, FINE_STEPS[0])
    sweep(vb1, va1, d1, j1, ws1, (2, 14), rows1, 1, FINE_STEPS[1])
    sweep(va1, vb1, d1, j1, ws1, (3, 13), rows1, 1, FINE_STEPS[2])
    sweep(vb1, va1, d1, j1, ws1, (4, 12), rows1, 1, FINE_STEPS[3])

    h_pre.arrive()
    for moved in (h_k1, h_s2, h_s3, h_k2):
        moved.drain()

    def finish0(m):
        for t in range(5):
            e = va1[4 + m, 14 + 8 * t:22 + 8 * t]
            to_lane = lanes((8, 128)) // 2
            for h in range(2):
                half = jnp.take_along_axis(e, to_lane + 64 * h, axis=1)
                for x in range(2):
                    a = 1 + 2 * m + x
                    for odd in range(2):
                        at = pl.ds(12 + 16 * t + odd, 8, stride=2)
                        va[a, h, at] = pre[a, h, at] + half

    loop(0, 8, finish0)
    fine_sweep(va, vb, 0, 2, 14)
    fine_sweep(vb, va, 1, 3, 12)
    fine_sweep(va, vb, 2, 4, 10)
    fine_sweep(vb, va, 3, 5, 8)
    give = pltpu.make_async_remote_copy(
        src_ref=va.at[pl.ds(5, 8), 1 - k, pl.ds(16, 64)],
        dst_ref=out.at[pl.ds(8 * k, 8)],
        send_sem=sem.at[out_send],
        recv_sem=sem.at[out_recv],
        device_id=(i, j, 1 - k),
        device_id_type=MESH,
    )
    give.start()
    out[pl.ds(8 * k, 8)] = va[5:13, k, own]
    give.wait_send()
    pltpu.make_async_remote_copy(
        src_ref=va.at[pl.ds(5, 8), k, pl.ds(16, 64)],
        dst_ref=out.at[pl.ds(8 * (1 - k), 8)],
        send_sem=sem.at[out_send],
        recv_sem=sem.at[out_recv],
        device_id=(i, j, 1 - k),
        device_id_type=MESH,
    ).wait_recv()


def on_device(iterate, right_side, diffusion):
    def buf(*shape):
        return pltpu.VMEM(shape, F32)

    scratch = [buf(18, 2, 96, 128)] * 3 + [buf(4, 2, 64, 128)] + [buf(18, 2, 96, 128)] * 13
    scratch += [buf(16, 64, 128)] * 13
    scratch += [buf(16, 96, 128)] * 13 + [buf(16, 40, 128), buf(16, 16, 128)]
    scratch += [buf(18, 56, 128)] * 12 + [buf(18, 8, 128)] * 2
    scratch += [buf(3, 2, 16, 8, 128)] + [buf(3, 2, 2, 64, 128), buf(3, 2, 2, 24, 128)] * 2
    dma = pltpu.SemaphoreType.DMA
    scratch += [dma((SEMS,)), dma((9,))]
    return pl.pallas_call(
        kernel,
        out_shape=pltpu.VMEM((16, 64, 128), F32),
        in_specs=[pl.BlockSpec(memory_space=pl.ANY)] * 3,
        out_specs=pl.BlockSpec(memory_space=pltpu.VMEM),
        scratch_shapes=scratch,
        compiler_params=pltpu.CompilerParams(
            collective_id=0, has_side_effects=True, vmem_limit_bytes=60 * 2**20
        ),
        cost_estimate=pl.CostEstimate(flops=10**8, bytes_accessed=2 * 10**6, transcendentals=0),
        name="vcycle",
    )(iterate, right_side, diffusion)


def solution(mesh):
    placed = (P("gx", "gy", "gz"), P("gx", "gy", "gz"), P("gx", "gy", "gz"))
    return jax.shard_map(
        on_device, mesh=mesh, in_specs=placed, out_specs=P("gx", "gy", "gz"), check_vma=False
    )
```

```python
import jax
import jax.numpy as jnp
from jax import lax
from jax.experimental import pallas as pl
from jax.experimental.pallas import tpu as pltpu
from jax.sharding import PartitionSpec as P

DEGREE = 4
BOTTOM = 8
SMOOTH_LOW = 0.25
SMOOTH_HIGH = 2.0
BOTTOM_LOW = 0.05

F32 = jnp.float32
MESH = pl.DeviceIdType.MESH
NP = 16
NJ = 8
FINE_SEND = 0
FINE_RECV = 95
SEMS = 95 + 33 + 6 + 13 + 8 + 4 + 24 + 6 + 4 + 1 + 8 + 1


def chebyshev_steps(sweeps, low_end, high_end):
    center = 0.5 * (high_end + low_end)
    radius = 0.5 * (high_end - low_end)
    sigma_ratio = center / radius
    rho_old = 1.0 / sigma_ratio
    steps_out = [(0.0, 1.0 / center)]
    for sweep_index in range(1, sweeps):
        rho_new = 1.0 / (2.0 * sigma_ratio - rho_old)
        steps_out.append((rho_new * rho_old, 2.0 * rho_new / radius))
        rho_old = rho_new
    return steps_out


FINE_STEPS = chebyshev_steps(DEGREE, SMOOTH_LOW, SMOOTH_HIGH)
BOTTOM_STEPS = chebyshev_steps(BOTTOM, BOTTOM_LOW, SMOOTH_HIGH)


def loop(low, high, body):
    def step(index, carry):
        body(index)
        return carry

    lax.fori_loop(low, high, step, 0)


def spread(low, count, most, body):
    runs = -(-count // most)
    each = -(-count // runs)
    full = count // each
    if full > 1:
        loop(0, full, lambda r: body(low + r * each, each))
    elif full == 1:
        body(low, each)
    if count % each:
        body(low + full * each, count % each)


def lanes(shape):
    return lax.broadcasted_iota(jnp.int32, shape, len(shape) - 1)


class Moves:
    def __init__(self, place, ref, sem, send, recv, dirs):
        self.place, self.ref, self.sem, self.dirs = place, ref, sem, dirs
        self.send, self.recv = send, recv

    def copy(self, at):
        p, j = self.place
        dp, dj, src, dst = self.dirs[at]
        to = p + dp
        return pltpu.make_async_remote_copy(
            src_ref=self.ref.at[src],
            dst_ref=self.ref.at[dst],
            send_sem=self.sem.at[self.send + at],
            recv_sem=self.sem.at[self.recv + at],
            device_id=(to // 2, j + dj, to % 2),
            device_id_type=MESH,
        )

    def each(self, sign, act):
        p, j = self.place
        for at, (dp, dj, src, dst) in enumerate(self.dirs):
            ok = None
            for value, count, shift in ((p, NP, sign * dp), (j, NJ, sign * dj)):
                if shift > 0:
                    good = value < count - shift
                elif shift < 0:
                    good = value >= -shift
                else:
                    continue
                ok = good if ok is None else jnp.logical_and(ok, good)

            @pl.when(ok)
            def _():
                act(self.copy(at))

    def start(self):
        self.each(1, lambda c: c.start())

    def arrive(self):
        self.each(-1, lambda c: c.wait_recv())

    def drain(self):
        self.each(1, lambda c: c.wait_send())


def block_dirs(planes, first, halo, row, rows, dps, djs, wide, mid=()):
    out = []
    for dj in djs:
        for dp in dps:
            if dp == 0 and dj == 0:
                continue
            if dp > 0:
                x0 = max(0, planes * dp - halo)
                count = planes - x0
            elif dp < 0:
                x0 = 0
                count = min(planes, planes + halo + planes * dp)
            else:
                x0, count = 0, planes
            if dj == 0:
                low, size = (row - 8, rows + 16) if wide else (row, rows)
                to = low
            elif dj > 0:
                low, size, to = row + rows - 8, 8, row - 8
            else:
                low, size, to = row, 8, row + rows
            a = first + x0
            src = (pl.ds(a, count),) + mid + (pl.ds(low, size),)
            dst = (pl.ds(a - planes * dp, count),) + mid + (pl.ds(to, size),)
            out.append((dp, dj, src, dst))
    return out


def line(ref, start):
    return ref[pl.ds(start, 8, stride=2)]


def kernel(
    iterate, right_side, diffusion, out,
    va, cc, gg, tmp, vb, vc, vd, ve,
    dd, jj, di, wx, wl, wr, zl, zr, pre,
    s1, c1, k1, va1, vb1, d1, j1, i1, wx1, wl1, wr1, zl1, zr1,
    s2, c2, k2, va2, vb2, d2, j2, i2, wx2, wl2, wr2, zl2, zr2, pc2, pk2,
    s3, c3, va3, vb3, d3, j3, i3, wx3, wl3, wr3, zl3, zr3, pc3, ps3,
    face, yb, yd, ry, rd,
    sem, self_sem,
):
    i = lax.axis_index("gx")
    j = lax.axis_index("gy")
    k = lax.axis_index("gz")
    p = 2 * i + k
    place = (p, j)

    faces = []
    for at, src in enumerate((diffusion, iterate, right_side)):
        for t, low in enumerate((56, 0)):
            faces.append(pltpu.make_async_copy(src.at[pl.ds(0, 16), pl.ds(low, 8)], face.at[at, t], self_sem.at[3 + 2 * at + t]))
    for load in faces:
        load.start()

    barrier = pltpu.get_barrier_semaphore()

    def greet(to, tj):
        pl.semaphore_signal(
            barrier, inc=1, device_id=(to // 2, tj, to % 2), device_id_type=MESH
        )

    loop(1, NP, lambda q: greet((p + q) % NP, j))
    count = NP - 1
    for dj in (-1, 1, -2, 2):
        okj = jnp.logical_and(j + dj >= 0, j + dj < NJ)
        for dp in range(-2, 3):
            ok = jnp.logical_and(okj, jnp.logical_and(p + dp >= 0, p + dp < NP))
            count = count + ok.astype(jnp.int32)

            @pl.when(ok)
            def _():
                greet(p + dp, j + dj)

    for load in faces:
        load.wait()

    def strips(at, planes):
        halo = 4 if at == 2 else 5
        res, start = [], 0
        for m, steps in enumerate(planes):
            if halo > steps:
                res.append((m, start, halo - steps))
                start += halo - steps
        return res, -(-start // 8) * 8

    near = ((0,) * 8 + (1, 2, 3, 4), (4, 3, 2, 1) + (0,) * 8)
    corners = ((4, 3, 2, 1), (1, 2, 3, 4))
    for at in range(3):
        for t in range(2):
            for half in range(2):
                for m, start, rows in strips(at, near[half])[0]:
                    low = (1 - t) * (8 - rows)
                    yb[at, t, half, start:start + rows] = face[at, t, m + 4 * half, low:low + rows]
                for m, start, rows in strips(at, corners[half])[0]:
                    low = (1 - t) * (8 - rows)
                    yd[at, t, half, start:start + rows] = face[at, t, m + 12 * (1 - half), low:low + rows]

    pl.semaphore_wait(barrier, count)

    def fine_moves(at, src, dst, halo):
        n = 8 + halo

        def copy(slot_s, slot_r, x0, nx, a0, low, size, to, zh, dev):
            return pltpu.make_async_remote_copy(
                src_ref=src.at[pl.ds(x0, nx), pl.ds(low, size)],
                dst_ref=dst.at[pl.ds(a0, nx), zh, pl.ds(to, size)],
                send_sem=sem.at[FINE_SEND + 11 * at + slot_s],
                recv_sem=sem.at[FINE_RECV + 11 * at + slot_r],
                device_id=dev,
                device_id_type=MESH,
            )

        mine = pltpu.make_async_copy(
            src.at[pl.ds(k * (8 - halo), n)],
            dst.at[pl.ds(5 - halo * k, n), k, pl.ds(16, 64)],
            self_sem.at[at],
        )
        other = 1 - k
        def outer_rows(slot_s, slot_r, src_rows, dst_rows, dev):
            return pltpu.make_async_remote_copy(
                src_ref=src_rows,
                dst_ref=dst_rows,
                send_sem=sem.at[FINE_SEND + 11 * at + slot_s],
                recv_sem=sem.at[FINE_RECV + 11 * at + slot_r],
                device_id=dev,
                device_id_type=MESH,
            )

        inner = [(None, copy(0, 0, other * (8 - halo), n, 5 - halo * other, 0, 64, 16, k, (i, j, other)))]
        sends = []
        sends.append((i < 7, copy(1, 1 + k, 16 - halo, halo, 5 - halo, 0, 64, 16, k, (i + 1, j, 0))))
        sends.append((i > 0, copy(2, 1 + k, 0, halo, 13, 0, 64, 16, k, (i - 1, j, 1))))
        turns = ((0, 1), (1, -1))
        near_rows = pl.ds(0, strips(at, near[0])[1])
        corner_rows = pl.ds(0, strips(at, corners[0])[1])
        for t, dj in turns:
            okj = jnp.logical_and(j + dj >= 0, j + dj < NJ)
            up = jnp.logical_and(i < 7, okj)
            down = jnp.logical_and(i > 0, okj)
            slot = 3 + 2 * t
            sends.append((up, outer_rows(slot, slot + k, yd.at[at, t, 0, corner_rows], rd.at[at, t, k, corner_rows], (i + 1, j + dj, 0))))
            sends.append((down, outer_rows(slot + 1, slot + k, yd.at[at, t, 1, corner_rows], rd.at[at, t, k, corner_rows], (i - 1, j + dj, 1))))
            slot = 7 + 2 * t
            for half in (0, 1):
                inner.append((okj, outer_rows(slot + half, slot + k, yb.at[at, t, half, near_rows], ry.at[at, t, k, near_rows], (i, j + dj, half))))

        def start(part):
            if part == 0:
                mine.start()
            for ok, c in (inner, sends)[part]:
                if ok is None:
                    c.start()
                else:
                    pl.when(ok)(c.start)

        def unpack(buf, t, firsts, tables):
            for mine_half in range(2):

                @pl.when(k == mine_half)
                def _():
                    for m, start, rows in strips(at, tables[mine_half])[0]:
                        low = 16 - rows if t == 0 else 80
                        for half in (0, 1):
                            dst[firsts[mine_half] + m, half, low:low + rows] = buf[at, t, half, start:start + rows]

        def arrive_inner():
            mine.wait()
            copy(0, 0, 0, n, 5 - halo * k, 0, 64, 16, other, (i, j, other)).wait_recv()
            for t, dj in turns:

                @pl.when(jnp.logical_and(j - dj >= 0, j - dj < NJ))
                def _():
                    for half in (0, 1):
                        outer_rows(0, 7 + 2 * t + half, yb.at[at, t, 0, near_rows], ry.at[at, t, half, near_rows], (i, j, other)).wait_recv()
                    unpack(ry, t, (5, 1), near)

        def arrive_outer():
            beside = jnp.logical_or(jnp.logical_and(k == 0, i > 0), jnp.logical_and(k == 1, i < 7))
            a0 = (5 - halo) * (1 - k) + 13 * k

            @pl.when(beside)
            def _():
                for half in (0, 1):
                    copy(0, 1 + half, 0, halo, a0, 0, 64, 16, half, (i, j, other)).wait_recv()

            for t, dj in turns:

                @pl.when(jnp.logical_and(beside, jnp.logical_and(j - dj >= 0, j - dj < NJ)))
                def _():
                    for half in (0, 1):
                        outer_rows(0, 3 + 2 * t + half, yd.at[at, t, 0, corner_rows], rd.at[at, t, half, corner_rows], (i, j, other)).wait_recv()
                    unpack(rd, t, (1, 13), corners)

        def drain():
            for ok, c in inner + sends:
                if ok is None:
                    c.wait_send()
                else:
                    pl.when(ok)(c.wait_send)

        return start, arrive_inner, arrive_outer, drain

    moves_c = fine_moves(0, diffusion, cc, 5)
    moves_v = fine_moves(1, iterate, va, 5)
    moves_g = fine_moves(2, right_side, gg, 4)
    for part in range(2):
        for moved in (moves_c, moves_v, moves_g):
            moved[0](part)

    def clear(ref, planes, low_planes, high_from, edges, own=None):
        def wipe(a):
            ref[a] = jnp.zeros(ref.shape[1:], F32)

        loop(0, low_planes, wipe)
        loop(high_from, planes, wipe)

        def wipe_rows(low, size):
            def one(a):
                if len(ref.shape) == 4:
                    ref[a, :, low:low + size] = jnp.zeros((2, size, 128), F32)
                else:
                    ref[a, low:low + size] = jnp.zeros((size, 128), F32)

            loop(*(own or (0, planes)), one)

        for test, low, size in edges:
            pl.when(test)(lambda low=low, size=size: wipe_rows(low, size))

    def outer(first, planes, per, total):
        low = jnp.clip(first - per * p, 0, planes)
        high = jnp.clip(total - per * p + first, 0, planes)
        return low, high

    low, high = outer(5, 18, 8, 128)
    for ref in (va, cc, gg):
        clear(ref, 18, low, high, [(j == 0, 8, 8), (j == 7, 80, 8)])
    clear(pre, 18, low, high, [(j == 0, 8, 8), (j == 7, 80, 8)], (5, 13))
    low, high = outer(6, 16, 4, 64)
    for ref, owned in ((s1, None), (c1, (6, 10)), (k1, (6, 10))):
        clear(ref, 16, low, high, [(j == 0, 8, 8), (j == 7, 48, 8)], owned)
    low, high = outer(7, 16, 2, 32)
    for ref, owned in ((s2, None), (c2, (7, 9))):
        clear(ref, 16, low, high, [(j == 0, 8, 32), (j == 1, 8, 16), (j == 6, 72, 16), (j == 7, 56, 32)], owned)
    for ref in (pc2, pk2):
        clear(ref, 16, low, high, [])
    for ref in (c3, va3, vb3):
        clear(ref, 18, 1, 17, [])

    def fold_rows(ref, at):
        return line(ref, 16 * at) + line(ref, 16 * at + 1)

    def fold_lanes(value, step):
        even = (lanes(value.shape) // step) % 2 == 0
        return value + jnp.where(even, pltpu.roll(value, 128 - step, 1), pltpu.roll(value, step, 1))

    def pack(halves, at):
        low, high = (fold_lanes(fold_rows(half, at), 1) for half in halves)
        from_lane = (2 * lanes((8, 128))) % 128
        low = jnp.take_along_axis(low, from_lane, axis=1)
        high = jnp.take_along_axis(high, from_lane, axis=1)
        return 0.125 * jnp.where(lanes((8, 128)) < 64, low, high)

    def squeeze(ref, a, row, rows, parts):
        size = rows // parts
        spot = lanes((size, 128)) % parts
        res = ref[a, row:row + size]
        for q in range(1, parts):
            res = jnp.where(spot == q, ref[a, row + q * size:row + (q + 1) * size], res)
        return res

    def widen(src, dst, planes, row, rows, parts):
        size = rows // parts
        spot = lanes((8, 128))
        spot = spot - spot % parts
        for a in planes:
            for r in range(0, size, 8):
                value = src[a, r:r + 8]
                for q in range(parts):
                    at = row + q * size + r
                    dst[a, at:at + 8] = jnp.take_along_axis(value, spot + q, axis=1)

    own = slice(16, 80)
    moves_c[1]()

    def coarsen_c(m):
        a = 5 + 2 * m
        for h in range(2):
            tmp[m, h] = cc[a, h, own] + cc[a + 1, h, own]
        for t in range(4):
            c1[6 + m, 16 + 8 * t:24 + 8 * t] = pack((tmp.at[m, 0], tmp.at[m, 1]), t)

    for m in range(4):
        coarsen_c(m)
    for m in range(2):
        tmp[m, 0, 0:32] = c1[6 + 2 * m, 16:48] + c1[7 + 2 * m, 16:48]
        for t in range(2):
            c2[7 + m, 40 + 8 * t:48 + 8 * t] = 0.125 * fold_lanes(fold_rows(tmp.at[m, 0], t), 1)

    used = {"recv": FINE_RECV + 33, "send": 0}

    def moves(ref, send, dirs):
        recv = used["recv"]
        used["recv"] = recv + len(dirs)
        return Moves(place, ref, sem, send, recv, dirs)

    def y_moves(send, ref, planes, first, row, rows, mid=()):
        return moves(ref, send, block_dirs(planes, first, 0, row, rows, (0,), (-1, 1), False, mid))

    def h_moves(send, ref, planes, first, halo, row, rows, dps, mid=()):
        return moves(ref, send, block_dirs(planes, first, halo, row, rows, dps, (0,), True, mid))

    def column_moves(send, ref, dps, djs):
        dirs = []
        for dp, dj, src, dst in block_dirs(2, 7, 4, 40, 16, dps, (0,), False):
            dirs.append((dp, 0, src, dst))
        for dj in djs:
            for dp in (0,) + tuple(dps):
                row = pl.ds(40 - 16 * dj, 16)
                dirs.append((dp, dj, (pl.ds(7, 2), pl.ds(40, 16)), (pl.ds(7 - 2 * dp, 2), row)))
        return moves(ref, send, dirs)

    class Around:
        def __init__(self, send, ref):
            self.send, self.ref, self.recv = send, ref, used["recv"]
            used["recv"] += 1

        def copy(self, q, src, dst):
            to = (p + q) % NP
            return pltpu.make_async_remote_copy(
                src_ref=self.ref.at[src],
                dst_ref=self.ref.at[dst],
                send_sem=sem.at[self.send],
                recv_sem=sem.at[self.recv],
                device_id=(to // 2, j, to % 2),
                device_id_type=MESH,
            )

        def start(self):
            loop(1, NP, lambda q: self.copy(q, p + 1, p + 1).start())

        def all(self):
            planes = pl.ds(1, NP - 1)
            return self.copy(1, planes, planes)

        def arrive(self):
            self.all().wait_recv()

        def drain(self):
            self.all().wait_send()

    y_c1 = y_moves(33, c1, 4, 6, 16, 32)
    y_c2 = column_moves(35, c2, (), (-2, -1, 1, 2))
    h_c1 = h_moves(0, c1, 4, 6, 6, 16, 32, (-2, -1, 1, 2))
    h_c2 = h_moves(4, pc2, 2, 7, 7, 8, 24, (-4, -3, -2, -1, 1, 2, 3, 4))
    h_c3 = Around(12, pc3)
    m_s1 = moves(s1, 39, block_dirs(4, 6, 4, 16, 32, (-1, 0, 1), (0, -1, 1), False))
    y_pre = y_moves(47, pre, 8, 5, 16, 64, (slice(None),))
    h_pre = h_moves(49, pre, 8, 5, 4, 16, 64, (-1, 1), (slice(None),))
    m_s2 = column_moves(51, s2, (-2, -1, 1, 2), (-2, -1, 1, 2))
    y_k1 = y_moves(75, k1, 4, 6, 16, 32)
    h_k1 = h_moves(77, k1, 4, 6, 6, 16, 32, (-2, -1, 1, 2))
    h_s1 = h_moves(81, s1, 4, 6, 5, 16, 32, (-2, 2))
    h_s2 = h_moves(83, s2, 2, 7, 6, 40, 16, (-3, 3))
    h_s3 = Around(85, ps3)
    h_k2 = h_moves(86, pk2, 2, 7, 7, 8, 0, (-4, -3, -2, -1, 1, 2, 3, 4))
    out_send, out_recv = 94, used["recv"]
    assert out_recv < SEMS, out_recv

    y_c1.start()
    y_c2.start()

    wide = slice(12, 84)
    lane = lanes((72, 128))

    def fine_setup(low, n):
        for a in [low + u for u in range(n)]:
            mid = [cc[a, h, wide] for h in range(2)]
            prev = [pltpu.roll(m, 1, 1) for m in mid]
            foll = [pltpu.roll(m, 127, 1) for m in mid]
            left = (jnp.where(lane == 0, 0.0, prev[0]), jnp.where(lane == 0, prev[0], prev[1]))
            right = (jnp.where(lane == 127, foll[1], foll[0]), jnp.where(lane == 127, 0.0, foll[1]))
            for h in range(2):
                ahead = cc[a + 1, h, wide]
                yl = cc[a, h, 11:83]
                yr = cc[a, h, 13:85]
                wx[a, h, wide] = 0.5 * (mid[h] + ahead)
                wl[a, h, wide] = 0.5 * (mid[h] + yl)
                wr[a, h, wide] = 0.5 * (mid[h] + yr)
                low_edge = 0.5 * (mid[h] + left[h])
                high_edge = 0.5 * (mid[h] + right[h])
                zl[a, h, wide] = jnp.where(lane == 0, 0.0, low_edge) if h == 0 else low_edge
                zr[a, h, wide] = jnp.where(lane == 127, 0.0, high_edge) if h == 1 else high_edge
                diag = 0.5 * (6.0 * mid[h] + (cc[a - 1, h, wide] + ahead) + (yl + yr) + (left[h] + right[h]))
                di[a, h, wide] = diag
                jj[a, h, wide] = jnp.where(mid[h] > 0.0, 1.0 / diag, 0.0)

    def fine_setups(low, count):
        wx[low - 1, :, wide] = 0.5 * (cc[low - 1, :, wide] + cc[low, :, wide])
        spread(low, count, 3, fine_setup)

    fine_setups(6 - 5 * k, 11)
    moves_v[1]()
    moves_g[1]()

    def fine_sum(src, low, n, r0, r1):
        for r in range(r0, r1, 24 if (r1 - r0) % 24 == 0 else 32):
            e = r + (24 if (r1 - r0) % 24 == 0 else 32)
            w = slice(r, e)
            spot = lanes((e - r, 128))
            v = [[src[low + u, h, w] for h in range(2)] for u in range(-1, n + 1)]
            x = [[wx[low + u, h, w] for h in range(2)] for u in range(-1, n)]
            for u in range(n):
                a = low + u
                mid = v[u + 1]
                prev = [pltpu.roll(m, 1, 1) for m in mid]
                foll = [pltpu.roll(m, 127, 1) for m in mid]
                left = (prev[0], jnp.where(spot == 0, prev[0], prev[1]))
                right = (jnp.where(spot == 127, foll[1], foll[0]), foll[1])
                for h in range(2):
                    total = gg[a, h, w] + x[u][h] * v[u][h] + x[u + 1][h] * v[u + 2][h]
                    total = total + wl[a, h, w] * src[a, h, r - 1:e - 1] + wr[a, h, w] * src[a, h, r + 1:e + 1]
                    total = total + zl[a, h, w] * left[h] + zr[a, h, w] * right[h]
                    yield u, a, h, w, mid[h], total

    def fine_sweep(src, dst, step, low_plane, count, most=4):
        keep, new = FINE_STEPS[step]

        def run(low, n):
            for u, a, h, w, mid, total in fine_sum(src, low, n, 12, 84):
                move = new * (jj[a, h, w] * total - mid)
                if step > 0:
                    move = move + keep * dd[a, h, w]
                dd[a, h, w] = move
                dst[a, h, w] = mid + move

        spread(low_plane, count, most, run)

    rounds = ((va, vb), (vb, vc), (vc, vd), (vd, ve))
    for step, (src, dst) in enumerate(rounds):
        fine_sweep(src, dst, step, 6 + step - 5 * k, 11 - 2 * step)
    moves_c[2]()
    fine_setups(1 + 11 * k, 5)
    moves_v[2]()
    moves_g[2]()
    for moved in (moves_c, moves_v, moves_g):
        moved[3]()
    y_c1.arrive()
    h_c1.start()
    for step, (src, dst) in enumerate(rounds):
        fine_sweep(src, dst, step, 1 + step + (11 - 2 * step) * k, 5, 5)

    for m in range(4):
        for u, a, h, w, mid, total in fine_sum(ve, 5 + 2 * m, 2, 16, 80):
            part = total - di[a, h, w] * mid
            spot = slice(w.start - 16, w.stop - 16)
            tmp[m, h, spot] = part if u == 0 else tmp[m, h, spot] + part
        for t in range(4):
            s1[6 + m, 16 + 8 * t:24 + 8 * t] = pack((tmp.at[m, 0], tmp.at[m, 1]), t)

    m_s1.start()

    def keep_fine(a):
        pre[a, :, own] = ve[a, :, own]

    loop(5, 13, keep_fine)
    y_pre.start()
    y_c2.arrive()
    for a in (7, 8):
        pc2[a] = squeeze(c2, a, 8, 80, 2)
    h_c2.start()
    tmp[2, 0] = c2[7, 16:80] + c2[8, 16:80]
    for t in range(4):
        c3[p + 1, 12 + 8 * t:20 + 8 * t] = 0.125 * fold_lanes(fold_rows(tmp.at[2, 0], t), 2)
    pc3[p + 1] = squeeze(c3, p + 1, 12, 32, 4)
    h_c3.start()

    def setup(c, jn, dn, wxn, wln, wrn, zln, zrn, planes, rows, step, scale):
        low, high = planes
        r0, r1 = rows
        w = slice(r0, r1)
        spot = lanes((r1 - r0, 128))
        half = 0.5 * scale

        def run(first_plane, n):
            for a in [first_plane + u for u in range(n)]:
                mid = c[a, w]
                ahead = c[a + 1, w]
                left = jnp.where(spot < step, 0.0, pltpu.roll(mid, step, 1))
                right = jnp.where(spot >= 128 - step, 0.0, pltpu.roll(mid, 128 - step, 1))
                yl = c[a, r0 - 1:r1 - 1]
                yr = c[a, r0 + 1:r1 + 1]
                wxn[a, w] = half * (mid + ahead)
                wln[a, w] = half * (mid + yl)
                wrn[a, w] = half * (mid + yr)
                zln[a, w] = jnp.where(spot < step, 0.0, half * (mid + left))
                zrn[a, w] = jnp.where(spot >= 128 - step, 0.0, half * (mid + right))
                diag = half * (6.0 * mid + (c[a - 1, w] + ahead) + (yl + yr) + (left + right))
                dn[a, w] = diag
                jn[a, w] = jnp.where(mid > 0.0, 1.0 / diag, 0.0)

        wxn[low - 1, w] = half * (c[low - 1, w] + c[low, w])
        spread(low, high - low, 7 if high - low == 14 else 8, run)

    def gather_sum(src, low, n, g, wxn, wln, wrn, zln, zrn, rows, step):
        r0, r1 = rows
        w = slice(r0, r1)
        v = [src[low + u, w] for u in range(-1, n + 1)]
        x = [wxn[low + u, w] for u in range(-1, n)]
        for u in range(n):
            a = low + u
            mid = v[u + 1]
            total = g[a, w] + x[u] * v[u] + x[u + 1] * v[u + 2]
            total = total + wln[a, w] * src[a, r0 - 1:r1 - 1] + wrn[a, w] * src[a, r0 + 1:r1 + 1]
            total = total + zln[a, w] * pltpu.roll(mid, step, 1) + zrn[a, w] * pltpu.roll(mid, 128 - step, 1)
            yield a, mid, total

    def sweep(src, dst, d, jn, ws, planes, rows, step, pair):
        keep, new = pair
        w = slice(*rows)

        def run(low, n):
            for a, mid, total in gather_sum(src, low, n, *ws, rows, step):
                move = new * (jn[a, w] * total - mid)
                if keep != 0.0:
                    move = move + keep * d[a, w]
                d[a, w] = move
                dst[a, w] = mid + move

        spread(planes[0], planes[1] - planes[0], 8, run)

    def first(dst, d, g, jn, planes, rows, new):
        w = slice(*rows)

        for a in range(*planes):
            move = new * (jn[a, w] * g[a, w])
            d[a, w] = move
            dst[a, w] = move

    ws1 = (s1, wx1, wl1, wr1, zl1, zr1)
    ws2 = (s2, wx2, wl2, wr2, zl2, zr2)
    ws3 = (s3, wx3, wl3, wr3, zl3, zr3)
    rows1, wide2, rows2, rows3 = (8, 56), (8, 88), (32, 64), (8, 48)

    h_c1.arrive()
    setup(c1, j1, i1, wx1, wl1, wr1, zl1, zr1, (1, 15), rows1, 1, 0.25)
    m_s1.arrive()
    first(va1, d1, s1, j1, (2, 14), rows1, FINE_STEPS[0][1])
    sweep(va1, vb1, d1, j1, ws1, (3, 13), rows1, 1, FINE_STEPS[1])
    sweep(vb1, va1, d1, j1, ws1, (4, 12), rows1, 1, FINE_STEPS[2])
    sweep(va1, vb1, d1, j1, ws1, (5, 11), rows1, 1, FINE_STEPS[3])

    def residual(src, low, ws, dn, rows, step):
        parts = [total - dn[a, slice(*rows)] * mid for a, mid, total in gather_sum(src, low, 2, *ws, rows, step)]
        return parts[0] + parts[1]

    for m in range(2):
        tmp[m, 0, 0:32] = residual(vb1, 6 + 2 * m, ws1, i1, (16, 48), 1)
    for m in range(2):
        for t in range(2):
            s2[7 + m, 40 + 8 * t:48 + 8 * t] = 0.125 * fold_lanes(fold_rows(tmp.at[m, 0], t), 1)
    m_s2.start()
    k1[6:10, 16:48] = vb1[6:10, 16:48]
    y_k1.start()
    h_s1.start()
    y_pre.arrive()
    h_pre.start()
    h_c2.arrive()
    others2 = tuple(range(7)) + tuple(range(9, 16))
    widen(pc2, c2, others2, 8, 80, 2)
    setup(c2, j2, i2, wx2, wl2, wr2, zl2, zr2, (1, 15), wide2, 2, 0.0625)
    for moved in (y_c1, y_c2, h_c1, h_c2, m_s1, y_pre):
        moved.drain()

    m_s2.arrive()
    first(va2, d2, s2, j2, (3, 13), wide2, FINE_STEPS[0][1])
    sweep(va2, vb2, d2, j2, ws2, (4, 12), wide2, 2, FINE_STEPS[1])
    sweep(vb2, va2, d2, j2, ws2, (5, 11), wide2, 2, FINE_STEPS[2])
    sweep(va2, vb2, d2, j2, ws2, (6, 10), wide2, 2, FINE_STEPS[3])
    tmp[2, 0] = residual(vb2, 7, ws2, i2, (16, 80), 2)
    for t in range(4):
        s3[p + 1, 12 + 8 * t:20 + 8 * t] = 0.125 * fold_lanes(fold_rows(tmp.at[2, 0], t), 2)
    ps3[p + 1] = squeeze(s3, p + 1, 12, 32, 4)
    h_s3.start()
    k2[7:9, 32:64] = vb2[7:9, 32:64]
    for a in (7, 8):
        pk2[a] = squeeze(vb2, a, 32, 32, 2)
    h_k2.start()
    y_k1.arrive()
    h_k1.start()
    h_s2.start()
    h_c3.arrive()
    widen(pc3, c3, range(1, 17), 12, 32, 4)
    setup(c3, j3, i3, wx3, wl3, wr3, zl3, zr3, (1, 17), rows3, 4, 0.015625)
    for moved in (h_c3, h_pre, m_s2, y_k1, h_s1):
        moved.drain()

    h_s3.arrive()
    widen(ps3, s3, range(1, 17), 12, 32, 4)
    first(va3, d3, s3, j3, (1, 17), rows3, BOTTOM_STEPS[0][1])
    here, there = va3, vb3
    for at in range(1, BOTTOM):
        halo = BOTTOM + 3 - at
        rows = (12, 44) if halo > 8 else (16, 40)
        sweep(here, there, d3, j3, ws3, (1, 17), rows, 4, BOTTOM_STEPS[at])
        here, there = there, here

    h_k2.arrive()
    widen(pk2, k2, others2, 32, 32, 2)
    h_s2.arrive()

    def finish2(a):
        up = jnp.clip(p - 3 + (a + 1) // 2, 0, 17)
        for t in range(2):
            e = here[up, 20 + 8 * t:28 + 8 * t]
            for odd in range(2):
                at = pl.ds(32 + 16 * t + odd, 8, stride=2)
                va2[a, at] = k2[a, at] + e

    for a in range(16):
        finish2(a)
    sweep(va2, vb2, d2, j2, ws2, (1, 15), rows2, 2, FINE_STEPS[0])
    sweep(vb2, va2, d2, j2, ws2, (2, 14), rows2, 2, FINE_STEPS[1])
    sweep(va2, vb2, d2, j2, ws2, (3, 13), rows2, 2, FINE_STEPS[2])
    sweep(vb2, va2, d2, j2, ws2, (4, 12), rows2, 2, FINE_STEPS[3])

    h_k1.arrive()
    h_s1.arrive()

    def finish1(a):
        up = 4 + a // 2
        for t in range(3):
            e = va2[up, 36 + 8 * t:44 + 8 * t]
            for odd in range(2):
                at = pl.ds(8 + 16 * t + odd, 8, stride=2)
                va1[a, at] = k1[a, at] + e

    for a in range(16):
        finish1(a)
    sweep(va1, vb1, d1, j1, ws1, (1, 15), rows1, 1, FINE_STEPS[0])
    sweep(vb1, va1, d1, j1, ws1, (2, 14), rows1, 1, FINE_STEPS[1])
    sweep(va1, vb1, d1, j1, ws1, (3, 13), rows1, 1, FINE_STEPS[2])
    sweep(vb1, va1, d1, j1, ws1, (4, 12), rows1, 1, FINE_STEPS[3])

    h_pre.arrive()
    for moved in (h_k1, h_s2, h_s3, h_k2):
        moved.drain()

    def finish0(m):
        for t in range(5):
            e = va1[4 + m, 14 + 8 * t:22 + 8 * t]
            to_lane = lanes((8, 128)) // 2
            for h in range(2):
                half = jnp.take_along_axis(e, to_lane + 64 * h, axis=1)
                for x in range(2):
                    a = 1 + 2 * m + x
                    for odd in range(2):
                        at = pl.ds(12 + 16 * t + odd, 8, stride=2)
                        va[a, h, at] = pre[a, h, at] + half

    loop(0, 8, finish0)
    fine_sweep(va, vb, 0, 2, 14)
    fine_sweep(vb, va, 1, 3, 12)
    fine_sweep(va, vb, 2, 4, 10)
    fine_sweep(vb, va, 3, 5, 8)
    give = pltpu.make_async_remote_copy(
        src_ref=va.at[pl.ds(5, 8), 1 - k, pl.ds(16, 64)],
        dst_ref=out.at[pl.ds(8 * k, 8)],
        send_sem=sem.at[out_send],
        recv_sem=sem.at[out_recv],
        device_id=(i, j, 1 - k),
        device_id_type=MESH,
    )
    give.start()
    out[pl.ds(8 * k, 8)] = va[5:13, k, own]
    give.wait_send()
    pltpu.make_async_remote_copy(
        src_ref=va.at[pl.ds(5, 8), k, pl.ds(16, 64)],
        dst_ref=out.at[pl.ds(8 * (1 - k), 8)],
        send_sem=sem.at[out_send],
        recv_sem=sem.at[out_recv],
        device_id=(i, j, 1 - k),
        device_id_type=MESH,
    ).wait_recv()


def on_device(iterate, right_side, diffusion):
    def buf(*shape):
        return pltpu.VMEM(shape, F32)

    scratch = [buf(18, 2, 96, 128)] * 3 + [buf(4, 2, 64, 128)] + [buf(18, 2, 96, 128)] * 13
    scratch += [buf(16, 64, 128)] * 13
    scratch += [buf(16, 96, 128)] * 13 + [buf(16, 40, 128), buf(16, 16, 128)]
    scratch += [buf(18, 56, 128)] * 12 + [buf(18, 8, 128)] * 2
    scratch += [buf(3, 2, 16, 8, 128)] + [buf(3, 2, 2, 56, 128), buf(3, 2, 2, 16, 128)] * 2
    dma = pltpu.SemaphoreType.DMA
    scratch += [dma((SEMS,)), dma((9,))]
    return pl.pallas_call(
        kernel,
        out_shape=pltpu.VMEM((16, 64, 128), F32),
        in_specs=[pl.BlockSpec(memory_space=pl.ANY)] * 3,
        out_specs=pl.BlockSpec(memory_space=pltpu.VMEM),
        scratch_shapes=scratch,
        compiler_params=pltpu.CompilerParams(
            collective_id=0, has_side_effects=True, vmem_limit_bytes=60 * 2**20
        ),
        cost_estimate=pl.CostEstimate(flops=10**8, bytes_accessed=2 * 10**6, transcendentals=0),
        name="vcycle",
    )(iterate, right_side, diffusion)


def solution(mesh):
    placed = (P("gx", "gy", "gz"), P("gx", "gy", "gz"), P("gx", "gy", "gz"))
    return jax.shard_map(
        on_device, mesh=mesh, in_specs=placed, out_specs=P("gx", "gy", "gz"), check_vma=False
    )
```
